32 devices in a mesh: pairs: 2 (over x), src: 16 (over z, y, core).
Axes of the slice: x: 2, y: 2, z: 4, core: 2. Of those that a mesh axis runs over, the one named last changes fastest.
Arguments:
- src_feat: bfloat16 [32768, 256], P(('pairs', 'src')), parts along dimension 0, may hold values from -6 to 6
- tile_feat: bfloat16 [256, 16, 128, 256], P(('pairs', 'src')), parts along dimension 0, may hold values from -6 to 6
- tile_tgt: int32 [256, 16], P(('pairs', 'src')), parts along dimension 0, may hold values from 0 to 127, as said below
- tile_live: int32 [256], P(('pairs', 'src')), parts along dimension 0, may hold values from 1 to 16, as said below
- src_lin: float32 [32768], P(('pairs', 'src')), parts along dimension 0, may hold values from 0 to 1
- tgt_lin: float32 [32768], P(('pairs', 'src')), parts along dimension 0, may hold values from 0 to 1
- src_mass: float32 [32768], P(('pairs', 'src')), parts along dimension 0, may hold values from 0.5 to 2
- tgt_mass: float32 [32768], P(('pairs', 'src')), parts along dimension 0, may hold values from 0.25 to 6
- tgt_count: int32 [256], P(('pairs', 'src')), parts along dimension 0, may hold values from 1 to 128
Outputs:
- src_scale: float32 [32768], P(('pairs', 'src')), parts along dimension 0
- tgt_scale: float32 [32768], P(('pairs', 'src')), parts along dimension 0
The draws below stay inside these ranges and needn't reach their ends.
There are 2 independent parts, one for each index of `pairs`. The reference program is written for one: setup_inputs(seed, part) draws one part's arguments, and reference() takes and returns one part's arrays. A program takes and returns all parts, laid end to end along the dimension named above; each array names one. Nothing has to cross between parts.
Inputs may be any that keep to these rules, and one draw needn't show every extreme that they name: tile_tgt[s, 0] = s; the slots of one source block name distinct target blocks. `tile_live`: every source block has between 1 and 16 live slots.
All inputs are finite; a program needn't handle non-finite values.
Results may differ from the reference program's by a relative error of at most 0.0003.
Values sent between devices are 32-bit elements; how exact they have to be, the bound alone decides.
No kernel may reach another device: no remote copies, remote signals or barrier semaphores. Data moves between devices by JAX's collectives and lax.ppermute only.
A program may use at most 64 MiB of HBM per device.

```python
import math
import jax
import jax.numpy as jnp
from jax import lax

BLK = 128
NC = 256
SB_DEV = 8
KP = 16
ITERS = 3
NSB = 128
NTB = 128
NS = 16384
NT = 16384


def draw_tile_tgt(key, part):
    key = jax.random.fold_in(key, 11)
    spacing = NSB // KP
    jitter = jax.random.randint(key, (NSB, KP), 0, spacing)
    slots = jnp.arange(KP, dtype=jnp.int32)[None, :]
    offsets = jnp.where(slots == 0, 0, slots * spacing + jitter)
    blocks = jnp.arange(NSB, dtype=jnp.int32)[:, None]
    return ((blocks + offsets) % NSB).astype(jnp.int32)


def draw_tile_live(key, part):
    key = jax.random.fold_in(key, 12)
    counts = jax.random.randint(key, (NSB,), 1, KP + 1)
    first = jnp.arange(NSB, dtype=jnp.int32) % SB_DEV == 0
    return jnp.where(first, KP, counts).astype(jnp.int32)


def draw_tgt_count(key, part):
    key = jax.random.fold_in(key, 13)
    first_key, second_key = jax.random.split(key)
    partial_fill = jax.random.randint(first_key, (NTB,), 1, BLK + 1)
    pick = jax.random.randint(second_key, (NTB,), 0, 3)
    counts = jnp.where(pick == 0, partial_fill, BLK)
    counts = jnp.where(jnp.arange(NTB, dtype=jnp.int32) == 0, BLK, counts)
    return counts.astype(jnp.int32)


def draw_tgt_mass(key, part):
    key = jax.random.fold_in(key, 14)
    ramp = 1.0 + 2.0 * jnp.arange(NT, dtype=jnp.float32) / NT
    base = jnp.exp(jax.random.uniform(key, (NT,), jnp.float32, jnp.log(0.5), jnp.log(2.0)))
    return (base * ramp).astype(jnp.float32)


def block_levels(rng, dims, pieces, smallest, top_value):
    gain = 1.0
    for axis_at, parts in pieces:
        heights = jax.random.uniform(jax.random.fold_in(jax.random.fold_in(rng, 6), axis_at), (parts,), jnp.float32, smallest / len(pieces), top_value / len(pieces))
        gain = gain * jnp.repeat(jnp.exp(heights), dims[axis_at] // parts).reshape((-1,) + (1,) * (len(dims) - 1 - axis_at))
    return gain


def bell_draw(key, dims, deviation, reach, shards=(), held_as=jnp.bfloat16):
    factor_of = block_levels(key, dims, shards, -0.22, 0.18) if shards else 1.0
    array = jax.random.normal(key, dims, jnp.float32) * deviation * factor_of
    return jnp.minimum(jnp.maximum(array, -reach), reach).astype(held_as)


def setup_inputs(seed: int = 0, part: int = 0) -> dict:
    seeds = jax.random.split(jax.random.key(seed), 10)
    part_keys = jax.random.split(jax.random.fold_in(seeds[9], part), 10)
    src_feat = bell_draw(part_keys[0], (NS, NC), 1.0, 6.0, ((0, 16),))
    tile_feat = bell_draw(part_keys[1], (NSB, KP, BLK, NC), 1.0, 6.0, ((0, 16),))
    tile_tgt = draw_tile_tgt(jax.random.fold_in(jax.random.fold_in(seeds[9], part), 71), part)
    tile_live = draw_tile_live(jax.random.fold_in(jax.random.fold_in(seeds[9], part), 71), part)
    src_lin = jnp.clip(1.0 * jax.random.uniform(part_keys[4], (NS,), jnp.float32) ** block_levels(part_keys[4], (NS,), ((0, 16),), -0.2, 0.2), 0.0, 1.0)
    tgt_lin = jnp.clip(1.0 * jax.random.uniform(part_keys[5], (NT,), jnp.float32) ** block_levels(part_keys[5], (NT,), ((0, 16),), -0.2, 0.2), 0.0, 1.0)
    src_mass = jnp.clip(jnp.exp(math.log(2.0) - 1.3862944 * jax.random.uniform(part_keys[6], (NS,), jnp.float32) ** block_levels(part_keys[6], (NS,), ((0, 16),), -0.2, 0.2)), 0.5, 2.0)
    tgt_mass = draw_tgt_mass(jax.random.fold_in(jax.random.fold_in(seeds[9], part), 71), part)
    tgt_count = draw_tgt_count(jax.random.fold_in(jax.random.fold_in(seeds[9], part), 71), part)
    return {"src_feat": src_feat, "tile_feat": tile_feat, "tile_tgt": tile_tgt, "tile_live": tile_live, "src_lin": src_lin, "tgt_lin": tgt_lin, "src_mass": src_mass, "tgt_mass": tgt_mass, "tgt_count": tgt_count}


EPS = 0.1
RHO = 1.0
ALPHA = 0.5

def reference(src_feat, tile_feat, tile_tgt, tile_live, src_lin, tgt_lin, src_mass, tgt_mass, tgt_count):
    expo = RHO / (RHO + EPS)
    nblocks = tgt_count.shape[0]
    src_rows = src_feat.reshape(NSB, BLK, NC).astype(jnp.float32)
    src_sq = lax.optimization_barrier(jnp.sum(src_rows * src_rows, axis=-1))
    valid = (lax.broadcasted_iota(jnp.int32, (nblocks, BLK), 1) < tgt_count[:, None]).astype(jnp.float32)
    bmass = tgt_mass.reshape(nblocks, BLK) * valid
    present = bmass > 0.0
    live_mask = (lax.broadcasted_iota(jnp.int32, (NSB, KP), 1) < tile_live[:, None]).astype(jnp.float32)
    amass = src_mass.reshape(NSB, BLK)
    target_total = jnp.sqrt(jnp.sum(src_mass) * jnp.sum(bmass))
    tile_lin = tgt_lin.reshape(nblocks, BLK)[tile_tgt]
    src_part = src_lin.reshape(NSB, BLK)
    tgt_scale = valid
    src_scale = jnp.zeros((NSB, BLK), jnp.float32)
    for iteration in range(ITERS):
        tile_scale = tgt_scale[tile_tgt]

        def one_block(packed):
            rows, rows_sq, tiles, lins, live_row, scales, spart, masses = packed
            tiles32 = tiles.astype(jnp.float32)
            tiles_sq = lax.optimization_barrier(jnp.sum(tiles32 * tiles32, axis=-1))
            cross = jnp.einsum('id,kjd->kij', rows, tiles32, precision=lax.Precision.HIGHEST)
            cost = (rows_sq[None, :, None] + tiles_sq[:, None, :] - 2.0 * cross) / NC - 2.0
            cost = cost + ALPHA * (spart[None, :, None] + lins[:, None, :])
            kernel = jnp.exp(-cost / EPS) * live_row[:, None, None]
            row_sums = jnp.einsum('kij,kj->i', kernel, scales, precision=lax.Precision.HIGHEST)
            new_scale = (masses / row_sums) ** expo
            col_part = jnp.einsum('kij,i->kj', kernel, new_scale, precision=lax.Precision.HIGHEST)
            return (new_scale, col_part)
        src_scale, col_parts = lax.map(one_block, (src_rows, src_sq, tile_feat, tile_lin, live_mask, tile_scale, src_part, amass))
        col_sums = jnp.zeros((nblocks, BLK), jnp.float32).at[tile_tgt.reshape(-1)].add(col_parts.reshape(-1, BLK))
        tgt_scale = jnp.where(present, (bmass / jnp.where(present, col_sums, 1.0)) ** expo, 0.0)
        mass = jnp.sum(tgt_scale * col_sums)
        factor = jnp.sqrt(target_total / mass)
        src_scale = src_scale * factor
        tgt_scale = tgt_scale * factor
    return (src_scale.reshape(-1), tgt_scale.reshape(-1))
```

```python
import functools

import jax
import jax.numpy as jnp
from jax import lax
from jax.experimental import pallas as pl
from jax.experimental.pallas import tpu as pltpu
from jax.sharding import PartitionSpec as P

ITERS = 3
EPS = 0.1
RHO = 1.0
ALPHA = 0.5
F = RHO / (RHO + EPS)

VMEM = pltpu.VMEM
SMEM = pltpu.SMEM
ANY = pl.ANY


def diag_mask(block):
    return lax.broadcasted_iota(jnp.int32, (block, block), 0) == lax.broadcasted_iota(
        jnp.int32, (block, block), 1
    )


def to_column(row, mask):
    return jnp.sum(jnp.where(mask, row, 0.0), axis=1, keepdims=True)


def to_row(column, mask):
    return jnp.sum(jnp.where(mask, column, 0.0), axis=0, keepdims=True)


def build_kernel(live, x_ref, feat, lin_ref, mass_ref, k_ref, la_ref, ybuf, sems):
    blocks, slots, block, width = ybuf.shape

    def copy(s):
        return pltpu.make_async_copy(feat.at[s], ybuf.at[s], sems.at[s])

    for s in range(blocks):
        copy(s).start()
    mask = diag_mask(block)
    ones = jnp.ones((8, width), jnp.bfloat16)
    nt = (((1,), (1,)), ((), ()))
    for s in range(blocks):
        x = x_ref[s * block : (s + 1) * block, :]
        x32 = x.astype(jnp.float32)
        sq = jnp.sum(x32 * x32, axis=1, keepdims=True)
        lin = to_column(lin_ref[s : s + 1, :], mask)
        base = (2.0 - sq / width - ALPHA * lin) / EPS
        la = F * jnp.log(to_column(mass_ref[s : s + 1, :], mask))
        la_ref[s * block : (s + 1) * block, :] = jnp.broadcast_to(la, (block, block))
        copy(s).wait()

        def tile(k, _):
            y = ybuf[s, k]
            y32 = y.astype(jnp.float32)
            y2 = y32 * y32
            hi = y2.astype(jnp.bfloat16)
            lo = (y2 - hi.astype(jnp.float32)).astype(jnp.bfloat16)
            cross = lax.dot_general(x, y, nt, preferred_element_type=jnp.float32)
            ysq = lax.dot_general(ones, hi, nt, preferred_element_type=jnp.float32)
            ysq += lax.dot_general(ones, lo, nt, preferred_element_type=jnp.float32)
            e = base + (2.0 / (width * EPS)) * cross - ysq[0:1, :] / (width * EPS)
            start = pl.multiple_of((s * slots + k) * block, block)
            k_ref[pl.ds(start, block), :] = jnp.exp(e)
            return 0

        lax.fori_loop(0, live[s], tile, 0)


def power_of_ratio(num, den):
    return jnp.exp(F * (jnp.log(num) - jnp.log(den)))


def sweep(live, tgt, idx_ref, w_ref, k_ref, la_ref, dense_ref, acc_ref, u_ref, col_ref):
    blocks, slots = tgt.shape
    block = w_ref.shape[1]
    for s in range(blocks):

        def add_row(k, acc):
            w = w_ref[pl.ds(tgt[s, k], 1), :]
            start = pl.multiple_of((s * slots + k) * block, block)
            return acc + k_ref[pl.ds(start, block), :] * w

        acc_ref[s * block : (s + 1) * block, :] = lax.fori_loop(
            0, live[s], add_row, jnp.zeros((block, block), jnp.float32)
        )
    for s in range(blocks):
        rows = pl.ds(s * block, block)
        total = jnp.sum(acc_ref[rows, :], axis=1, keepdims=True)
        u_ref[rows, :] = jnp.exp(la_ref[rows, :] - F * jnp.log(total))
    col_ref[...] = jnp.zeros_like(col_ref)
    for s in range(blocks):
        u = u_ref[s * block : (s + 1) * block, :]

        def add_col(k, _):
            start = pl.multiple_of((s * slots + k) * block, block)
            col_ref[pl.ds(s * slots + k, 1), :] = jnp.sum(
                k_ref[pl.ds(start, block), :] * u, axis=0, keepdims=True
            )
            return 0

        lax.fori_loop(0, live[s], add_col, 0)
    col = col_ref[...]
    hit = lax.broadcasted_iota(jnp.int32, (dense_ref.shape[0], blocks * slots), 0) == idx_ref[...]
    hit = jnp.where(hit, 1.0, 0.0).astype(jnp.bfloat16)
    dense = jnp.zeros(dense_ref.shape, jnp.float32)
    for _ in range(3):
        piece = col.astype(jnp.bfloat16)
        dense += jnp.dot(hit, piece, preferred_element_type=jnp.float32)
        col = col - piece.astype(jnp.float32)
    dense_ref[...] = dense


def total_of(x):
    return jnp.sum(jnp.sum(x, axis=0, keepdims=True), axis=1, keepdims=True)


def first_sweep(n, live, tgt, me, idx_ref, *refs):
    parts = refs[:n]
    k_ref, la_ref, dense_ref, b_ref, et_ref, tot_ref, w_ref, acc_ref, u_ref, col_ref = refs[n:]
    local = parts[0].shape[0] // 3
    for d in range(n):
        rows = pl.ds(pl.multiple_of((me[0] ^ d) * local, local), local)
        b = parts[d][0:local, :]
        et = jnp.exp((-ALPHA / EPS) * parts[d][local : 2 * local, :])
        b_ref[rows, :] = b
        et_ref[rows, :] = et
        w_ref[rows, :] = jnp.where(b > 0.0, et, 0.0)
    am = sum(total_of(parts[d][2 * local : 3 * local, :]) for d in range(n))
    tot = jnp.sqrt(am * total_of(b_ref[...]))
    tot_ref[...] = jnp.broadcast_to(tot, tot_ref.shape)
    sweep(live, tgt, idx_ref, w_ref, k_ref, la_ref, dense_ref, acc_ref, u_ref, col_ref)


def new_scale(mine, other, b_ref, et_ref, tot_ref):
    et = et_ref[...]
    b = b_ref[...]
    col = (mine[...] + other[...]) * et
    t = jnp.where(b > 0.0, power_of_ratio(b, col), 0.0)
    factor = jnp.sqrt(tot_ref[0:1, 0:1] / total_of(t * col))
    return t, factor


def next_sweep(
    live, tgt, idx_ref, mine, other, b_ref, et_ref, tot_ref, k_ref, la_ref,
    dense_ref, u_ref, w_ref, acc_ref, col_ref,
):
    t, factor = new_scale(mine, other, b_ref, et_ref, tot_ref)
    w_ref[...] = t * factor * et_ref[...]
    sweep(live, tgt, idx_ref, w_ref, k_ref, la_ref, dense_ref, acc_ref, u_ref, col_ref)


def last_kernel(me, mine, other, b_ref, et_ref, tot_ref, u_ref, src_ref, tgt_ref, t_ref):
    local, block = src_ref.shape
    t, factor = new_scale(mine, other, b_ref, et_ref, tot_ref)
    t_ref[...] = t * factor
    tgt_ref[...] = t_ref[pl.ds(pl.multiple_of(me[0] * local, local), local), :]
    mask = diag_mask(block)
    for s in range(local):
        src_ref[s : s + 1, :] = to_row(u_ref[s * block : (s + 1) * block, :] * factor, mask)


def call(kernel, ins, outs, scratch=(), smem=0, anys=(), vmem_mb=32, **cost):
    specs = [pl.BlockSpec(memory_space=SMEM)] * smem
    for at in range(smem, len(ins)):
        specs.append(pl.BlockSpec(memory_space=ANY if at in anys else VMEM))
    return pl.pallas_call(
        kernel,
        out_shape=outs,
        in_specs=specs,
        out_specs=[pl.BlockSpec(memory_space=VMEM)] * len(outs),
        scratch_shapes=scratch,
        compiler_params=pltpu.CompilerParams(vmem_limit_bytes=vmem_mb << 20),
        cost_estimate=pl.CostEstimate(**cost) if cost else None,
    )(*ins)


def exchange(x, n, d):
    return lax.ppermute(x, "src", [(i, i ^ d) for i in range(n)])


def shards(
    src_feat, tile_feat, tile_tgt, tile_live, src_lin, tgt_lin, src_mass, tgt_mass, tgt_count
):
    f32 = jnp.float32
    local, slots, block, width = tile_feat.shape
    n = lax.axis_size("src")
    me = lax.axis_index("src").astype(jnp.int32).reshape(1)
    every = local * n
    pairs = local * slots
    valid = lax.broadcasted_iota(jnp.int32, (local, block), 1) < tgt_count[:, None]
    bmass = jnp.where(valid, tgt_mass.reshape(local, block), 0.0)
    amass = src_mass.reshape(local, block)
    own = jnp.concatenate([bmass, tgt_lin.reshape(local, block), amass], axis=0)
    parts = [own] + [exchange(own, n, d) for d in range(1, n)]
    grid = jax.ShapeDtypeStruct((pairs * block, block), f32)
    tall = jax.ShapeDtypeStruct((local * block, block), f32)
    wide = jax.ShapeDtypeStruct((every, block), f32)
    one = jax.ShapeDtypeStruct((8, block), f32)
    kern, la = call(
        build_kernel,
        (tile_live, src_feat, tile_feat, src_lin.reshape(local, block), amass),
        (grid, tall),
        scratch=[VMEM(tile_feat.shape, tile_feat.dtype), pltpu.SemaphoreType.DMA((local,))],
        smem=1,
        anys=(2,),
        flops=2 * pairs * block * block * width,
        bytes_accessed=2 * pairs * block * width,
        transcendentals=pairs * block * block,
    )
    idx = tile_tgt.reshape(1, pairs)
    work = [VMEM((local * block, block), f32), VMEM((pairs, block), f32)]
    w_work = VMEM((every, block), f32)
    dense, b_all, et_all, tot = call(
        functools.partial(first_sweep, n),
        (tile_live, tile_tgt, me, idx, *parts, kern, la),
        (wide, wide, wide, one),
        scratch=[w_work, work[0], VMEM((local * block, block), f32), work[1]],
        smem=3,
    )
    u = None
    for iteration in range(ITERS):
        d = 1
        while d < n:
            other = exchange(dense, n, d)
            if 2 * d < n:
                dense = dense + other
            d *= 2
        if iteration < ITERS - 1:
            dense, u = call(
                next_sweep,
                (tile_live, tile_tgt, idx, dense, other, b_all, et_all, tot, kern, la),
                (wide, tall),
                scratch=[w_work, *work],
                smem=2,
            )
    out = jax.ShapeDtypeStruct((local, block), f32)
    src, tgt = call(
        last_kernel,
        (me, dense, other, b_all, et_all, tot, u),
        (out, out),
        scratch=[w_work],
        smem=1,
    )
    return (src.reshape(-1), tgt.reshape(-1))


def solution(mesh):
    split = P(("pairs", "src"))
    rows = P(("pairs", "src"), None)
    in_specs = (rows, P(("pairs", "src"), None, None, None), rows) + (split,) * 6
    return jax.shard_map(
        shards, mesh=mesh, in_specs=in_specs, out_specs=(split, split), check_vma=False
    )
```

```python
import functools

import jax
import jax.numpy as jnp
from jax import lax
from jax.experimental import pallas as pl
from jax.experimental.pallas import tpu as pltpu
from jax.sharding import PartitionSpec as P

ITERS = 3
EPS = 0.1
RHO = 1.0
ALPHA = 0.5
F = RHO / (RHO + EPS)
STEP = 4
HALVINGS = 1
PIECES = 4

VMEM = pltpu.VMEM
SMEM = pltpu.SMEM
NT = (((1,), (1,)), ((), ()))


def diag_mask(block):
    return lax.broadcasted_iota(jnp.int32, (block, block), 0) == lax.broadcasted_iota(
        jnp.int32, (block, block), 1
    )


def to_column(row, mask):
    return jnp.sum(jnp.where(mask, row, 0.0), axis=1, keepdims=True)


def to_row(column, mask):
    return jnp.sum(jnp.where(mask, column, 0.0), axis=0, keepdims=True)


def total_of(x):
    return jnp.sum(jnp.sum(x, axis=0, keepdims=True), axis=1, keepdims=True)


def steps_of(live_s):
    return (live_s + (STEP - 1)) // STEP


def build_kernel(first, live, x_ref, feat, lin_ref, mass_ref, k_ref, la_ref, ybuf, sems):
    blocks, slots, block, width = ybuf.shape

    def copy(s):
        return pltpu.make_async_copy(feat.at[first + s], ybuf.at[s], sems.at[s])

    for s in range(blocks):
        copy(s).start()
    mask = diag_mask(block)
    ones = jnp.ones((8, width), jnp.bfloat16)
    for s in range(blocks):
        at = first + s
        x = x_ref[at * block : (at + 1) * block, :]
        x32 = x.astype(jnp.float32)
        sq = jnp.sum(x32 * x32, axis=1, keepdims=True)
        lin = to_column(lin_ref[at : at + 1, :], mask)
        base = (2.0 - sq / width - ALPHA * lin) / EPS
        base = jnp.broadcast_to(base, (block, block))
        la = F * jnp.log(to_column(mass_ref[at : at + 1, :], mask))
        la_ref[s * block : (s + 1) * block, :] = jnp.broadcast_to(la, (block, block))
        copy(s).wait()

        def tiles(p, _):
            y = ybuf[s, pl.ds(p * STEP, STEP)].reshape(STEP * block, width)
            y32 = y.astype(jnp.float32)
            y2 = y32 * y32
            y2 = y2[:, : width // 2] + y2[:, width // 2 :]
            hi = y2.astype(jnp.bfloat16)
            lo = (y2 - hi.astype(jnp.float32)).astype(jnp.bfloat16)
            both = jnp.concatenate([hi, lo], axis=1)
            cross = lax.dot_general(x, y, NT, preferred_element_type=jnp.float32)
            ysq = lax.dot_general(ones, both, NT, preferred_element_type=jnp.float32)
            for q in range(STEP):
                cols = slice(q * block, (q + 1) * block)
                e = (2.0 / (width * EPS)) * cross[:, cols] + (
                    base - ysq[0:1, cols] * (1.0 / (width * EPS))
                )
                start = pl.multiple_of((s * slots + p * STEP + q) * block, block)
                k_ref[pl.ds(start, block), :] = jnp.exp(e)
            return 0

        lax.fori_loop(0, steps_of(live[at]), tiles, 0)


def sweep(live, tgt, flip, idx_ref, w_ref, k_refs, la_refs, outs, acc_ref, u_ref, col_ref):
    blocks, slots = tgt.shape
    block = w_ref.shape[1]
    every = w_ref.shape[0] - 8
    each = blocks // len(k_refs)
    w_ref[every:, :] = jnp.zeros((8, block), jnp.float32)
    for s in range(blocks):
        k_ref = k_refs[s // each]

        def add_row(p, acc):
            for q in range(STEP):
                k = p * STEP + q
                row = jnp.where(k < live[s], tgt[s, k] ^ flip, every)
                start = pl.multiple_of(((s % each) * slots + k) * block, block)
                acc = acc + k_ref[pl.ds(start, block), :] * w_ref[pl.ds(row, 1), :]
            return acc

        acc_ref[s * block : (s + 1) * block, :] = lax.fori_loop(
            0, steps_of(live[s]), add_row, jnp.zeros((block, block), jnp.float32)
        )
    for s in range(blocks):
        rows = pl.ds(s * block, block)
        total = jnp.sum(acc_ref[rows, :], axis=1, keepdims=True)
        la = la_refs[s // each][pl.ds((s % each) * block, block), :]
        u_ref[rows, :] = jnp.exp(la - F * jnp.log(total))
    col_ref[...] = jnp.zeros_like(col_ref)
    for s in range(blocks):
        k_ref = k_refs[s // each]
        u = u_ref[s * block : (s + 1) * block, :]

        def add_col(p, _):
            for q in range(STEP):
                k = p * STEP + q
                start = pl.multiple_of(((s % each) * slots + k) * block, block)
                col_ref[pl.ds(s * slots + k, 1), :] = jnp.sum(
                    k_ref[pl.ds(start, block), :] * u, axis=0, keepdims=True
                )
            return 0

        lax.fori_loop(0, steps_of(live[s]), add_col, 0)
    col = col_ref[...]
    rows = lax.broadcasted_iota(jnp.int32, (every, blocks * slots), 0)
    idx = idx_ref[...]
    hit = jnp.where(rows == (idx ^ flip), 1.0, 0.0).astype(jnp.bfloat16)
    dense = jnp.zeros((every, block), jnp.float32)
    for _ in range(3):
        piece = col.astype(jnp.bfloat16)
        dense += jnp.dot(hit, piece, preferred_element_type=jnp.float32)
        col = col - piece.astype(jnp.float32)
    at = 0
    for out in outs:
        out[...] = dense[at : at + out.shape[0], :]
        at += out.shape[0]


def power_of_ratio(num, den):
    return jnp.exp(F * (jnp.log(num) - jnp.log(den)))


def first_sweep(npieces, halves, live, tgt, me, idx_ref, *refs):
    k_refs, la_refs = refs[:npieces], refs[npieces : 2 * npieces]
    parts = refs[2 * npieces : 2 * npieces + 2]
    refs = refs[2 * npieces + 2 :]
    outs = refs[:2]
    b_ref, et_ref, tot_ref, w_ref, acc_ref, u_ref, col_ref = refs[2:]
    every = b_ref.shape[0]
    local = tgt.shape[0]
    n = every // local
    low = me[0] & ((1 << halves) - 1)
    flip = low * (every >> halves)
    am = jnp.zeros((1, 1), jnp.float32)
    bits = n.bit_length() - 1
    for at in range(n):
        m = sum(((at >> r) & 1) << (bits - 1 - r) for r in range(bits))
        part = parts[at // (n // 2)]
        at = (at % (n // 2)) * 3 * local
        owner = (me[0] ^ m) * local
        rows = pl.ds(pl.multiple_of(owner ^ flip, local), local)
        b = part[at : at + local, :]
        et = jnp.exp((-ALPHA / EPS) * part[at + local : at + 2 * local, :])
        b_ref[rows, :] = b
        et_ref[rows, :] = et
        w_ref[rows, :] = jnp.where(b > 0.0, et, 0.0)
        am += total_of(part[at + 2 * local : at + 3 * local, :])
    tot = jnp.sqrt(am * total_of(b_ref[...]))
    tot_ref[...] = jnp.broadcast_to(tot, tot_ref.shape)
    sweep(live, tgt, flip, idx_ref, w_ref, k_refs, la_refs, outs, acc_ref, u_ref, col_ref)


def new_scale(sums, b_ref, et_ref, tot_ref, t_ref):
    mass = jnp.zeros((1, b_ref.shape[1]), jnp.float32)
    at = 0
    for terms in sums:
        rows = slice(at, at + terms[0].shape[0])
        at = rows.stop
        b = b_ref[rows, :]
        col = functools.reduce(lambda p, q: p + q, [t[...] for t in terms]) * et_ref[rows, :]
        t = jnp.where(b > 0.0, power_of_ratio(b, col), 0.0)
        t_ref[rows, :] = t
        mass += jnp.sum(t * col, axis=0, keepdims=True)
    return jnp.sqrt(tot_ref[0:1, 0:1] / jnp.sum(mass, axis=1, keepdims=True))


def next_sweep(
    npieces, halves, live, tgt, me, idx_ref, keep, other, b_ref, et_ref, tot_ref, *refs
):
    k_refs, la_refs = refs[:npieces], refs[npieces : 2 * npieces]
    out0, out1, u_ref, w_ref, acc_ref, col_ref = refs[2 * npieces :]
    every = b_ref.shape[0]
    flip = (me[0] & ((1 << halves) - 1)) * (every >> halves)
    factor = new_scale([[keep], [other]], b_ref, et_ref, tot_ref, w_ref)
    w_ref[:every, :] = w_ref[:every, :] * (factor * et_ref[...])
    sweep(
        live, tgt, flip, idx_ref, w_ref, k_refs, la_refs, (out0, out1), acc_ref, u_ref, col_ref
    )


def last_kernel(halves, me, keep, other, b_ref, et_ref, tot_ref, u_ref, src_ref, tgt_ref, t_ref):
    local, block = src_ref.shape
    every = b_ref.shape[0]
    flip = (me[0] & ((1 << halves) - 1)) * (every >> halves)
    factor = new_scale([[keep], [other]], b_ref, et_ref, tot_ref, t_ref)
    own = pl.multiple_of((me[0] * local) ^ flip, local)
    tgt_ref[...] = t_ref[pl.ds(own, local), :] * factor
    mask = diag_mask(block)
    for s in range(local):
        src_ref[s : s + 1, :] = to_row(u_ref[s * block : (s + 1) * block, :] * factor, mask)


def call(kernel, ins, outs, scratch=(), smem=0, hbm=(), vmem_mb=32, **cost):
    specs = [pl.BlockSpec(memory_space=SMEM)] * smem
    for at in range(smem, len(ins)):
        specs.append(pl.BlockSpec(memory_space=pl.ANY if at in hbm else VMEM))
    ins = [
        pltpu.with_memory_space_constraint(x, pltpu.HBM) if at in hbm else x
        for at, x in enumerate(ins)
    ]
    return pl.pallas_call(
        kernel,
        out_shape=outs,
        in_specs=specs,
        out_specs=[pl.BlockSpec(memory_space=VMEM)] * len(outs),
        scratch_shapes=scratch,
        compiler_params=pltpu.CompilerParams(vmem_limit_bytes=vmem_mb << 20),
        cost_estimate=pl.CostEstimate(**cost) if cost else None,
    )(*ins)


def exchange(x, n, d):
    return lax.ppermute(x, "src", [(i, i ^ d) for i in range(n)])


def shards(
    src_feat, tile_feat, tile_tgt, tile_live, src_lin, tgt_lin, src_mass, tgt_mass, tgt_count
):
    f32 = jnp.float32
    local, slots, block, width = tile_feat.shape
    n = lax.axis_size("src")
    me = lax.axis_index("src").astype(jnp.int32).reshape(1)
    every = local * n
    pairs = local * slots
    valid = lax.broadcasted_iota(jnp.int32, (local, block), 1) < tgt_count[:, None]
    bmass = jnp.where(valid, tgt_mass.reshape(local, block), 0.0)
    amass = src_mass.reshape(local, block)
    part = jnp.concatenate([bmass, tgt_lin.reshape(local, block), amass], axis=0)

    def shape(rows, dtype=f32):
        return pltpu.VMEM((rows, block), dtype)

    each = local // PIECES
    order = []
    d = n // 2
    while d:
        order.append(d)
        d //= 2
    kern, la = [], []
    feat = tile_feat
    parts = None
    for at, d in enumerate(order):
        got = exchange(part, n, d)
        if at < PIECES:
            k_piece, la_piece = call(
                functools.partial(build_kernel, at * each),
                (tile_live, src_feat, feat, src_lin.reshape(local, block), amass),
                (shape(each * slots * block), shape(each * block)),
                scratch=[
                    VMEM((each, slots, block, width), tile_feat.dtype),
                    pltpu.SemaphoreType.DMA((each,)),
                ],
                smem=1,
                hbm=(2,),
                flops=2 * each * slots * block * block * width,
                bytes_accessed=2 * each * slots * block * width,
                transcendentals=each * slots * block * block,
            )
            kern.append(k_piece)
            la.append(la_piece)
        if d > 1:
            part = jnp.stack([part, got], axis=0)
            part = part.reshape(-1, block)
            if at < PIECES:
                part, feat, k_piece = lax.optimization_barrier((part, feat, kern[-1]))
                kern[-1] = k_piece
        else:
            parts = (part, got)
    slot = lax.broadcasted_iota(jnp.int32, (local, slots), 1)
    idx = jnp.where(slot < tile_live[:, None], tile_tgt, -1).reshape(1, pairs)
    half = every >> HALVINGS
    acc = VMEM((local * block, block), f32)
    col = VMEM((pairs, block), f32)
    w = VMEM((every + 8, block), f32)
    keep, send, b_all, et_all, tot = call(
        functools.partial(first_sweep, PIECES, HALVINGS),
        (tile_live, tile_tgt, me, idx, *kern, *la, *parts),
        (shape(half), shape(half), shape(every), shape(every), shape(8)),
        scratch=[w, acc, VMEM((local * block, block), f32), col],
        smem=3,
    )
    u = None
    for iteration in range(ITERS):
        keep = keep + exchange(send, n, 1)
        d = 2
        while d < n:
            keep = keep + exchange(keep, n, d)
            d *= 2
        other = exchange(keep, n, 1)
        if iteration < ITERS - 1:
            keep, send, u = call(
                functools.partial(next_sweep, PIECES, HALVINGS),
                (tile_live, tile_tgt, me, idx, keep, other, b_all, et_all, tot, *kern, *la),
                (shape(half), shape(half), shape(local * block)),
                scratch=[w, acc, col],
                smem=3,
            )
    src, tgt = call(
        functools.partial(last_kernel, HALVINGS),
        (me, keep, other, b_all, et_all, tot, u),
        [jax.ShapeDtypeStruct((local, block), f32)] * 2,
        scratch=[VMEM((every, block), f32)],
        smem=1,
    )
    return (src.reshape(-1), tgt.reshape(-1))


def solution(mesh):
    split = P(("pairs", "src"))
    rows = P(("pairs", "src"), None)
    in_specs = (rows, P(("pairs", "src"), None, None, None), rows) + (split,) * 6
    return jax.shard_map(
        shards, mesh=mesh, in_specs=in_specs, out_specs=(split, split), check_vma=False
    )
```

```python
import functools

import jax
import jax.numpy as jnp
from jax import lax
from jax.experimental import pallas as pl
from jax.experimental.pallas import tpu as pltpu
from jax.sharding import PartitionSpec as P

ITERS = 3
EPS = 0.1
RHO = 1.0
ALPHA = 0.5
F = RHO / (RHO + EPS)
STEP = 4
PIECES = 4

VMEM = pltpu.VMEM
SMEM = pltpu.SMEM
NT = (((1,), (1,)), ((), ()))


def diag_mask(block):
    return lax.broadcasted_iota(jnp.int32, (block, block), 0) == lax.broadcasted_iota(
        jnp.int32, (block, block), 1
    )


def to_column(row, mask):
    return jnp.sum(jnp.where(mask, row, 0.0), axis=1, keepdims=True)


def to_row(column, mask):
    return jnp.sum(jnp.where(mask, column, 0.0), axis=0, keepdims=True)


def total_of(x):
    return jnp.sum(jnp.sum(x, axis=0, keepdims=True), axis=1, keepdims=True)


def steps_of(live_s):
    return (live_s + (STEP - 1)) // STEP


def build_tiles(live, first, x_ref, lin_ref, mass_ref, feat, waits, k_ref, la_ref):
    blocks, slots, block, width = feat.shape
    mask = diag_mask(block)
    for s in range(blocks):
        at = first + s
        x = x_ref[at * block : (at + 1) * block, :]
        x32 = x.astype(jnp.float32)
        sq = jnp.sum(x32 * x32, axis=1, keepdims=True)
        lin = to_column(lin_ref[at : at + 1, :], mask)
        base = (2.0 - sq / width - ALPHA * lin) / EPS
        base = jnp.broadcast_to(base, (block, block))
        la = F * jnp.log(to_column(mass_ref[at : at + 1, :], mask))
        la_ref[s * block : (s + 1) * block, :] = jnp.broadcast_to(la, (block, block))
        if waits:
            waits[s].wait()

        def tiles(p, _):
            y = feat[s, pl.ds(p * STEP, STEP)].reshape(STEP * block, width)
            y32 = y.astype(jnp.float32)
            y2 = y32 * y32
            ysq = jnp.sum(y2[:, : width // 2] + y2[:, width // 2 :], axis=1, keepdims=True)
            cross = lax.dot_general(x, y, NT, preferred_element_type=jnp.float32)
            for q in range(STEP):
                cols = slice(q * block, (q + 1) * block)
                row = to_row(ysq[cols, :], mask)
                e = (2.0 / (width * EPS)) * cross[:, cols] + (base - row * (1.0 / (width * EPS)))
                start = pl.multiple_of((s * slots + p * STEP + q) * block, block)
                k_ref[pl.ds(start, block), :] = jnp.exp(e)
            return 0

        lax.fori_loop(0, steps_of(live[at]), tiles, 0)


def first_build(live_hbm, x_hbm, feat, lin_hbm, mass_hbm, *refs):
    k_ref, la_ref, x_ref, lin_ref, mass_ref, *rest = refs
    later, (live, own, sems) = rest[:-3], rest[-3:]
    each = own.shape[0]
    copies = [(live_hbm, live), (x_hbm, x_ref), (lin_hbm, lin_ref), (mass_hbm, mass_ref)]
    copies += [(feat.at[s], own.at[s]) for s in range(each)]
    copies += [(feat.at[pl.ds((i + 1) * each, each)], to) for i, to in enumerate(later)]
    copies = [pltpu.make_async_copy(f, t, sems.at[i]) for i, (f, t) in enumerate(copies)]
    for c in copies:
        c.start()
    for c in copies[:4]:
        c.wait()
    build_tiles(
        live, 0, x_ref, lin_ref, mass_ref, own, copies[4 : 4 + each], k_ref, la_ref
    )
    for c in copies[4 + each :]:
        c.wait()


def later_build(first, live, x_ref, feat, lin_ref, mass_ref, k_ref, la_ref):
    build_tiles(live, first, x_ref, lin_ref, mass_ref, feat, (), k_ref, la_ref)


def sweep(live, tgt, idx_ref, w_ref, k_refs, la_refs, dense_ref, acc_ref, u_ref, col_ref):
    blocks, slots = tgt.shape
    block = w_ref.shape[1]
    every = w_ref.shape[0] - 8
    each = blocks // len(k_refs)
    w_ref[every:, :] = jnp.zeros((8, block), jnp.float32)
    for s in range(blocks):
        k_ref = k_refs[s // each]

        def add_row(p, acc):
            for q in range(STEP):
                k = p * STEP + q
                row = jnp.where(k < live[s], tgt[s, k], every)
                start = pl.multiple_of(((s % each) * slots + k) * block, block)
                acc = acc + k_ref[pl.ds(start, block), :] * w_ref[pl.ds(row, 1), :]
            return acc

        acc_ref[s * block : (s + 1) * block, :] = lax.fori_loop(
            0, steps_of(live[s]), add_row, jnp.zeros((block, block), jnp.float32)
        )
    for s in range(blocks):
        rows = pl.ds(s * block, block)
        total = jnp.sum(acc_ref[rows, :], axis=1, keepdims=True)
        la = la_refs[s // each][pl.ds((s % each) * block, block), :]
        u_ref[rows, :] = jnp.exp(la - F * jnp.log(total))
    col_ref[...] = jnp.zeros_like(col_ref)
    for s in range(blocks):
        k_ref = k_refs[s // each]
        u = u_ref[s * block : (s + 1) * block, :]

        def add_col(p, _):
            for q in range(STEP):
                k = p * STEP + q
                start = pl.multiple_of(((s % each) * slots + k) * block, block)
                col_ref[pl.ds(s * slots + k, 1), :] = jnp.sum(
                    k_ref[pl.ds(start, block), :] * u, axis=0, keepdims=True
                )
            return 0

        lax.fori_loop(0, steps_of(live[s]), add_col, 0)
    col = col_ref[...]
    rows = lax.broadcasted_iota(jnp.int32, (every, blocks * slots), 0)
    hit = jnp.where(rows == idx_ref[...], 1.0, 0.0).astype(jnp.bfloat16)
    dense = jnp.zeros((every, block), jnp.float32)
    for _ in range(3):
        piece = col.astype(jnp.bfloat16)
        dense += jnp.dot(hit, piece, preferred_element_type=jnp.float32)
        col = col - piece.astype(jnp.float32)
    dense_ref[...] = dense


def power_of_ratio(num, den):
    return jnp.exp(F * (jnp.log(num) - jnp.log(den)))


def first_sweep(npieces, live, tgt, me, idx_ref, *refs):
    k_refs, la_refs = refs[:npieces], refs[npieces : 2 * npieces]
    parts = refs[2 * npieces : 2 * npieces + 2]
    dense_ref, b_ref, et_ref, tot_ref, w_ref, acc_ref, u_ref, col_ref = refs[2 * npieces + 2 :]
    local = tgt.shape[0]
    n = b_ref.shape[0] // local
    bits = n.bit_length() - 1
    am = jnp.zeros((local, b_ref.shape[1]), jnp.float32)
    for at in range(n):
        m = sum(((at >> r) & 1) << (bits - 1 - r) for r in range(bits))
        part = parts[at // (n // 2)]
        at = (at % (n // 2)) * 3 * local
        rows = pl.ds(pl.multiple_of((me[0] ^ m) * local, local), local)
        b = part[at : at + local, :]
        et = jnp.exp((-ALPHA / EPS) * part[at + local : at + 2 * local, :])
        b_ref[rows, :] = b
        et_ref[rows, :] = et
        w_ref[rows, :] = jnp.where(b > 0.0, et, 0.0)
        am += part[at + 2 * local : at + 3 * local, :]
    tot = jnp.sqrt(total_of(am) * total_of(b_ref[...]))
    tot_ref[...] = jnp.broadcast_to(tot, tot_ref.shape)
    sweep(live, tgt, idx_ref, w_ref, k_refs, la_refs, dense_ref, acc_ref, u_ref, col_ref)


def new_scale(me, mine, other, b_ref, et_ref, tot_ref):
    b = b_ref[...]
    col = jnp.where((me[0] & 1) == 1, mine[...], other[...]) * et_ref[...]
    t = jnp.where(b > 0.0, power_of_ratio(b, col), 0.0)
    return t, jnp.sqrt(tot_ref[0:1, 0:1] / total_of(t * col))


def next_sweep(npieces, live, tgt, me, idx_ref, mine, other, b_ref, et_ref, tot_ref, *refs):
    k_refs, la_refs = refs[:npieces], refs[npieces : 2 * npieces]
    dense_ref, u_ref, w_ref, acc_ref, col_ref = refs[2 * npieces :]
    t, factor = new_scale(me, mine, other, b_ref, et_ref, tot_ref)
    w_ref[: b_ref.shape[0], :] = t * (factor * et_ref[...])
    sweep(live, tgt, idx_ref, w_ref, k_refs, la_refs, dense_ref, acc_ref, u_ref, col_ref)


def last_kernel(me, mine, other, b_ref, et_ref, tot_ref, u_ref, src_ref, tgt_ref, t_ref):
    local, block = src_ref.shape
    t, factor = new_scale(me, mine, other, b_ref, et_ref, tot_ref)
    t_ref[...] = t * factor
    tgt_ref[...] = t_ref[pl.ds(pl.multiple_of(me[0] * local, local), local), :]
    mask = diag_mask(block)
    for s in range(local):
        src_ref[s : s + 1, :] = to_row(u_ref[s * block : (s + 1) * block, :] * factor, mask)


def call(kernel, ins, outs, scratch=(), smem=0, hbm=(), vmem_mb=12, **cost):
    specs = [pl.BlockSpec(memory_space=SMEM)] * smem
    for at in range(smem, len(ins)):
        specs.append(pl.BlockSpec(memory_space=pl.ANY if at in hbm else VMEM))
    ins = [
        pltpu.with_memory_space_constraint(x, pltpu.HBM) if at in hbm else x
        for at, x in enumerate(ins)
    ]
    return pl.pallas_call(
        kernel,
        out_shape=outs,
        in_specs=specs,
        out_specs=[pl.BlockSpec(memory_space=VMEM)] * len(outs),
        scratch_shapes=scratch,
        compiler_params=pltpu.CompilerParams(vmem_limit_bytes=vmem_mb << 20),
        cost_estimate=pl.CostEstimate(**cost) if cost else None,
    )(*ins)


def exchange(x, n, d, cores=(0, 1)):
    return lax.ppermute(x, "src", [(i, i ^ d) for i in range(n) if i & 1 in cores])


def shards(
    src_feat, tile_feat, tile_tgt, tile_live, src_lin, tgt_lin, src_mass, tgt_mass, tgt_count
):
    f32 = jnp.float32
    local, slots, block, width = tile_feat.shape
    n = lax.axis_size("src")
    me = lax.axis_index("src").astype(jnp.int32).reshape(1)
    every = local * n
    pairs = local * slots
    lin = src_lin.reshape(local, block)
    amass = src_mass.reshape(local, block)
    part = jnp.concatenate([tgt_mass, tgt_lin, src_mass]).reshape(3 * local, block)
    count = jnp.concatenate([tgt_count, jnp.full((2 * local,), block, jnp.int32)])
    part = jnp.where(lax.broadcasted_iota(jnp.int32, part.shape, 1) < count[:, None], part, 0.0)

    def shape(rows, cols=block, dtype=f32):
        return pltpu.VMEM((rows, cols), dtype)

    each = local // PIECES
    feats = pltpu.VMEM((each, slots, block, width), tile_feat.dtype)
    cost = dict(
        flops=2 * each * slots * block * block * width,
        bytes_accessed=2 * each * slots * block * width,
        transcendentals=each * slots * block * block,
    )
    order = []
    d = n // 2
    while d:
        order.append(d)
        d //= 2
    kern, la = [], []
    for at, d in enumerate(order):
        got = exchange(part, n, d)
        if at == 0:
            k0, la0, xv, linv, massv, *later = call(
                first_build,
                (tile_live, src_feat, tile_feat, lin, amass),
                (
                    shape(each * slots * block),
                    shape(each * block),
                    shape(local * block, width, src_feat.dtype),
                    shape(local),
                    shape(local),
                    *[feats] * (PIECES - 1),
                ),
                scratch=[
                    SMEM((local,), jnp.int32),
                    feats,
                    pltpu.SemaphoreType.DMA((4 + each + PIECES - 1,)),
                ],
                hbm=(0, 1, 2, 3, 4),
                **cost,
            )
            kern.append(k0)
            la.append(la0)
        elif at < PIECES:
            k0, la0 = call(
                functools.partial(later_build, at * each),
                (tile_live, xv, later[at - 1], linv, massv),
                (shape(each * slots * block), shape(each * block)),
                smem=1,
                **cost,
            )
            kern.append(k0)
            la.append(la0)
        if d > 1:
            part = jnp.stack([part, got], axis=0).reshape(-1, block)
            if at < PIECES - 1:
                part, later[at], kern[-1] = lax.optimization_barrier(
                    (part, later[at], kern[-1])
                )
    slot = lax.broadcasted_iota(jnp.int32, (local, slots), 1)
    idx = jnp.where(slot < tile_live[:, None], tile_tgt, -1).reshape(1, pairs)
    acc = VMEM((local * block, block), f32)
    col = VMEM((pairs, block), f32)
    w = VMEM((every + 8, block), f32)
    mine, b_all, et_all, tot = call(
        functools.partial(first_sweep, PIECES),
        (tile_live, tile_tgt, me, idx, *kern, *la, part, got),
        (shape(every), shape(every), shape(every), shape(8)),
        scratch=[w, acc, acc, col],
        smem=3,
    )
    u = None
    for iteration in range(ITERS):
        mine = mine + exchange(mine, n, 1, (0,))
        d = 2
        while d < n:
            mine = mine + exchange(mine, n, d, (1,))
            d *= 2
        other = exchange(mine, n, 1, (1,))
        if iteration < ITERS - 1:
            mine, u = call(
                functools.partial(next_sweep, PIECES),
                (tile_live, tile_tgt, me, idx, mine, other, b_all, et_all, tot, *kern, *la),
                (shape(every), shape(local * block)),
                scratch=[w, acc, col],
                smem=3,
            )
    src, tgt = call(
        last_kernel,
        (me, mine, other, b_all, et_all, tot, u),
        [jax.ShapeDtypeStruct((local, block), f32)] * 2,
        scratch=[VMEM((every, block), f32)],
        smem=1,
    )
    return (src.reshape(-1), tgt.reshape(-1))


def solution(mesh):
    split = P(("pairs", "src"))
    rows = P(("pairs", "src"), None)
    in_specs = (rows, P(("pairs", "src"), None, None, None), rows) + (split,) * 6
    return jax.shard_map(
        shards, mesh=mesh, in_specs=in_specs, out_specs=(split, split), check_vma=False
    )
```

```python
import functools

import jax
import jax.numpy as jnp
from jax import lax
from jax.experimental import pallas as pl
from jax.experimental.pallas import tpu as pltpu
from jax.sharding import PartitionSpec as P

ITERS = 3
EPS = 0.1
RHO = 1.0
ALPHA = 0.5
F = RHO / (RHO + EPS)
STEP = 4
PIECES = 4

VMEM = pltpu.VMEM
SMEM = pltpu.SMEM
NT = (((1,), (1,)), ((), ()))


def diag_mask(block):
    return lax.broadcasted_iota(jnp.int32, (block, block), 0) == lax.broadcasted_iota(
        jnp.int32, (block, block), 1
    )


def to_column(row, mask):
    return jnp.sum(jnp.where(mask, row, 0.0), axis=1, keepdims=True)


def to_row(column, mask):
    return jnp.sum(jnp.where(mask, column, 0.0), axis=0, keepdims=True)


def position():
    return lax.axis_index("src").astype(jnp.int32)


def total_of(x):
    return jnp.sum(jnp.sum(x, axis=0, keepdims=True), axis=1, keepdims=True)


def steps_of(live_s):
    return (live_s + (STEP - 1)) // STEP


def pack_kernel(count_hbm, mass_hbm, lin_hbm, amass_hbm, out_ref, count, sems):
    local, block = mass_hbm.shape
    copies = [(count_hbm, count)]
    for i, x in enumerate((mass_hbm, lin_hbm, amass_hbm)):
        copies.append((x, out_ref.at[pl.ds(i * local, local)]))
    copies = [pltpu.make_async_copy(f, t, sems.at[i]) for i, (f, t) in enumerate(copies)]
    for c in copies:
        c.start()
    for c in copies:
        c.wait()
    lane = lax.broadcasted_iota(jnp.int32, (1, block), 1)
    for i in range(local):
        row = slice(i, i + 1)
        out_ref[row, :] = jnp.where(lane < count[i], out_ref[row, :], 0.0)


def build_tiles(live, first, x_ref, lin_ref, mass_ref, feat, waits, k_ref, la_ref):
    blocks, slots, block, width = feat.shape
    mask = diag_mask(block)
    for s in range(blocks):
        at = first + s
        x = x_ref[at * block : (at + 1) * block, :]
        x32 = x.astype(jnp.float32)
        sq = jnp.sum(x32 * x32, axis=1, keepdims=True)
        lin = to_column(lin_ref[at : at + 1, :], mask)
        base = (2.0 - sq / width - ALPHA * lin) / EPS
        base = jnp.broadcast_to(base, (block, block))
        la = F * jnp.log(to_column(mass_ref[at : at + 1, :], mask))
        la_ref[s * block : (s + 1) * block, :] = jnp.broadcast_to(la, (block, block))
        if waits:
            waits[s].wait()

        def tiles(p, _):
            y = feat[s, pl.ds(p * STEP, STEP)].reshape(STEP * block, width)
            y32 = y.astype(jnp.float32)
            y2 = y32 * y32
            ysq = jnp.sum(y2[:, : width // 2] + y2[:, width // 2 :], axis=1, keepdims=True)
            cross = lax.dot_general(x, y, NT, preferred_element_type=jnp.float32)
            for q in range(STEP):
                cols = slice(q * block, (q + 1) * block)
                row = to_row(ysq[cols, :], mask)
                e = (2.0 / (width * EPS)) * cross[:, cols] + (base - row * (1.0 / (width * EPS)))
                start = pl.multiple_of((s * slots + p * STEP + q) * block, block)
                k_ref[pl.ds(start, block), :] = jnp.exp(e)
            return 0

        lax.fori_loop(0, steps_of(live[at]), tiles, 0)


def first_build(live_hbm, tgt_hbm, x_hbm, feat, lin_hbm, mass_hbm, *refs):
    k_ref, la_ref, hit_ref, x_ref, lin_ref, mass_ref, *rest = refs
    later, (live, tgt, flags, own, sems) = rest[:-5], rest[-5:]
    each = own.shape[0]
    slots = tgt.shape[1]
    copies = [(live_hbm, live), (x_hbm, x_ref), (lin_hbm, lin_ref), (mass_hbm, mass_ref)]
    copies += [(tgt_hbm, tgt)]
    copies += [(feat.at[s], own.at[s]) for s in range(each)]
    copies += [(feat.at[pl.ds((i + 1) * each, each)], to) for i, to in enumerate(later)]
    copies = [pltpu.make_async_copy(f, t, sems.at[i]) for i, (f, t) in enumerate(copies)]
    for c in copies:
        c.start()
    for c in copies[:5]:
        c.wait()
    lane = lax.broadcasted_iota(jnp.int32, (1, flags.shape[1]), 1)
    for at in range(flags.shape[0]):
        s, k = divmod(at, slots)
        row = jnp.where(k < live[s], tgt[s, k], -1)
        flags[at : at + 1, :] = jnp.where(lane == row, 1.0, 0.0)
    hit_ref[...] = jnp.transpose(flags[...]).astype(jnp.bfloat16)
    build_tiles(
        live, 0, x_ref, lin_ref, mass_ref, own, copies[5 : 5 + each], k_ref, la_ref
    )
    for c in copies[5 + each :]:
        c.wait()


def later_build(first, live, x_ref, feat, lin_ref, mass_ref, k_ref, la_ref):
    build_tiles(live, first, x_ref, lin_ref, mass_ref, feat, (), k_ref, la_ref)


def sweep(live, tgt, hit_ref, w_ref, k_refs, la_refs, dense_ref, acc_ref, u_ref, col_ref):
    blocks, slots = tgt.shape
    block = w_ref.shape[1]
    every = w_ref.shape[0] - 8
    each = blocks // len(k_refs)
    w_ref[every:, :] = jnp.zeros((8, block), jnp.float32)
    for s in range(blocks):
        k_ref = k_refs[s // each]

        def add_row(p, acc):
            for q in range(STEP):
                k = p * STEP + q
                row = jnp.where(k < live[s], tgt[s, k], every)
                start = pl.multiple_of(((s % each) * slots + k) * block, block)
                acc = acc + k_ref[pl.ds(start, block), :] * w_ref[pl.ds(row, 1), :]
            return acc

        acc_ref[s * block : (s + 1) * block, :] = lax.fori_loop(
            0, steps_of(live[s]), add_row, jnp.zeros((block, block), jnp.float32)
        )
    for s in range(blocks):
        rows = pl.ds(s * block, block)
        total = jnp.sum(acc_ref[rows, :], axis=1, keepdims=True)
        la = la_refs[s // each][pl.ds((s % each) * block, block), :]
        u_ref[rows, :] = jnp.exp(la - F * jnp.log(total))
    col_ref[...] = jnp.zeros_like(col_ref)
    for s in range(blocks):
        k_ref = k_refs[s // each]
        u = u_ref[s * block : (s + 1) * block, :]

        def add_col(p, _):
            for q in range(STEP):
                k = p * STEP + q
                start = pl.multiple_of(((s % each) * slots + k) * block, block)
                col_ref[pl.ds(s * slots + k, 1), :] = jnp.sum(
                    k_ref[pl.ds(start, block), :] * u, axis=0, keepdims=True
                )
            return 0

        lax.fori_loop(0, steps_of(live[s]), add_col, 0)
    col = col_ref[...]
    hit = hit_ref[...]
    dense = jnp.zeros((every, block), jnp.float32)
    for _ in range(3):
        piece = col.astype(jnp.bfloat16)
        dense += jnp.dot(hit, piece, preferred_element_type=jnp.float32)
        col = col - piece.astype(jnp.float32)
    dense_ref[...] = dense


def power_of_ratio(num, den):
    return jnp.exp(F * (jnp.log(num) - jnp.log(den)))


def first_sweep(npieces, live, tgt, hit_ref, *refs):
    k_refs, la_refs = refs[:npieces], refs[npieces : 2 * npieces]
    parts = refs[2 * npieces : 2 * npieces + 2]
    dense_ref, b_ref, et_ref, tot_ref, w_ref, acc_ref, u_ref, col_ref = refs[2 * npieces + 2 :]
    local = tgt.shape[0]
    n = b_ref.shape[0] // local
    bits = n.bit_length() - 1
    am = jnp.zeros((local, b_ref.shape[1]), jnp.float32)
    for at in range(n):
        m = sum(((at >> r) & 1) << (bits - 1 - r) for r in range(bits))
        part = parts[at // (n // 2)]
        at = (at % (n // 2)) * 3 * local
        rows = pl.ds(pl.multiple_of((position() ^ m) * local, local), local)
        b = part[at : at + local, :]
        et = jnp.exp((-ALPHA / EPS) * part[at + local : at + 2 * local, :])
        b_ref[rows, :] = b
        et_ref[rows, :] = et
        w_ref[rows, :] = jnp.where(b > 0.0, et, 0.0)
        am += part[at + 2 * local : at + 3 * local, :]
    tot = jnp.sqrt(total_of(am) * total_of(b_ref[...]))
    tot_ref[...] = jnp.broadcast_to(tot, tot_ref.shape)
    sweep(live, tgt, hit_ref, w_ref, k_refs, la_refs, dense_ref, acc_ref, u_ref, col_ref)


def new_scale(mine, other, b_ref, et_ref, tot_ref):
    b = b_ref[...]
    col = jnp.where(position() & 1 == 1, mine[...], other[...]) * et_ref[...]
    t = jnp.where(b > 0.0, power_of_ratio(b, col), 0.0)
    return t, jnp.sqrt(tot_ref[0:1, 0:1] / total_of(t * col))


def next_sweep(npieces, live, tgt, hit_ref, mine, other, b_ref, et_ref, tot_ref, *refs):
    k_refs, la_refs = refs[:npieces], refs[npieces : 2 * npieces]
    dense_ref, u_ref, w_ref, acc_ref, col_ref = refs[2 * npieces :]
    t, factor = new_scale(mine, other, b_ref, et_ref, tot_ref)
    w_ref[: b_ref.shape[0], :] = t * (factor * et_ref[...])
    sweep(live, tgt, hit_ref, w_ref, k_refs, la_refs, dense_ref, acc_ref, u_ref, col_ref)


def last_kernel(mine, other, b_ref, et_ref, tot_ref, u_ref, src_ref, tgt_ref, t_ref):
    local, block = src_ref.shape
    t, factor = new_scale(mine, other, b_ref, et_ref, tot_ref)
    t_ref[...] = t * factor
    tgt_ref[...] = t_ref[pl.ds(pl.multiple_of(position() * local, local), local), :]
    mask = diag_mask(block)
    for s in range(local):
        src_ref[s : s + 1, :] = to_row(u_ref[s * block : (s + 1) * block, :] * factor, mask)


def call(kernel, ins, outs, scratch=(), smem=0, hbm=(), vmem_mb=12, **cost):
    specs = [pl.BlockSpec(memory_space=SMEM)] * smem
    for at in range(smem, len(ins)):
        specs.append(pl.BlockSpec(memory_space=pl.ANY if at in hbm else VMEM))
    ins = [
        pltpu.with_memory_space_constraint(x, pltpu.HBM) if at in hbm else x
        for at, x in enumerate(ins)
    ]
    return pl.pallas_call(
        kernel,
        out_shape=outs,
        in_specs=specs,
        out_specs=[pl.BlockSpec(memory_space=VMEM)] * len(outs),
        scratch_shapes=scratch,
        compiler_params=pltpu.CompilerParams(vmem_limit_bytes=vmem_mb << 20),
        cost_estimate=pl.CostEstimate(**cost) if cost else None,
    )(*ins)


def exchange(x, n, d, cores=(0, 1)):
    return lax.ppermute(x, "src", [(i, i ^ d if i & 1 in cores else i) for i in range(n)])


def shards(
    src_feat, tile_feat, tile_tgt, tile_live, src_lin, tgt_lin, src_mass, tgt_mass, tgt_count
):
    f32 = jnp.float32
    local, slots, block, width = tile_feat.shape
    n = lax.axis_size("src")
    every = local * n
    pairs = local * slots
    lin = src_lin.reshape(local, block)
    amass = src_mass.reshape(local, block)
    def shape(rows, cols=block, dtype=f32):
        return pltpu.VMEM((rows, cols), dtype)

    (part,) = call(
        pack_kernel,
        (tgt_count, tgt_mass.reshape(local, block), tgt_lin.reshape(local, block), amass),
        (shape(3 * local),),
        scratch=[SMEM((local,), jnp.int32), pltpu.SemaphoreType.DMA((4,))],
        hbm=(0, 1, 2, 3),
    )
    each = local // PIECES
    feats = pltpu.VMEM((each, slots, block, width), tile_feat.dtype)
    cost = dict(
        flops=2 * each * slots * block * block * width,
        bytes_accessed=2 * each * slots * block * width,
        transcendentals=each * slots * block * block,
    )
    order = []
    d = n // 2
    while d:
        order.append(d)
        d //= 2
    kern, la = [], []
    for at, d in enumerate(order):
        got = exchange(part, n, d)
        if at == 0:
            k0, la0, hit, xv, linv, massv, *later = call(
                first_build,
                (tile_live, tile_tgt, src_feat, tile_feat, lin, amass),
                (
                    shape(each * slots * block),
                    shape(each * block),
                    shape(every, pairs, jnp.bfloat16),
                    shape(local * block, width, src_feat.dtype),
                    shape(local),
                    shape(local),
                    *[feats] * (PIECES - 1),
                ),
                scratch=[
                    SMEM((local,), jnp.int32),
                    SMEM((local, slots), jnp.int32),
                    VMEM((pairs, every), f32),
                    feats,
                    pltpu.SemaphoreType.DMA((5 + each + PIECES - 1,)),
                ],
                hbm=(0, 1, 2, 3, 4, 5),
                **cost,
            )
            kern.append(k0)
            la.append(la0)
        elif at < PIECES:
            k0, la0 = call(
                functools.partial(later_build, at * each),
                (tile_live, xv, later[at - 1], linv, massv),
                (shape(each * slots * block), shape(each * block)),
                smem=1,
                **cost,
            )
            kern.append(k0)
            la.append(la0)
        if d > 1:
            part = jnp.stack([part, got], axis=0).reshape(-1, block)
            if at < PIECES - 1:
                part, later[at], kern[-1] = lax.optimization_barrier(
                    (part, later[at], kern[-1])
                )
    acc = VMEM((local * block, block), f32)
    col = VMEM((pairs, block), f32)
    w = VMEM((every + 8, block), f32)
    mine, b_all, et_all, tot = call(
        functools.partial(first_sweep, PIECES),
        (tile_live, tile_tgt, hit, *kern, *la, part, got),
        (shape(every), shape(every), shape(every), shape(8)),
        scratch=[w, acc, acc, col],
        smem=2,
    )
    u = None
    for iteration in range(ITERS):
        mine = mine + exchange(mine, n, 1)
        d = 2
        while d < n:
            mine = mine + exchange(mine, n, d, (1,))
            d *= 2
        other = exchange(mine, n, 1)
        if iteration < ITERS - 1:
            mine, u = call(
                functools.partial(next_sweep, PIECES),
                (tile_live, tile_tgt, hit, mine, other, b_all, et_all, tot, *kern, *la),
                (shape(every), shape(local * block)),
                scratch=[w, acc, col],
                smem=2,
            )
    src, tgt = call(
        last_kernel,
        (mine, other, b_all, et_all, tot, u),
        [jax.ShapeDtypeStruct((local, block), f32)] * 2,
        scratch=[VMEM((every, block), f32)],
    )
    return (src.reshape(-1), tgt.reshape(-1))


def solution(mesh):
    split = P(("pairs", "src"))
    rows = P(("pairs", "src"), None)
    in_specs = (rows, P(("pairs", "src"), None, None, None), rows) + (split,) * 6
    return jax.shard_map(
        shards, mesh=mesh, in_specs=in_specs, out_specs=(split, split), check_vma=False
    )
```

```python
import functools

import jax
import jax.numpy as jnp
from jax import lax
from jax.experimental import pallas as pl
from jax.experimental.pallas import tpu as pltpu
from jax.sharding import PartitionSpec as P

ITERS = 3
EPS = 0.1
RHO = 1.0
ALPHA = 0.5
F = RHO / (RHO + EPS)
STEP = 4
PIECES = 4

VMEM = pltpu.VMEM
SMEM = pltpu.SMEM
NT = (((1,), (1,)), ((), ()))


def diag_mask(block):
    return lax.broadcasted_iota(jnp.int32, (block, block), 0) == lax.broadcasted_iota(
        jnp.int32, (block, block), 1
    )


def to_column(row, mask):
    return jnp.sum(jnp.where(mask, row, 0.0), axis=1, keepdims=True)


def to_row(column, mask):
    return jnp.sum(jnp.where(mask, column, 0.0), axis=0, keepdims=True)


def position():
    return lax.axis_index("src").astype(jnp.int32)


def total_of(x):
    return jnp.sum(jnp.sum(x, axis=0, keepdims=True), axis=1, keepdims=True)


def steps_of(live_s):
    return (live_s + (STEP - 1)) // STEP


def pack_kernel(count_hbm, mass_hbm, lin_hbm, amass_hbm, out_ref, count, sems):
    local, block = mass_hbm.shape
    copies = [(count_hbm, count)]
    for i, x in enumerate((mass_hbm, lin_hbm, amass_hbm)):
        copies.append((x, out_ref.at[pl.ds(i * local, local)]))
    copies = [pltpu.make_async_copy(f, t, sems.at[i]) for i, (f, t) in enumerate(copies)]
    for c in copies:
        c.start()
    for c in copies:
        c.wait()
    lane = lax.broadcasted_iota(jnp.int32, (1, block), 1)
    for i in range(local):
        row = slice(i, i + 1)
        out_ref[row, :] = jnp.where(lane < count[i], out_ref[row, :], 0.0)


def build_tiles(live, first, x_ref, lin_ref, mass_ref, feat, waits, k_ref, la_ref):
    blocks, slots, block, width = feat.shape
    mask = diag_mask(block)
    for s in range(blocks):
        at = first + s
        x = x_ref[at * block : (at + 1) * block, :]
        x32 = x.astype(jnp.float32)
        sq = jnp.sum(x32 * x32, axis=1, keepdims=True)
        lin = to_column(lin_ref[at : at + 1, :], mask)
        base = (2.0 - sq / width - ALPHA * lin) / EPS
        base = jnp.broadcast_to(base, (block, block))
        la = F * jnp.log(to_column(mass_ref[at : at + 1, :], mask))
        la_ref[s * block : (s + 1) * block, :] = jnp.broadcast_to(la, (block, block))
        if waits:
            waits[s].wait()

        def tiles(p, _):
            y = feat[s, pl.ds(p * STEP, STEP)].reshape(STEP * block, width)
            y32 = y.astype(jnp.float32)
            y2 = y32 * y32
            ysq = jnp.sum(y2[:, : width // 2] + y2[:, width // 2 :], axis=1, keepdims=True)
            cross = lax.dot_general(x, y, NT, preferred_element_type=jnp.float32)
            for q in range(STEP):
                cols = slice(q * block, (q + 1) * block)
                row = to_row(ysq[cols, :], mask)
                e = (2.0 / (width * EPS)) * cross[:, cols] + (base - row * (1.0 / (width * EPS)))
                start = pl.multiple_of((s * slots + p * STEP + q) * block, block)
                k_ref[pl.ds(start, block), :] = jnp.exp(e)
            return 0

        lax.fori_loop(0, steps_of(live[at]), tiles, 0)


def first_build(live_hbm, tgt_hbm, x_hbm, feat, lin_hbm, mass_hbm, *refs):
    k_ref, la_ref, hit_ref, x_ref, lin_ref, mass_ref, *rest = refs
    later, (live, tgt, flags, own, sems) = rest[:-5], rest[-5:]
    each = own.shape[0]
    slots = tgt.shape[1]
    copies = [(live_hbm, live), (x_hbm, x_ref), (lin_hbm, lin_ref), (mass_hbm, mass_ref)]
    copies += [(tgt_hbm, tgt)]
    copies += [(feat.at[s], own.at[s]) for s in range(each)]
    copies += [(feat.at[pl.ds((i + 1) * each, each)], to) for i, to in enumerate(later)]
    copies = [pltpu.make_async_copy(f, t, sems.at[i]) for i, (f, t) in enumerate(copies)]
    for c in copies:
        c.start()
    for c in copies[:5]:
        c.wait()
    lane = lax.broadcasted_iota(jnp.int32, (1, flags.shape[1]), 1)
    for at in range(flags.shape[0]):
        s, k = divmod(at, slots)
        row = jnp.where(k < live[s], tgt[s, k], -1)
        flags[at : at + 1, :] = jnp.where(lane == row, 1.0, 0.0)
    hit_ref[...] = jnp.transpose(flags[...]).astype(jnp.bfloat16)
    build_tiles(
        live, 0, x_ref, lin_ref, mass_ref, own, copies[5 : 5 + each], k_ref, la_ref
    )
    for c in copies[5 + each :]:
        c.wait()


def later_build(first, live, x_ref, feat, lin_ref, mass_ref, k_ref, la_ref):
    build_tiles(live, first, x_ref, lin_ref, mass_ref, feat, (), k_ref, la_ref)


def sweep(live, tgt, hit_ref, w_ref, k_refs, la_refs, dense_ref, acc_ref, u_ref, col_ref):
    blocks, slots = tgt.shape
    block = w_ref.shape[1]
    every = w_ref.shape[0] - 8
    each = blocks // len(k_refs)
    w_ref[every:, :] = jnp.zeros((8, block), jnp.float32)
    for s in range(blocks):
        k_ref = k_refs[s // each]

        def add_row(p, acc):
            for q in range(STEP):
                k = p * STEP + q
                row = jnp.where(k < live[s], tgt[s, k], every)
                start = pl.multiple_of(((s % each) * slots + k) * block, block)
                acc = acc + k_ref[pl.ds(start, block), :] * w_ref[pl.ds(row, 1), :]
            return acc

        acc_ref[s * block : (s + 1) * block, :] = lax.fori_loop(
            0, steps_of(live[s]), add_row, jnp.zeros((block, block), jnp.float32)
        )
    for s in range(blocks):
        rows = pl.ds(s * block, block)
        total = jnp.sum(acc_ref[rows, :], axis=1, keepdims=True)
        la = la_refs[s // each][pl.ds((s % each) * block, block), :]
        u_ref[rows, :] = jnp.exp(la - F * jnp.log(total))
    col_ref[...] = jnp.zeros_like(col_ref)
    for s in range(blocks):
        k_ref = k_refs[s // each]
        u = u_ref[s * block : (s + 1) * block, :]

        def add_col(p, _):
            for q in range(STEP):
                k = p * STEP + q
                start = pl.multiple_of(((s % each) * slots + k) * block, block)
                col_ref[pl.ds(s * slots + k, 1), :] = jnp.sum(
                    k_ref[pl.ds(start, block), :] * u, axis=0, keepdims=True
                )
            return 0

        lax.fori_loop(0, steps_of(live[s]), add_col, 0)
    col = col_ref[...]
    hit = hit_ref[...]
    dense = jnp.zeros((every, block), jnp.float32)
    for _ in range(3):
        piece = col.astype(jnp.bfloat16)
        dense += jnp.dot(hit, piece, preferred_element_type=jnp.float32)
        col = col - piece.astype(jnp.float32)
    dense_ref[...] = dense


def power_of_ratio(num, den):
    return jnp.exp(F * (jnp.log(num) - jnp.log(den)))


def first_sweep(npieces, live, tgt, hit_ref, *refs):
    k_refs, la_refs = refs[:npieces], refs[npieces : 2 * npieces]
    parts = refs[2 * npieces : 2 * npieces + 2]
    dense_ref, b_ref, et_ref, tot_ref, w_ref, acc_ref, u_ref, col_ref = refs[2 * npieces + 2 :]
    local = tgt.shape[0]
    n = b_ref.shape[0] // local
    bits = n.bit_length() - 1
    am = jnp.zeros((local, b_ref.shape[1]), jnp.float32)
    for at in range(n):
        m = sum(((at >> r) & 1) << (bits - 1 - r) for r in range(bits))
        part = parts[at // (n // 2)]
        at = (at % (n // 2)) * 3 * local
        rows = pl.ds(pl.multiple_of((position() ^ m) * local, local), local)
        b = part[at : at + local, :]
        et = jnp.exp((-ALPHA / EPS) * part[at + local : at + 2 * local, :])
        b_ref[rows, :] = b
        et_ref[rows, :] = et
        w_ref[rows, :] = jnp.where(b > 0.0, et, 0.0)
        am += part[at + 2 * local : at + 3 * local, :]
    tot = jnp.sqrt(total_of(am) * total_of(b_ref[...]))
    tot_ref[...] = jnp.broadcast_to(tot, tot_ref.shape)
    sweep(live, tgt, hit_ref, w_ref, k_refs, la_refs, dense_ref, acc_ref, u_ref, col_ref)


def new_scale(mine, b_ref, et_ref, tot_ref):
    b = b_ref[...]
    col = mine[...] * et_ref[...]
    t = jnp.where(b > 0.0, power_of_ratio(b, col), 0.0)
    return t, jnp.sqrt(tot_ref[0:1, 0:1] / total_of(t * col))


def next_sweep(npieces, live, tgt, hit_ref, mine, b_ref, et_ref, tot_ref, *refs):
    k_refs, la_refs = refs[:npieces], refs[npieces : 2 * npieces]
    dense_ref, u_ref, w_ref, acc_ref, col_ref = refs[2 * npieces :]
    t, factor = new_scale(mine, b_ref, et_ref, tot_ref)
    w_ref[: b_ref.shape[0], :] = t * (factor * et_ref[...])
    sweep(live, tgt, hit_ref, w_ref, k_refs, la_refs, dense_ref, acc_ref, u_ref, col_ref)


def last_kernel(mine, b_ref, et_ref, tot_ref, u_ref, src_ref, tgt_ref, t_ref):
    local, block = src_ref.shape
    t, factor = new_scale(mine, b_ref, et_ref, tot_ref)
    t_ref[...] = t * factor
    tgt_ref[...] = t_ref[pl.ds(pl.multiple_of(position() * local, local), local), :]
    mask = diag_mask(block)
    for s in range(local):
        src_ref[s : s + 1, :] = to_row(u_ref[s * block : (s + 1) * block, :] * factor, mask)


def call(kernel, ins, outs, scratch=(), smem=0, hbm=(), vmem_mb=12, **cost):
    specs = [pl.BlockSpec(memory_space=SMEM)] * smem
    for at in range(smem, len(ins)):
        specs.append(pl.BlockSpec(memory_space=pl.ANY if at in hbm else VMEM))
    ins = [
        pltpu.with_memory_space_constraint(x, pltpu.HBM) if at in hbm else x
        for at, x in enumerate(ins)
    ]
    return pl.pallas_call(
        kernel,
        out_shape=outs,
        in_specs=specs,
        out_specs=[pl.BlockSpec(memory_space=VMEM)] * len(outs),
        scratch_shapes=scratch,
        compiler_params=pltpu.CompilerParams(vmem_limit_bytes=vmem_mb << 20),
        cost_estimate=pl.CostEstimate(**cost) if cost else None,
    )(*ins)


def exchange(x, n, d):
    return lax.ppermute(x, "src", [(i, i ^ d) for i in range(n)])


def shards(
    src_feat, tile_feat, tile_tgt, tile_live, src_lin, tgt_lin, src_mass, tgt_mass, tgt_count
):
    f32 = jnp.float32
    local, slots, block, width = tile_feat.shape
    n = lax.axis_size("src")
    every = local * n
    pairs = local * slots
    lin = src_lin.reshape(local, block)
    amass = src_mass.reshape(local, block)
    def shape(rows, cols=block, dtype=f32):
        return pltpu.VMEM((rows, cols), dtype)

    (part,) = call(
        pack_kernel,
        (tgt_count, tgt_mass.reshape(local, block), tgt_lin.reshape(local, block), amass),
        (shape(3 * local),),
        scratch=[SMEM((local,), jnp.int32), pltpu.SemaphoreType.DMA((4,))],
        hbm=(0, 1, 2, 3),
    )
    each = local // PIECES
    feats = pltpu.VMEM((each, slots, block, width), tile_feat.dtype)
    cost = dict(
        flops=2 * each * slots * block * block * width,
        bytes_accessed=2 * each * slots * block * width,
        transcendentals=each * slots * block * block,
    )
    order = []
    d = n // 2
    while d:
        order.append(d)
        d //= 2
    kern, la = [], []
    for at, d in enumerate(order):
        got = exchange(part, n, d)
        if at == 0:
            k0, la0, hit, xv, linv, massv, *later = call(
                first_build,
                (tile_live, tile_tgt, src_feat, tile_feat, lin, amass),
                (
                    shape(each * slots * block),
                    shape(each * block),
                    shape(every, pairs, jnp.bfloat16),
                    shape(local * block, width, src_feat.dtype),
                    shape(local),
                    shape(local),
                    *[feats] * (PIECES - 1),
                ),
                scratch=[
                    SMEM((local,), jnp.int32),
                    SMEM((local, slots), jnp.int32),
                    VMEM((pairs, every), f32),
                    feats,
                    pltpu.SemaphoreType.DMA((5 + each + PIECES - 1,)),
                ],
                hbm=(0, 1, 2, 3, 4, 5),
                **cost,
            )
            kern.append(k0)
            la.append(la0)
        elif at < PIECES:
            k0, la0 = call(
                functools.partial(later_build, at * each),
                (tile_live, xv, later[at - 1], linv, massv),
                (shape(each * slots * block), shape(each * block)),
                smem=1,
                **cost,
            )
            kern.append(k0)
            la.append(la0)
        if d > 1:
            part = jnp.stack([part, got], axis=0).reshape(-1, block)
            if at < PIECES - 1:
                part, later[at], kern[-1] = lax.optimization_barrier(
                    (part, later[at], kern[-1])
                )
    acc = VMEM((local * block, block), f32)
    col = VMEM((pairs, block), f32)
    w = VMEM((every + 8, block), f32)
    mine, b_all, et_all, tot = call(
        functools.partial(first_sweep, PIECES),
        (tile_live, tile_tgt, hit, *kern, *la, part, got),
        (shape(every), shape(every), shape(every), shape(8)),
        scratch=[w, acc, acc, col],
        smem=2,
    )
    u = None
    for iteration in range(ITERS):
        parts = lax.all_to_all(mine.reshape(n, local, block), "src", 0, 0)
        own = jnp.broadcast_to(jnp.sum(parts, axis=0), (n, local, block))
        mine = lax.all_to_all(own, "src", 0, 0).reshape(every, block)
        if iteration < ITERS - 1:
            mine, u = call(
                functools.partial(next_sweep, PIECES),
                (tile_live, tile_tgt, hit, mine, b_all, et_all, tot, *kern, *la),
                (shape(every), shape(local * block)),
                scratch=[w, acc, col],
                smem=2,
            )
    src, tgt = call(
        last_kernel,
        (mine, b_all, et_all, tot, u),
        [jax.ShapeDtypeStruct((local, block), f32)] * 2,
        scratch=[VMEM((every, block), f32)],
    )
    return (src.reshape(-1), tgt.reshape(-1))


def solution(mesh):
    split = P(("pairs", "src"))
    rows = P(("pairs", "src"), None)
    in_specs = (rows, P(("pairs", "src"), None, None, None), rows) + (split,) * 6
    return jax.shard_map(
        shards, mesh=mesh, in_specs=in_specs, out_specs=(split, split), check_vma=False
    )
```

```python
import functools

import jax
import jax.numpy as jnp
from jax import lax
from jax.experimental import pallas as pl
from jax.experimental.pallas import tpu as pltpu
from jax.sharding import PartitionSpec as P

ITERS = 3
EPS = 0.1
RHO = 1.0
ALPHA = 0.5
F = RHO / (RHO + EPS)
STEP = 4
PIECES = 4

VMEM = pltpu.VMEM
SMEM = pltpu.SMEM
NT = (((1,), (1,)), ((), ()))


def diag_mask(block):
    return lax.broadcasted_iota(jnp.int32, (block, block), 0) == lax.broadcasted_iota(
        jnp.int32, (block, block), 1
    )


def to_column(row, mask):
    return jnp.sum(jnp.where(mask, row, 0.0), axis=1, keepdims=True)


def to_row(column, mask):
    return jnp.sum(jnp.where(mask, column, 0.0), axis=0, keepdims=True)


def position():
    return lax.axis_index("src").astype(jnp.int32)


def total_of(x):
    return jnp.sum(jnp.sum(x, axis=0, keepdims=True), axis=1, keepdims=True)


def steps_of(live_s):
    return (live_s + (STEP - 1)) // STEP


def pack_kernel(count_hbm, mass_hbm, lin_hbm, amass_hbm, out_ref, count, sems):
    local, block = mass_hbm.shape
    copies = [(count_hbm, count)]
    for i, x in enumerate((mass_hbm, lin_hbm, amass_hbm)):
        copies.append((x, out_ref.at[pl.ds(i * local, local)]))
    copies = [pltpu.make_async_copy(f, t, sems.at[i]) for i, (f, t) in enumerate(copies)]
    for c in copies:
        c.start()
    for c in copies:
        c.wait()
    lane = lax.broadcasted_iota(jnp.int32, (1, block), 1)
    for i in range(local):
        row = slice(i, i + 1)
        out_ref[row, :] = jnp.where(lane < count[i], out_ref[row, :], 0.0)


def build_tiles(live, first, x_ref, lin_ref, mass_ref, feat, waits, k_ref, la_ref):
    blocks, slots, block, width = feat.shape
    mask = diag_mask(block)
    for s in range(blocks):
        at = first + s
        x = x_ref[at * block : (at + 1) * block, :]
        x32 = x.astype(jnp.float32)
        sq = jnp.sum(x32 * x32, axis=1, keepdims=True)
        lin = to_column(lin_ref[at : at + 1, :], mask)
        base = (2.0 - sq / width - ALPHA * lin) / EPS
        base = jnp.broadcast_to(base, (block, block))
        la = F * jnp.log(to_column(mass_ref[at : at + 1, :], mask))
        la_ref[s * block : (s + 1) * block, :] = jnp.broadcast_to(la, (block, block))
        if waits:
            waits[s].wait()

        def tiles(p, _):
            y = feat[s, pl.ds(p * STEP, STEP)].reshape(STEP * block, width)
            y32 = y.astype(jnp.float32)
            y2 = y32 * y32
            ysq = jnp.sum(y2[:, : width // 2] + y2[:, width // 2 :], axis=1, keepdims=True)
            cross = lax.dot_general(x, y, NT, preferred_element_type=jnp.float32)
            for q in range(STEP):
                cols = slice(q * block, (q + 1) * block)
                row = to_row(ysq[cols, :], mask)
                e = (2.0 / (width * EPS)) * cross[:, cols] + (base - row * (1.0 / (width * EPS)))
                start = pl.multiple_of((s * slots + p * STEP + q) * block, block)
                k_ref[pl.ds(start, block), :] = jnp.exp(e)
            return 0

        lax.fori_loop(0, steps_of(live[at]), tiles, 0)


def first_build(live_hbm, tgt_hbm, x_hbm, feat, lin_hbm, mass_hbm, *refs):
    k_ref, la_ref, hit_ref, x_ref, lin_ref, mass_ref, *rest = refs
    later, (live, tgt, flags, own, sems) = rest[:-5], rest[-5:]
    each = own.shape[0]
    slots = tgt.shape[1]
    copies = [(live_hbm, live), (x_hbm, x_ref), (lin_hbm, lin_ref), (mass_hbm, mass_ref)]
    copies += [(tgt_hbm, tgt)]
    copies += [(feat.at[s], own.at[s]) for s in range(each)]
    copies += [(feat.at[pl.ds((i + 1) * each, each)], to) for i, to in enumerate(later)]
    copies = [pltpu.make_async_copy(f, t, sems.at[i]) for i, (f, t) in enumerate(copies)]
    for c in copies:
        c.start()
    for c in copies[:5]:
        c.wait()
    lane = lax.broadcasted_iota(jnp.int32, (1, flags.shape[1]), 1)
    for at in range(flags.shape[0]):
        s, k = divmod(at, slots)
        row = jnp.where(k < live[s], tgt[s, k], -1)
        flags[at : at + 1, :] = jnp.where(lane == row, 1.0, 0.0)
    hit_ref[...] = jnp.transpose(flags[...]).astype(jnp.bfloat16)
    build_tiles(
        live, 0, x_ref, lin_ref, mass_ref, own, copies[5 : 5 + each], k_ref, la_ref
    )
    for c in copies[5 + each :]:
        c.wait()


def later_build(first, live, x_ref, feat, lin_ref, mass_ref, k_ref, la_ref):
    build_tiles(live, first, x_ref, lin_ref, mass_ref, feat, (), k_ref, la_ref)


def sweep(live, tgt, hit_ref, w_ref, k_refs, la_refs, dense_ref, acc_ref, u_ref, col_ref):
    blocks, slots = tgt.shape
    block = w_ref.shape[1]
    every = w_ref.shape[0] - 8
    each = blocks // len(k_refs)
    w_ref[every:, :] = jnp.zeros((8, block), jnp.float32)
    for s in range(blocks):
        k_ref = k_refs[s // each]

        def add_row(p, acc):
            for q in range(STEP):
                k = p * STEP + q
                row = jnp.where(k < live[s], tgt[s, k], every)
                start = pl.multiple_of(((s % each) * slots + k) * block, block)
                acc = acc + k_ref[pl.ds(start, block), :] * w_ref[pl.ds(row, 1), :]
            return acc

        acc_ref[s * block : (s + 1) * block, :] = lax.fori_loop(
            0, steps_of(live[s]), add_row, jnp.zeros((block, block), jnp.float32)
        )
    for s in range(blocks):
        rows = pl.ds(s * block, block)
        total = jnp.sum(acc_ref[rows, :], axis=1, keepdims=True)
        la = la_refs[s // each][pl.ds((s % each) * block, block), :]
        u_ref[rows, :] = jnp.exp(la - F * jnp.log(total))
    col_ref[...] = jnp.zeros_like(col_ref)
    for s in range(blocks):
        k_ref = k_refs[s // each]
        u = u_ref[s * block : (s + 1) * block, :]

        def add_col(p, _):
            for q in range(STEP):
                k = p * STEP + q
                start = pl.multiple_of(((s % each) * slots + k) * block, block)
                col_ref[pl.ds(s * slots + k, 1), :] = jnp.sum(
                    k_ref[pl.ds(start, block), :] * u, axis=0, keepdims=True
                )
            return 0

        lax.fori_loop(0, steps_of(live[s]), add_col, 0)
    col = col_ref[...]
    hit = hit_ref[...]
    dense = jnp.zeros((every, block), jnp.float32)
    for _ in range(3):
        piece = col.astype(jnp.bfloat16)
        dense += jnp.dot(hit, piece, preferred_element_type=jnp.float32)
        col = col - piece.astype(jnp.float32)
    dense_ref[...] = dense


def power_of_ratio(num, den):
    return jnp.exp(F * (jnp.log(num) - jnp.log(den)))


def first_sweep(npieces, live, tgt, hit_ref, *refs):
    k_refs, la_refs = refs[:npieces], refs[npieces : 2 * npieces]
    parts = refs[2 * npieces : 2 * npieces + 2]
    dense_ref, b_ref, et_ref, tot_ref, w_ref, acc_ref, u_ref, col_ref = refs[2 * npieces + 2 :]
    local = tgt.shape[0]
    n = b_ref.shape[0] // local
    am = jnp.zeros((local, b_ref.shape[1]), jnp.float32)
    order = distances(n)
    for at in range(n):
        m = functools.reduce(lambda p, q: p ^ q, [d for r, d in enumerate(order) if at >> r & 1], 0)
        part = parts[at // (n // 2)]
        at = (at % (n // 2)) * 3 * local
        rows = pl.ds(pl.multiple_of((position() ^ m) * local, local), local)
        b = part[at : at + local, :]
        et = jnp.exp((-ALPHA / EPS) * part[at + local : at + 2 * local, :])
        b_ref[rows, :] = b
        et_ref[rows, :] = et
        w_ref[rows, :] = jnp.where(b > 0.0, et, 0.0)
        am += part[at + 2 * local : at + 3 * local, :]
    tot = jnp.sqrt(total_of(am) * total_of(b_ref[...]))
    tot_ref[...] = jnp.broadcast_to(tot, tot_ref.shape)
    sweep(live, tgt, hit_ref, w_ref, k_refs, la_refs, dense_ref, acc_ref, u_ref, col_ref)


def new_scale(mine, other, b_ref, et_ref, tot_ref):
    b = b_ref[...]
    col = (mine[...] + other[...]) * et_ref[...]
    t = jnp.where(b > 0.0, power_of_ratio(b, col), 0.0)
    return t, jnp.sqrt(tot_ref[0:1, 0:1] / total_of(t * col))


def next_sweep(npieces, live, tgt, hit_ref, mine, other, b_ref, et_ref, tot_ref, *refs):
    k_refs, la_refs = refs[:npieces], refs[npieces : 2 * npieces]
    dense_ref, u_ref, w_ref, acc_ref, col_ref = refs[2 * npieces :]
    t, factor = new_scale(mine, other, b_ref, et_ref, tot_ref)
    w_ref[: b_ref.shape[0], :] = t * (factor * et_ref[...])
    sweep(live, tgt, hit_ref, w_ref, k_refs, la_refs, dense_ref, acc_ref, u_ref, col_ref)


def last_kernel(mine, other, b_ref, et_ref, tot_ref, u_ref, src_ref, tgt_ref, t_ref):
    local, block = src_ref.shape
    t, factor = new_scale(mine, other, b_ref, et_ref, tot_ref)
    t_ref[...] = t * factor
    tgt_ref[...] = t_ref[pl.ds(pl.multiple_of(position() * local, local), local), :]
    mask = diag_mask(block)
    for s in range(local):
        src_ref[s : s + 1, :] = to_row(u_ref[s * block : (s + 1) * block, :] * factor, mask)


def call(kernel, ins, outs, scratch=(), smem=0, hbm=(), vmem_mb=12, **cost):
    specs = [pl.BlockSpec(memory_space=SMEM)] * smem
    for at in range(smem, len(ins)):
        specs.append(pl.BlockSpec(memory_space=pl.ANY if at in hbm else VMEM))
    ins = [
        pltpu.with_memory_space_constraint(x, pltpu.HBM) if at in hbm else x
        for at, x in enumerate(ins)
    ]
    return pl.pallas_call(
        kernel,
        out_shape=outs,
        in_specs=specs,
        out_specs=[pl.BlockSpec(memory_space=VMEM)] * len(outs),
        scratch_shapes=scratch,
        compiler_params=pltpu.CompilerParams(vmem_limit_bytes=vmem_mb << 20),
        cost_estimate=pl.CostEstimate(**cost) if cost else None,
    )(*ins)


def distances(n):
    return [d | 1 for d in (n >> r for r in range(1, n.bit_length()))]


def exchange(x, n, d):
    return lax.ppermute(x, "src", [(i, i ^ d) for i in range(n)])


def shards(
    src_feat, tile_feat, tile_tgt, tile_live, src_lin, tgt_lin, src_mass, tgt_mass, tgt_count
):
    f32 = jnp.float32
    local, slots, block, width = tile_feat.shape
    n = lax.axis_size("src")
    every = local * n
    pairs = local * slots
    lin = src_lin.reshape(local, block)
    amass = src_mass.reshape(local, block)
    def shape(rows, cols=block, dtype=f32):
        return pltpu.VMEM((rows, cols), dtype)

    (part,) = call(
        pack_kernel,
        (tgt_count, tgt_mass.reshape(local, block), tgt_lin.reshape(local, block), amass),
        (shape(3 * local),),
        scratch=[SMEM((local,), jnp.int32), pltpu.SemaphoreType.DMA((4,))],
        hbm=(0, 1, 2, 3),
    )
    each = local // PIECES
    feats = pltpu.VMEM((each, slots, block, width), tile_feat.dtype)
    cost = dict(
        flops=2 * each * slots * block * block * width,
        bytes_accessed=2 * each * slots * block * width,
        transcendentals=each * slots * block * block,
    )
    order = distances(n)
    kern, la = [], []
    for at, d in enumerate(order):
        got = exchange(part, n, d)
        if at == 0:
            k0, la0, hit, xv, linv, massv, *later = call(
                first_build,
                (tile_live, tile_tgt, src_feat, tile_feat, lin, amass),
                (
                    shape(each * slots * block),
                    shape(each * block),
                    shape(every, pairs, jnp.bfloat16),
                    shape(local * block, width, src_feat.dtype),
                    shape(local),
                    shape(local),
                    *[feats] * (PIECES - 1),
                ),
                scratch=[
                    SMEM((local,), jnp.int32),
                    SMEM((local, slots), jnp.int32),
                    VMEM((pairs, every), f32),
                    feats,
                    pltpu.SemaphoreType.DMA((5 + each + PIECES - 1,)),
                ],
                hbm=(0, 1, 2, 3, 4, 5),
                **cost,
            )
            kern.append(k0)
            la.append(la0)
        elif at < PIECES:
            k0, la0 = call(
                functools.partial(later_build, at * each),
                (tile_live, xv, later[at - 1], linv, massv),
                (shape(each * slots * block), shape(each * block)),
                smem=1,
                **cost,
            )
            kern.append(k0)
            la.append(la0)
        if at < len(order) - 1:
            part = jnp.stack([part, got], axis=0).reshape(-1, block)
            if at < PIECES - 1:
                part, later[at], kern[-1] = lax.optimization_barrier(
                    (part, later[at], kern[-1])
                )
    acc = VMEM((local * block, block), f32)
    col = VMEM((pairs, block), f32)
    w = VMEM((every + 8, block), f32)
    mine, b_all, et_all, tot = call(
        functools.partial(first_sweep, PIECES),
        (tile_live, tile_tgt, hit, *kern, *la, part, got),
        (shape(every), shape(every), shape(every), shape(8)),
        scratch=[w, acc, acc, col],
        smem=2,
    )
    u = None
    for iteration in range(ITERS):
        for d in order[::-1][:-1]:
            mine = mine + exchange(mine, n, d)
        other = exchange(mine, n, order[0])
        if iteration < ITERS - 1:
            last = iteration == ITERS - 2
            outs = (shape(every), shape(local * block)) if last else (shape(every),)
            mine, *u = call(
                functools.partial(next_sweep, PIECES),
                (tile_live, tile_tgt, hit, mine, other, b_all, et_all, tot, *kern, *la),
                outs,
                scratch=[w, acc, col] if last else [acc, w, acc, col],
                smem=2,
            )
    src, tgt = call(
        last_kernel,
        (mine, other, b_all, et_all, tot, *u),
        [jax.ShapeDtypeStruct((local, block), f32)] * 2,
        scratch=[VMEM((every, block), f32)],
    )
    return (src.reshape(-1), tgt.reshape(-1))


def solution(mesh):
    split = P(("pairs", "src"))
    rows = P(("pairs", "src"), None)
    in_specs = (rows, P(("pairs", "src"), None, None, None), rows) + (split,) * 6
    return jax.shard_map(
        shards, mesh=mesh, in_specs=in_specs, out_specs=(split, split), check_vma=False
    )
```

```python
import functools

import jax
import jax.numpy as jnp
from jax import lax
from jax.experimental import pallas as pl
from jax.experimental.pallas import tpu as pltpu
from jax.sharding import PartitionSpec as P

ITERS = 3
EPS = 0.1
RHO = 1.0
ALPHA = 0.5
F = RHO / (RHO + EPS)
STEP = 4
ABSENT = -1e30
PIECES = 4

VMEM = pltpu.VMEM
SMEM = pltpu.SMEM
NT = (((1,), (1,)), ((), ()))


def diag_mask(block):
    return lax.broadcasted_iota(jnp.int32, (block, block), 0) == lax.broadcasted_iota(
        jnp.int32, (block, block), 1
    )


def to_column(row, mask):
    return jnp.sum(jnp.where(mask, row, 0.0), axis=1, keepdims=True)


def to_row(column, mask):
    return jnp.sum(jnp.where(mask, column, 0.0), axis=0, keepdims=True)


def position():
    return lax.axis_index("src").astype(jnp.int32)


def half_flip(every):
    at = position()
    for r in (16, 8, 4, 2, 1):
        at = at ^ (at >> r)
    return (at & 1) * (every // 2)


def total_of(x):
    return jnp.sum(jnp.sum(x, axis=0, keepdims=True), axis=1, keepdims=True)


def steps_of(live_s):
    return (live_s + (STEP - 1)) // STEP


def pack_kernel(count_hbm, mass_hbm, lin_hbm, amass_hbm, out_ref, count, sems):
    local, block = mass_hbm.shape
    copies = [(count_hbm, count)]
    for i, x in enumerate((mass_hbm, lin_hbm, amass_hbm)):
        copies.append((x, out_ref.at[pl.ds(i * local, local)]))
    copies = [pltpu.make_async_copy(f, t, sems.at[i]) for i, (f, t) in enumerate(copies)]
    for c in copies:
        c.start()
    for c in copies:
        c.wait()
    lane = lax.broadcasted_iota(jnp.int32, (1, block), 1)
    for i in range(local):
        row = slice(i, i + 1)
        out_ref[row, :] = jnp.where(lane < count[i], out_ref[row, :], 0.0)


def build_tiles(steps, first, x_ref, lin_ref, mass_ref, feat, waits, k_ref, la_ref):
    blocks, slots, block, width = feat.shape
    mask = diag_mask(block)
    for s in range(blocks):
        at = first + s
        x = x_ref[at * block : (at + 1) * block, :]
        x32 = x.astype(jnp.float32)
        sq = jnp.sum(x32 * x32, axis=1, keepdims=True)
        lin = to_column(lin_ref[at : at + 1, :], mask)
        base = (2.0 - sq / width - ALPHA * lin) / EPS
        base = jnp.broadcast_to(base, (block, block))
        la = F * jnp.log(to_column(mass_ref[at : at + 1, :], mask))
        la_ref[s * block : (s + 1) * block, :] = jnp.broadcast_to(la, (block, block))
        if waits:
            waits[s].wait()

        def tiles(p, _):
            y = feat[s, pl.ds(p * STEP, STEP)].reshape(STEP * block, width)
            y32 = y.astype(jnp.float32)
            y2 = y32 * y32
            ysq = jnp.sum(y2[:, : width // 2] + y2[:, width // 2 :], axis=1, keepdims=True)
            cross = lax.dot_general(x, y, NT, preferred_element_type=jnp.float32)
            for q in range(STEP):
                cols = slice(q * block, (q + 1) * block)
                row = to_row(ysq[cols, :], mask)
                e = (2.0 / (width * EPS)) * cross[:, cols] + (base - row * (1.0 / (width * EPS)))
                start = pl.multiple_of((s * slots + p * STEP + q) * block, block)
                k_ref[pl.ds(start, block), :] = jnp.exp(e)
            return 0

        lax.fori_loop(0, steps(at), tiles, 0)


def first_build(live_hbm, tgt_hbm, x_hbm, feat, lin_hbm, mass_hbm, *refs):
    k_ref, la_ref, plan_ref, hit_ref, x_ref, lin_ref, mass_ref, *rest = refs
    later, (live, tgt, flags, own, sems) = rest[:-5], rest[-5:]
    each = own.shape[0]
    slots = tgt.shape[1]
    copies = [(live_hbm, live), (x_hbm, x_ref), (lin_hbm, lin_ref), (mass_hbm, mass_ref)]
    copies += [(tgt_hbm, tgt)]
    copies += [(feat.at[s], own.at[s]) for s in range(each)]
    copies += [(feat.at[pl.ds((i + 1) * each, each)], to) for i, to in enumerate(later)]
    copies = [pltpu.make_async_copy(f, t, sems.at[i]) for i, (f, t) in enumerate(copies)]
    for c in copies:
        c.start()
    for c in copies[:5]:
        c.wait()
    every = flags.shape[1]
    flip = half_flip(every)
    lane = lax.broadcasted_iota(jnp.int32, (1, every), 1)
    for at in range(flags.shape[0]):
        s, k = divmod(at, slots)
        row = jnp.where(k < live[s], tgt[s, k] ^ flip, every)
        plan_ref[s, k] = row
        flags[at : at + 1, :] = jnp.where(lane == row, 1.0, 0.0)
    for s in range(tgt.shape[0]):
        plan_ref[tgt.shape[0], s] = steps_of(live[s])
    hit_ref[...] = jnp.transpose(flags[...]).astype(jnp.bfloat16)
    build_tiles(
        lambda s: steps_of(live[s]), 0, x_ref, lin_ref, mass_ref, own, copies[5 : 5 + each], k_ref, la_ref
    )
    for c in copies[5 + each :]:
        c.wait()


def later_build(first, plan, x_ref, feat, lin_ref, mass_ref, k_ref, la_ref):
    build_tiles(lambda s: plan[plan.shape[0] - 1, s], first, x_ref, lin_ref, mass_ref, feat, (), k_ref, la_ref)


def sweep(plan, hit_ref, w_ref, k_refs, la_refs, keep_ref, send_ref, acc_ref, u_ref, col_ref):
    blocks, slots = plan.shape[0] - 1, plan.shape[1]
    block = w_ref.shape[1]
    every = w_ref.shape[0] - 8
    each = blocks // len(k_refs)
    w_ref[every:, :] = jnp.zeros((8, block), jnp.float32)
    for s in range(blocks):
        k_ref = k_refs[s // each]

        def add_row(p, acc):
            for q in range(STEP):
                k = p * STEP + q
                row = plan[s, k]
                start = pl.multiple_of(((s % each) * slots + k) * block, block)
                acc = acc + k_ref[pl.ds(start, block), :] * w_ref[pl.ds(row, 1), :]
            return acc

        acc_ref[s * block : (s + 1) * block, :] = lax.fori_loop(
            0, plan[blocks, s], add_row, jnp.zeros((block, block), jnp.float32)
        )
    for s in range(blocks):
        rows = pl.ds(s * block, block)
        total = jnp.sum(acc_ref[rows, :], axis=1, keepdims=True)
        la = la_refs[s // each][pl.ds((s % each) * block, block), :]
        u_ref[rows, :] = jnp.exp(la - F * jnp.log(total))
    col_ref[...] = jnp.zeros_like(col_ref)
    for s in range(blocks):
        k_ref = k_refs[s // each]
        u = u_ref[s * block : (s + 1) * block, :]

        def add_col(p, _):
            for q in range(STEP):
                k = p * STEP + q
                start = pl.multiple_of(((s % each) * slots + k) * block, block)
                col_ref[pl.ds(s * slots + k, 1), :] = jnp.sum(
                    k_ref[pl.ds(start, block), :] * u, axis=0, keepdims=True
                )
            return 0

        lax.fori_loop(0, plan[blocks, s], add_col, 0)
    col = col_ref[...]
    hit = hit_ref[...]
    dense = jnp.zeros((every, block), jnp.float32)
    for _ in range(3):
        piece = col.astype(jnp.bfloat16)
        dense += jnp.dot(hit, piece, preferred_element_type=jnp.float32)
        col = col - piece.astype(jnp.float32)
    keep_ref[...] = dense[: every // 2, :]
    send_ref[...] = dense[every // 2 :, :]


def first_sweep(npieces, plan, hit_ref, *refs):
    k_refs, la_refs = refs[:npieces], refs[npieces : 2 * npieces]
    parts = refs[2 * npieces : 2 * npieces + 2]
    keep_ref, send_ref, fb_ref, et_ref, tot_ref, w_ref, acc_ref, u_ref, col_ref = refs[
        2 * npieces + 2 :
    ]
    local = plan.shape[0] - 1
    flip = half_flip(fb_ref.shape[0])
    n = fb_ref.shape[0] // local
    am = jnp.zeros((local, fb_ref.shape[1]), jnp.float32)
    bm = am
    order = distances(n)
    for at in range(n):
        m = functools.reduce(lambda p, q: p ^ q, [d for r, d in enumerate(order) if at >> r & 1], 0)
        part = parts[at // (n // 2)]
        at = (at % (n // 2)) * 3 * local
        rows = pl.ds(pl.multiple_of(((position() ^ m) * local) ^ flip, local), local)
        b = part[at : at + local, :]
        et = jnp.exp((-ALPHA / EPS) * part[at + local : at + 2 * local, :])
        fb_ref[rows, :] = jnp.where(b > 0.0, F * jnp.log(b), ABSENT)
        et_ref[rows, :] = et
        w_ref[rows, :] = jnp.where(b > 0.0, et, 0.0)
        bm += b
        am += part[at + 2 * local : at + 3 * local, :]
    tot = jnp.sqrt(total_of(am) * total_of(bm))
    tot_ref[...] = jnp.broadcast_to(tot, tot_ref.shape)
    sweep(plan, hit_ref, w_ref, k_refs, la_refs, keep_ref, send_ref, acc_ref, u_ref, col_ref)


def new_scale(keep, other, fb_ref, et_ref, tot_ref, t_ref):
    half = keep.shape[0]
    mass = jnp.zeros((1, keep.shape[1]), jnp.float32)
    for at, sums in ((0, keep), (half, other)):
        rows = slice(at, at + half)
        fb = fb_ref[rows, :]
        col = sums[...] * et_ref[rows, :]
        t = jnp.where(fb > ABSENT, jnp.exp(fb - F * jnp.log(col)), 0.0)
        t_ref[rows, :] = t
        mass += jnp.sum(t * col, axis=0, keepdims=True)
    return jnp.sqrt(tot_ref[0:1, 0:1] / jnp.sum(mass, axis=1, keepdims=True))


def next_sweep(npieces, plan, hit_ref, keep, other, fb_ref, et_ref, tot_ref, *refs):
    k_refs, la_refs = refs[:npieces], refs[npieces : 2 * npieces]
    keep_ref, send_ref, u_ref, w_ref, acc_ref, col_ref = refs[2 * npieces :]
    factor = new_scale(keep, other, fb_ref, et_ref, tot_ref, w_ref)
    rows = slice(0, fb_ref.shape[0])
    w_ref[rows, :] = w_ref[rows, :] * (factor * et_ref[...])
    sweep(plan, hit_ref, w_ref, k_refs, la_refs, keep_ref, send_ref, acc_ref, u_ref, col_ref)


def last_kernel(keep, other, fb_ref, et_ref, tot_ref, u_ref, src_ref, tgt_ref, t_ref):
    local, block = src_ref.shape
    factor = new_scale(keep, other, fb_ref, et_ref, tot_ref, t_ref)
    own = (position() * local) ^ half_flip(fb_ref.shape[0])
    tgt_ref[...] = t_ref[pl.ds(pl.multiple_of(own, local), local), :] * factor
    mask = diag_mask(block)
    for s in range(local):
        src_ref[s : s + 1, :] = to_row(u_ref[s * block : (s + 1) * block, :] * factor, mask)


def call(kernel, ins, outs, scratch=(), smem=0, hbm=(), vmem_mb=12, **cost):
    specs = [pl.BlockSpec(memory_space=SMEM)] * smem
    for at in range(smem, len(ins)):
        specs.append(pl.BlockSpec(memory_space=pl.ANY if at in hbm else VMEM))
    ins = [
        pltpu.with_memory_space_constraint(x, pltpu.HBM) if at in hbm else x
        for at, x in enumerate(ins)
    ]
    return pl.pallas_call(
        kernel,
        out_shape=outs,
        in_specs=specs,
        out_specs=[
            pl.BlockSpec(memory_space=SMEM if out.dtype == jnp.int32 else VMEM) for out in outs
        ],
        scratch_shapes=scratch,
        compiler_params=pltpu.CompilerParams(vmem_limit_bytes=vmem_mb << 20),
        cost_estimate=pl.CostEstimate(**cost) if cost else None,
    )(*ins)


def distances(n):
    return [d | 1 for d in (n >> r for r in range(1, n.bit_length()))]


def exchange(x, n, d):
    return lax.ppermute(x, "src", [(i, i ^ d) for i in range(n)])


def shards(
    src_feat, tile_feat, tile_tgt, tile_live, src_lin, tgt_lin, src_mass, tgt_mass, tgt_count
):
    f32 = jnp.float32
    local, slots, block, width = tile_feat.shape
    n = lax.axis_size("src")
    every = local * n
    pairs = local * slots
    lin = src_lin.reshape(local, block)
    amass = src_mass.reshape(local, block)
    def shape(rows, cols=block, dtype=f32):
        return pltpu.VMEM((rows, cols), dtype)

    (part,) = call(
        pack_kernel,
        (tgt_count, tgt_mass.reshape(local, block), tgt_lin.reshape(local, block), amass),
        (shape(3 * local),),
        scratch=[SMEM((local,), jnp.int32), pltpu.SemaphoreType.DMA((4,))],
        hbm=(0, 1, 2, 3),
    )
    each = local // PIECES
    feats = pltpu.VMEM((each, slots, block, width), tile_feat.dtype)
    cost = dict(
        flops=2 * each * slots * block * block * width,
        bytes_accessed=2 * each * slots * block * width,
        transcendentals=each * slots * block * block,
    )
    order = distances(n)
    kern, la = [], []
    for at, d in enumerate(order):
        got = exchange(part, n, d)
        if at == 0:
            k0, la0, plan, hit, xv, linv, massv, *later = call(
                first_build,
                (tile_live, tile_tgt, src_feat, tile_feat, lin, amass),
                (
                    shape(each * slots * block),
                    shape(each * block),
                    SMEM((local + 1, slots), jnp.int32),
                    shape(every, pairs, jnp.bfloat16),
                    shape(local * block, width, src_feat.dtype),
                    shape(local),
                    shape(local),
                    *[feats] * (PIECES - 1),
                ),
                scratch=[
                    SMEM((local,), jnp.int32),
                    SMEM((local, slots), jnp.int32),
                    VMEM((pairs, every), f32),
                    feats,
                    pltpu.SemaphoreType.DMA((5 + each + PIECES - 1,)),
                ],
                hbm=(0, 1, 2, 3, 4, 5),
                **cost,
            )
            kern.append(k0)
            la.append(la0)
        elif at < PIECES:
            k0, la0 = call(
                functools.partial(later_build, at * each),
                (plan, xv, later[at - 1], linv, massv),
                (shape(each * slots * block), shape(each * block)),
                smem=1,
                **cost,
            )
            kern.append(k0)
            la.append(la0)
        if at < len(order) - 1:
            part = jnp.stack([part, got], axis=0).reshape(-1, block)
            if at < PIECES - 1:
                part, later[at], kern[-1] = lax.optimization_barrier(
                    (part, later[at], kern[-1])
                )
    acc = VMEM((local * block, block), f32)
    col = VMEM((pairs, block), f32)
    w = VMEM((every + 8, block), f32)
    half = every // 2
    keep, send, fb, et, tot = call(
        functools.partial(first_sweep, PIECES),
        (plan, hit, *kern, *la, part, got),
        (shape(half), shape(half), shape(every), shape(every), shape(8)),
        scratch=[w, acc, acc, col],
        smem=1,
    )
    u = None
    for iteration in range(ITERS):
        keep = keep + exchange(send, n, order[-1])
        for d in order[-2::-1]:
            keep = keep + exchange(keep, n, d)
        other = exchange(keep, n, order[-1])
        if iteration < ITERS - 1:
            last = iteration == ITERS - 2
            outs = (shape(half), shape(half)) + ((shape(local * block),) if last else ())
            keep, send, *u = call(
                functools.partial(next_sweep, PIECES),
                (plan, hit, keep, other, fb, et, tot, *kern, *la),
                outs,
                scratch=[w, acc, col] if last else [acc, w, acc, col],
                smem=1,
            )
    src, tgt = call(
        last_kernel,
        (keep, other, fb, et, tot, *u),
        [jax.ShapeDtypeStruct((local, block), f32)] * 2,
        scratch=[VMEM((every, block), f32)],
    )
    return (src.reshape(-1), tgt.reshape(-1))


def solution(mesh):
    split = P(("pairs", "src"))
    rows = P(("pairs", "src"), None)
    in_specs = (rows, P(("pairs", "src"), None, None, None), rows) + (split,) * 6
    return jax.shard_map(
        shards, mesh=mesh, in_specs=in_specs, out_specs=(split, split), check_vma=False
    )
```

```python
import functools

import jax
import jax.numpy as jnp
from jax import lax
from jax.experimental import pallas as pl
from jax.experimental.pallas import tpu as pltpu
from jax.sharding import PartitionSpec as P

ITERS = 3
EPS = 0.1
RHO = 1.0
ALPHA = 0.5
F = RHO / (RHO + EPS)
LOG2E = 1.4426950408889634
STEP = 4
ABSENT = -1e30
PIECES = (2, 2, 3, 1)

VMEM = pltpu.VMEM
SMEM = pltpu.SMEM
NT = (((1,), (1,)), ((), ()))


def diag_mask(block):
    return lax.broadcasted_iota(jnp.int32, (block, block), 0) == lax.broadcasted_iota(
        jnp.int32, (block, block), 1
    )


def to_column(row, mask):
    return jnp.sum(jnp.where(mask, row, 0.0), axis=1, keepdims=True)


def to_row(column, mask):
    return jnp.sum(jnp.where(mask, column, 0.0), axis=0, keepdims=True)


def position():
    return lax.axis_index("src").astype(jnp.int32)


def half_flip(every):
    at = position()
    for r in (16, 8, 4, 2, 1):
        at = at ^ (at >> r)
    return (at & 1) * (every // 2)


def total_of(x):
    return jnp.sum(jnp.sum(x, axis=0, keepdims=True), axis=1, keepdims=True)


def steps_of(live_s):
    return (live_s + (STEP - 1)) // STEP


def pack_kernel(count_hbm, mass_hbm, lin_hbm, amass_hbm, out_ref, count, sems):
    local, block = mass_hbm.shape
    copies = [(count_hbm, count)]
    for i, x in enumerate((mass_hbm, lin_hbm, amass_hbm)):
        copies.append((x, out_ref.at[pl.ds(i * local, local)]))
    copies = [pltpu.make_async_copy(f, t, sems.at[i]) for i, (f, t) in enumerate(copies)]
    for c in copies:
        c.start()
    for c in copies:
        c.wait()
    lane = lax.broadcasted_iota(jnp.int32, (1, block), 1)
    for i in range(local):
        row = slice(i, i + 1)
        out_ref[row, :] = jnp.where(lane < count[i], out_ref[row, :], 0.0)


def build_tiles(steps, first, x_ref, lin_ref, mass_ref, feat, waits, k_ref, la_ref):
    blocks, slots, block, width = feat.shape
    scale = LOG2E / (width * EPS)
    mask = diag_mask(block)
    for s in range(blocks):
        at = first + s
        x = x_ref[at * block : (at + 1) * block, :]
        x32 = x.astype(jnp.float32)
        sq = jnp.sum(x32 * x32, axis=1, keepdims=True)
        lin = to_column(lin_ref[at : at + 1, :], mask)
        base = (2.0 - sq / width - ALPHA * lin) * (LOG2E / EPS)
        base = jnp.broadcast_to(base, (block, block))
        la = F * jnp.log(to_column(mass_ref[at : at + 1, :], mask))
        la_ref[s * block : (s + 1) * block, :] = jnp.broadcast_to(la, (block, block))
        if waits:
            waits[s].wait()

        def tiles(p, _):
            y = feat[s, pl.ds(p * STEP, STEP)].reshape(STEP * block, width)
            y32 = y.astype(jnp.float32)
            y2 = y32 * y32
            ysq = jnp.sum(y2[:, : width // 2] + y2[:, width // 2 :], axis=1, keepdims=True)
            cross = lax.dot_general(x, y, NT, preferred_element_type=jnp.float32)
            for q in range(STEP):
                cols = slice(q * block, (q + 1) * block)
                row = to_row(ysq[cols, :], mask)
                e = (2.0 * scale) * cross[:, cols] + (base - row * scale)
                start = pl.multiple_of((s * slots + p * STEP + q) * block, block)
                k_ref[pl.ds(start, block), :] = jnp.exp2(e)
            return 0

        lax.fori_loop(0, steps(at), tiles, 0)


def first_build(live_hbm, tgt_hbm, x_hbm, lin_hbm, mass_hbm, feat, *refs):
    k_ref, la_ref, next_ref, plan_ref, hit_ref, x_ref, lin_ref, mass_ref = refs[:8]
    live, tgt, flags, own, sems = refs[8:]
    size, slots = own.shape[:2]
    copies = [(live_hbm, live), (tgt_hbm, tgt), (x_hbm, x_ref), (lin_hbm, lin_ref), (mass_hbm, mass_ref)]
    copies += [(feat.at[s], own.at[s]) for s in range(size)]
    copies += [(feat.at[pl.ds(size, next_ref.shape[0])], next_ref)]
    copies = [pltpu.make_async_copy(f, t, sems.at[i]) for i, (f, t) in enumerate(copies)]
    for c in copies:
        c.start()
    for c in copies[:5]:
        c.wait()
    every = flags.shape[1]
    flip = half_flip(every)
    lane = lax.broadcasted_iota(jnp.int32, (1, every), 1)
    for at in range(flags.shape[0]):
        s, k = divmod(at, slots)
        row = jnp.where(k < live[s], tgt[s, k] ^ flip, every)
        plan_ref[s, k] = row
        flags[at : at + 1, :] = jnp.where(lane == row, 1.0, 0.0)
    for s in range(tgt.shape[0]):
        plan_ref[tgt.shape[0], s] = steps_of(live[s])
    hit_ref[...] = jnp.transpose(flags[...]).astype(jnp.bfloat16)
    build_tiles(
        lambda s: steps_of(live[s]), 0, x_ref, lin_ref, mass_ref, own, copies[5:-1], k_ref, la_ref
    )
    copies[-1].wait()


def later_build(first, plan, x_ref, lin_ref, mass_ref, own, feat, k_ref, la_ref, *rest):
    copy = None
    if rest:
        next_ref, sem = rest
        copy = pltpu.make_async_copy(
            feat.at[pl.ds(first + own.shape[0], next_ref.shape[0])], next_ref, sem
        )
        copy.start()
    build_tiles(
        lambda s: plan[plan.shape[0] - 1, s], first, x_ref, lin_ref, mass_ref, own, (), k_ref, la_ref
    )
    if copy:
        copy.wait()


def place(s):
    piece = 0
    while s >= PIECES[piece]:
        s -= PIECES[piece]
        piece += 1
    return piece, s


def sweep(plan, hit_ref, w_ref, k_refs, la_refs, keep_ref, send_ref, acc_ref, u_ref, col_ref):
    blocks, slots = plan.shape[0] - 1, plan.shape[1]
    block = w_ref.shape[1]
    every = w_ref.shape[0] - 8
    w_ref[every:, :] = jnp.zeros((8, block), jnp.float32)
    for s in range(blocks):
        piece, at = place(s)
        k_ref, base = k_refs[piece], at * slots

        def add_row(p, acc):
            for q in range(STEP):
                k = p * STEP + q
                row = plan[s, k]
                start = pl.multiple_of((base + k) * block, block)
                acc = acc + k_ref[pl.ds(start, block), :] * w_ref[pl.ds(row, 1), :]
            return acc

        acc_ref[s * block : (s + 1) * block, :] = lax.fori_loop(
            0, plan[blocks, s], add_row, jnp.zeros((block, block), jnp.float32)
        )
    for s in range(blocks):
        rows = pl.ds(s * block, block)
        total = jnp.sum(acc_ref[rows, :], axis=1, keepdims=True)
        piece, at = place(s)
        la = la_refs[piece][pl.ds(at * block, block), :]
        u_ref[rows, :] = jnp.exp(la - F * jnp.log(total))
    col_ref[...] = jnp.zeros_like(col_ref)
    for s in range(blocks):
        piece, at = place(s)
        k_ref, base = k_refs[piece], at * slots
        u = u_ref[s * block : (s + 1) * block, :]

        def add_col(p, _):
            for q in range(STEP):
                k = p * STEP + q
                start = pl.multiple_of((base + k) * block, block)
                col_ref[pl.ds(s * slots + k, 1), :] = jnp.sum(
                    k_ref[pl.ds(start, block), :] * u, axis=0, keepdims=True
                )
            return 0

        lax.fori_loop(0, plan[blocks, s], add_col, 0)
    col = col_ref[...]
    hit = hit_ref[...]
    dense = jnp.zeros((every, block), jnp.float32)
    for _ in range(2):
        piece = col.astype(jnp.bfloat16)
        dense += jnp.dot(hit, piece, preferred_element_type=jnp.float32)
        col = col - piece.astype(jnp.float32)
    keep_ref[...] = dense[: every // 2, :]
    send_ref[...] = dense[every // 2 :, :]


def first_sweep(npieces, plan, hit_ref, *refs):
    k_refs, la_refs = refs[:npieces], refs[npieces : 2 * npieces]
    parts = refs[2 * npieces : 2 * npieces + 2]
    keep_ref, send_ref, fb_ref, et_ref, tot_ref, w_ref, acc_ref, u_ref, col_ref = refs[
        2 * npieces + 2 :
    ]
    local = plan.shape[0] - 1
    flip = half_flip(fb_ref.shape[0])
    n = fb_ref.shape[0] // local
    am = jnp.zeros((local, fb_ref.shape[1]), jnp.float32)
    bm = am
    order = distances(n)
    for at in range(n):
        m = functools.reduce(lambda p, q: p ^ q, [d for r, d in enumerate(order) if at >> r & 1], 0)
        part = parts[at // (n // 2)]
        at = (at % (n // 2)) * 3 * local
        rows = pl.ds(pl.multiple_of(((position() ^ m) * local) ^ flip, local), local)
        b = part[at : at + local, :]
        et = jnp.exp((-ALPHA / EPS) * part[at + local : at + 2 * local, :])
        fb_ref[rows, :] = jnp.where(b > 0.0, F * jnp.log(b), ABSENT)
        et_ref[rows, :] = et
        w_ref[rows, :] = jnp.where(b > 0.0, et, 0.0)
        bm += b
        am += part[at + 2 * local : at + 3 * local, :]
    tot = jnp.sqrt(total_of(am) * total_of(bm))
    tot_ref[...] = jnp.broadcast_to(tot, tot_ref.shape)
    sweep(plan, hit_ref, w_ref, k_refs, la_refs, keep_ref, send_ref, acc_ref, u_ref, col_ref)


def new_scale(keep, other, fb_ref, et_ref, tot_ref, t_ref):
    half = keep.shape[0]
    mass = jnp.zeros((1, keep.shape[1]), jnp.float32)
    for at, sums in ((0, keep), (half, other)):
        rows = slice(at, at + half)
        fb = fb_ref[rows, :]
        col = sums[...] * et_ref[rows, :]
        t = jnp.where(fb > ABSENT, jnp.exp(fb - F * jnp.log(col)), 0.0)
        t_ref[rows, :] = t
        mass += jnp.sum(t * col, axis=0, keepdims=True)
    return jnp.sqrt(tot_ref[0:1, 0:1] / jnp.sum(mass, axis=1, keepdims=True))


def next_sweep(npieces, plan, hit_ref, keep, other, fb_ref, et_ref, tot_ref, *refs):
    k_refs, la_refs = refs[:npieces], refs[npieces : 2 * npieces]
    keep_ref, send_ref, u_ref, w_ref, acc_ref, col_ref = refs[2 * npieces :]
    factor = new_scale(keep, other, fb_ref, et_ref, tot_ref, w_ref)
    rows = slice(0, fb_ref.shape[0])
    w_ref[rows, :] = w_ref[rows, :] * (factor * et_ref[...])
    sweep(plan, hit_ref, w_ref, k_refs, la_refs, keep_ref, send_ref, acc_ref, u_ref, col_ref)


def last_kernel(keep, other, fb_ref, et_ref, tot_ref, u_ref, src_ref, tgt_ref, t_ref):
    local, block = src_ref.shape
    factor = new_scale(keep, other, fb_ref, et_ref, tot_ref, t_ref)
    own = (position() * local) ^ half_flip(fb_ref.shape[0])
    tgt_ref[...] = t_ref[pl.ds(pl.multiple_of(own, local), local), :] * factor
    mask = diag_mask(block)
    for s in range(local):
        src_ref[s : s + 1, :] = to_row(u_ref[s * block : (s + 1) * block, :] * factor, mask)


def call(kernel, ins, outs, scratch=(), smem=0, hbm=(), vmem_mb=12, **cost):
    specs = [pl.BlockSpec(memory_space=SMEM)] * smem
    for at in range(smem, len(ins)):
        specs.append(pl.BlockSpec(memory_space=pl.ANY if at in hbm else VMEM))
    ins = [
        pltpu.with_memory_space_constraint(x, pltpu.HBM) if at in hbm else x
        for at, x in enumerate(ins)
    ]
    return pl.pallas_call(
        kernel,
        out_shape=outs,
        in_specs=specs,
        out_specs=[
            pl.BlockSpec(memory_space=SMEM if out.dtype == jnp.int32 else VMEM) for out in outs
        ],
        scratch_shapes=scratch,
        compiler_params=pltpu.CompilerParams(vmem_limit_bytes=vmem_mb << 20),
        cost_estimate=pl.CostEstimate(**cost) if cost else None,
    )(*ins)


def distances(n):
    return [d | 1 for d in (n >> r for r in range(1, n.bit_length()))]


def exchange(x, n, d):
    return lax.ppermute(x, "src", [(i, i ^ d) for i in range(n)])


def shards(
    src_feat, tile_feat, tile_tgt, tile_live, src_lin, tgt_lin, src_mass, tgt_mass, tgt_count
):
    f32 = jnp.float32
    local, slots, block, width = tile_feat.shape
    n = lax.axis_size("src")
    every = local * n
    pairs = local * slots
    lin = src_lin.reshape(local, block)
    amass = src_mass.reshape(local, block)
    def shape(rows, cols=block, dtype=f32):
        return pltpu.VMEM((rows, cols), dtype)

    (part,) = call(
        pack_kernel,
        (tgt_count, tgt_mass.reshape(local, block), tgt_lin.reshape(local, block), amass),
        (shape(3 * local),),
        scratch=[SMEM((local,), jnp.int32), pltpu.SemaphoreType.DMA((4,))],
        hbm=(0, 1, 2, 3),
    )
    def feats(size):
        return pltpu.VMEM((size, slots, block, width), tile_feat.dtype)

    order = distances(n)
    kern, la = [], []
    following = None
    for at, d in enumerate(order):
        got = exchange(part, n, d)
        if at < len(PIECES):
            size = PIECES[at]
            ahead = [feats(PIECES[at + 1])] if at + 1 < len(PIECES) else []
            outs = (shape(size * slots * block), shape(size * block), *ahead)
            cost = dict(
                flops=2 * size * slots * block * block * width,
                bytes_accessed=2 * size * slots * block * width,
                transcendentals=size * slots * block * block,
            )
        if at == 0:
            k0, la0, following, plan, hit, xv, linv, massv = call(
                first_build,
                (tile_live, tile_tgt, src_feat, lin, amass, tile_feat),
                (
                    *outs,
                    SMEM((local + 1, slots), jnp.int32),
                    shape(every, pairs, jnp.bfloat16),
                    shape(local * block, width, src_feat.dtype),
                    shape(local),
                    shape(local),
                ),
                scratch=[
                    SMEM((local,), jnp.int32),
                    SMEM((local, slots), jnp.int32),
                    VMEM((pairs, every), f32),
                    feats(size),
                    pltpu.SemaphoreType.DMA((6 + size,)),
                ],
                hbm=(0, 1, 2, 3, 4, 5),
                **cost,
            )
        elif at < len(PIECES):
            k0, la0, *following = call(
                functools.partial(later_build, sum(PIECES[:at])),
                (plan, xv, linv, massv, following, tile_feat),
                outs,
                scratch=[pltpu.SemaphoreType.DMA] if ahead else [],
                smem=1,
                hbm=(5,),
                **cost,
            )
            following = following[0] if following else None
        if at < len(PIECES):
            kern.append(k0)
            la.append(la0)
        if at < len(order) - 1:
            part = jnp.stack([part, got], axis=0).reshape(-1, block)
            if at < len(PIECES) - 1:
                part, following, kern[-1] = lax.optimization_barrier((part, following, kern[-1]))
    acc = VMEM((local * block, block), f32)
    col = VMEM((pairs, block), f32)
    w = VMEM((every + 8, block), f32)
    half = every // 2
    keep, send, fb, et, tot = call(
        functools.partial(first_sweep, len(PIECES)),
        (plan, hit, *kern, *la, part, got),
        (shape(half), shape(half), shape(every), shape(every), shape(8)),
        scratch=[w, acc, acc, col],
        smem=1,
    )
    u = None
    for iteration in range(ITERS):
        keep = keep + exchange(send, n, order[-1])
        for d in order[-2::-1]:
            keep = keep + exchange(keep, n, d)
        other = exchange(keep, n, order[-1])
        if iteration < ITERS - 1:
            last = iteration == ITERS - 2
            outs = (shape(half), shape(half)) + ((shape(local * block),) if last else ())
            keep, send, *u = call(
                functools.partial(next_sweep, len(PIECES)),
                (plan, hit, keep, other, fb, et, tot, *kern, *la),
                outs,
                scratch=[w, acc, col] if last else [acc, w, acc, col],
                smem=1,
            )
    src, tgt = call(
        last_kernel,
        (keep, other, fb, et, tot, *u),
        [jax.ShapeDtypeStruct((local, block), f32)] * 2,
        scratch=[VMEM((every, block), f32)],
    )
    return (src.reshape(-1), tgt.reshape(-1))


def solution(mesh):
    split = P(("pairs", "src"))
    rows = P(("pairs", "src"), None)
    in_specs = (rows, P(("pairs", "src"), None, None, None), rows) + (split,) * 6
    return jax.shard_map(
        shards, mesh=mesh, in_specs=in_specs, out_specs=(split, split), check_vma=False
    )
```

```python
import functools

import jax
import jax.numpy as jnp
from jax import lax
from jax.experimental import pallas as pl
from jax.experimental.pallas import tpu as pltpu
from jax.sharding import PartitionSpec as P

ITERS = 3
EPS = 0.1
RHO = 1.0
ALPHA = 0.5
F = RHO / (RHO + EPS)
LOG2E = 1.4426950408889634
STEP = 4
FAR = 4
ABSENT = -1e30
PIECES = (2, 2, 3, 1)

VMEM = pltpu.VMEM
SMEM = pltpu.SMEM
NT = (((1,), (1,)), ((), ()))


def diag_mask(block):
    return lax.broadcasted_iota(jnp.int32, (block, block), 0) == lax.broadcasted_iota(
        jnp.int32, (block, block), 1
    )


def to_column(row, mask):
    return jnp.sum(jnp.where(mask, row, 0.0), axis=1, keepdims=True)


def to_row(column, mask):
    return jnp.sum(jnp.where(mask, column, 0.0), axis=0, keepdims=True)


def position():
    return lax.axis_index("src").astype(jnp.int32)


def half_flip(every):
    at = position() & (lax.axis_size("src") // FAR - 1)
    for r in (16, 8, 4, 2, 1):
        at = at ^ (at >> r)
    return (at & 1) * (every // 2)


def total_of(x):
    return jnp.sum(jnp.sum(x, axis=0, keepdims=True), axis=1, keepdims=True)


def steps_of(live_s):
    return (live_s + (STEP - 1)) // STEP


def pack_kernel(count_hbm, mass_hbm, lin_hbm, amass_hbm, out_ref, count, sems):
    local, block = mass_hbm.shape
    copies = [(count_hbm, count)]
    for i, x in enumerate((mass_hbm, lin_hbm, amass_hbm)):
        copies.append((x, out_ref.at[pl.ds(i * local, local)]))
    copies = [pltpu.make_async_copy(f, t, sems.at[i]) for i, (f, t) in enumerate(copies)]
    for c in copies:
        c.start()
    for c in copies:
        c.wait()
    lane = lax.broadcasted_iota(jnp.int32, (1, block), 1)
    for i in range(local):
        row = slice(i, i + 1)
        out_ref[row, :] = jnp.where(lane < count[i], out_ref[row, :], 0.0)


def build_tiles(steps, first, x_ref, lin_ref, mass_ref, feat, waits, k_ref, la_ref):
    blocks, slots, block, width = feat.shape
    scale = LOG2E / (width * EPS)
    mask = diag_mask(block)
    for s in range(blocks):
        at = first + s
        x = x_ref[at * block : (at + 1) * block, :]
        x32 = x.astype(jnp.float32)
        sq = jnp.sum(x32 * x32, axis=1, keepdims=True)
        lin = to_column(lin_ref[at : at + 1, :], mask)
        base = (2.0 - sq / width - ALPHA * lin) * (LOG2E / EPS)
        base = jnp.broadcast_to(base, (block, block))
        la = F * jnp.log(to_column(mass_ref[at : at + 1, :], mask))
        la_ref[s * block : (s + 1) * block, :] = jnp.broadcast_to(la, (block, block))
        if waits:
            waits[s].wait()

        def tiles(p, _):
            y = feat[s, pl.ds(p * STEP, STEP)].reshape(STEP * block, width)
            y32 = y.astype(jnp.float32)
            y2 = y32 * y32
            ysq = jnp.sum(y2[:, : width // 2] + y2[:, width // 2 :], axis=1, keepdims=True)
            cross = lax.dot_general(x, y, NT, preferred_element_type=jnp.float32)
            for q in range(STEP):
                cols = slice(q * block, (q + 1) * block)
                row = to_row(ysq[cols, :], mask)
                e = (2.0 * scale) * cross[:, cols] + (base - row * scale)
                start = pl.multiple_of((s * slots + p * STEP + q) * block, block)
                k_ref[pl.ds(start, block), :] = jnp.exp2(e)
            return 0

        lax.fori_loop(0, steps(at), tiles, 0)


def first_build(live_hbm, tgt_hbm, x_hbm, lin_hbm, mass_hbm, feat, *refs):
    k_ref, la_ref, next_ref, plan_ref, hit_ref, x_ref, lin_ref, mass_ref = refs[:8]
    live, tgt, flags, own, sems = refs[8:]
    size, slots = own.shape[:2]
    copies = [(live_hbm, live), (tgt_hbm, tgt), (x_hbm, x_ref), (lin_hbm, lin_ref), (mass_hbm, mass_ref)]
    copies += [(feat.at[s], own.at[s]) for s in range(size)]
    copies += [(feat.at[pl.ds(size, next_ref.shape[0])], next_ref)]
    copies = [pltpu.make_async_copy(f, t, sems.at[i]) for i, (f, t) in enumerate(copies)]
    for c in copies:
        c.start()
    for c in copies[:5]:
        c.wait()
    every = flags.shape[1]
    flip = half_flip(every)
    lane = lax.broadcasted_iota(jnp.int32, (1, every), 1)
    for at in range(flags.shape[0]):
        s, k = divmod(at, slots)
        row = jnp.where(k < live[s], tgt[s, k] ^ flip, every)
        plan_ref[s, k] = row
        flags[at : at + 1, :] = jnp.where(lane == row, 1.0, 0.0)
    for s in range(tgt.shape[0]):
        plan_ref[tgt.shape[0], s] = steps_of(live[s])
    hit_ref[...] = jnp.transpose(flags[...]).astype(jnp.bfloat16)
    build_tiles(
        lambda s: steps_of(live[s]), 0, x_ref, lin_ref, mass_ref, own, copies[5:-1], k_ref, la_ref
    )
    copies[-1].wait()


def later_build(first, plan, x_ref, lin_ref, mass_ref, own, feat, k_ref, la_ref, *rest):
    copy = None
    if rest:
        next_ref, sem = rest
        copy = pltpu.make_async_copy(
            feat.at[pl.ds(first + own.shape[0], next_ref.shape[0])], next_ref, sem
        )
        copy.start()
    build_tiles(
        lambda s: plan[plan.shape[0] - 1, s], first, x_ref, lin_ref, mass_ref, own, (), k_ref, la_ref
    )
    if copy:
        copy.wait()


def place(s):
    piece = 0
    while s >= PIECES[piece]:
        s -= PIECES[piece]
        piece += 1
    return piece, s


def sweep(plan, hit_ref, w_ref, k_refs, la_refs, keep_ref, send_ref, acc_ref, u_ref, col_ref):
    blocks, slots = plan.shape[0] - 1, plan.shape[1]
    block = w_ref.shape[1]
    every = w_ref.shape[0] - 8
    w_ref[every:, :] = jnp.zeros((8, block), jnp.float32)
    for s in range(blocks):
        piece, at = place(s)
        k_ref, base = k_refs[piece], at * slots

        def add_row(p, acc):
            for q in range(STEP):
                k = p * STEP + q
                row = plan[s, k]
                start = pl.multiple_of((base + k) * block, block)
                acc = acc + k_ref[pl.ds(start, block), :] * w_ref[pl.ds(row, 1), :]
            return acc

        acc_ref[s * block : (s + 1) * block, :] = lax.fori_loop(
            0, plan[blocks, s], add_row, jnp.zeros((block, block), jnp.float32)
        )
    for s in range(blocks):
        rows = pl.ds(s * block, block)
        total = jnp.sum(acc_ref[rows, :], axis=1, keepdims=True)
        piece, at = place(s)
        la = la_refs[piece][pl.ds(at * block, block), :]
        u_ref[rows, :] = jnp.exp(la - F * jnp.log(total))
    col_ref[...] = jnp.zeros_like(col_ref)
    for s in range(blocks):
        piece, at = place(s)
        k_ref, base = k_refs[piece], at * slots
        u = u_ref[s * block : (s + 1) * block, :]

        def add_col(p, _):
            for q in range(STEP):
                k = p * STEP + q
                start = pl.multiple_of((base + k) * block, block)
                col_ref[pl.ds(s * slots + k, 1), :] = jnp.sum(
                    k_ref[pl.ds(start, block), :] * u, axis=0, keepdims=True
                )
            return 0

        lax.fori_loop(0, plan[blocks, s], add_col, 0)
    col = col_ref[...]
    hit = hit_ref[...]
    dense = jnp.zeros((every, block), jnp.float32)
    for _ in range(2):
        piece = col.astype(jnp.bfloat16)
        dense += jnp.dot(hit, piece, preferred_element_type=jnp.float32)
        col = col - piece.astype(jnp.float32)
    keep_ref[...] = dense[: every // 2, :]
    send_ref[...] = dense[every // 2 :, :]


def first_sweep(npieces, plan, hit_ref, *refs):
    k_refs, la_refs = refs[:npieces], refs[npieces : 2 * npieces]
    parts = refs[2 * npieces : 2 * npieces + 2]
    keep_ref, send_ref, fb_ref, et_ref, tot_ref, w_ref, acc_ref, u_ref, col_ref = refs[
        2 * npieces + 2 :
    ]
    local = plan.shape[0] - 1
    flip = half_flip(fb_ref.shape[0])
    n = fb_ref.shape[0] // local
    am = jnp.zeros((local, fb_ref.shape[1]), jnp.float32)
    bm = am
    order = distances(n)
    for at in range(n):
        m = functools.reduce(lambda p, q: p ^ q, [d for r, d in enumerate(order) if at >> r & 1], 0)
        part = parts[at // (n // 2)]
        at = (at % (n // 2)) * 3 * local
        rows = pl.ds(pl.multiple_of(((position() ^ m) * local) ^ flip, local), local)
        b = part[at : at + local, :]
        et = jnp.exp((-ALPHA / EPS) * part[at + local : at + 2 * local, :])
        fb_ref[rows, :] = jnp.where(b > 0.0, F * jnp.log(b), ABSENT)
        et_ref[rows, :] = et
        w_ref[rows, :] = jnp.where(b > 0.0, et, 0.0)
        bm += b
        am += part[at + 2 * local : at + 3 * local, :]
    tot = jnp.sqrt(total_of(am) * total_of(bm))
    tot_ref[...] = jnp.broadcast_to(tot, tot_ref.shape)
    sweep(plan, hit_ref, w_ref, k_refs, la_refs, keep_ref, send_ref, acc_ref, u_ref, col_ref)


def new_scale(keep, other, fb_ref, et_ref, tot_ref, t_ref):
    half = keep.shape[0]
    mass = jnp.zeros((1, keep.shape[1]), jnp.float32)
    for at, sums in ((0, keep), (half, other)):
        rows = slice(at, at + half)
        fb = fb_ref[rows, :]
        col = sums[...] * et_ref[rows, :]
        t = jnp.where(fb > ABSENT, jnp.exp(fb - F * jnp.log(col)), 0.0)
        t_ref[rows, :] = t
        mass += jnp.sum(t * col, axis=0, keepdims=True)
    return jnp.sqrt(tot_ref[0:1, 0:1] / jnp.sum(mass, axis=1, keepdims=True))


def next_sweep(npieces, plan, hit_ref, keep, other, fb_ref, et_ref, tot_ref, *refs):
    k_refs, la_refs = refs[:npieces], refs[npieces : 2 * npieces]
    keep_ref, send_ref, u_ref, w_ref, acc_ref, col_ref = refs[2 * npieces :]
    factor = new_scale(keep, other, fb_ref, et_ref, tot_ref, w_ref)
    rows = slice(0, fb_ref.shape[0])
    w_ref[rows, :] = w_ref[rows, :] * (factor * et_ref[...])
    sweep(plan, hit_ref, w_ref, k_refs, la_refs, keep_ref, send_ref, acc_ref, u_ref, col_ref)


def last_kernel(keep, other, fb_ref, et_ref, tot_ref, u_ref, src_ref, tgt_ref, t_ref):
    local, block = src_ref.shape
    factor = new_scale(keep, other, fb_ref, et_ref, tot_ref, t_ref)
    own = (position() * local) ^ half_flip(fb_ref.shape[0])
    tgt_ref[...] = t_ref[pl.ds(pl.multiple_of(own, local), local), :] * factor
    mask = diag_mask(block)
    for s in range(local):
        src_ref[s : s + 1, :] = to_row(u_ref[s * block : (s + 1) * block, :] * factor, mask)


def call(kernel, ins, outs, scratch=(), smem=0, hbm=(), vmem_mb=12, **cost):
    specs = [pl.BlockSpec(memory_space=SMEM)] * smem
    for at in range(smem, len(ins)):
        specs.append(pl.BlockSpec(memory_space=pl.ANY if at in hbm else VMEM))
    ins = [
        pltpu.with_memory_space_constraint(x, pltpu.HBM) if at in hbm else x
        for at, x in enumerate(ins)
    ]
    return pl.pallas_call(
        kernel,
        out_shape=outs,
        in_specs=specs,
        out_specs=[
            pl.BlockSpec(memory_space=SMEM if out.dtype == jnp.int32 else VMEM) for out in outs
        ],
        scratch_shapes=scratch,
        compiler_params=pltpu.CompilerParams(vmem_limit_bytes=vmem_mb << 20),
        cost_estimate=pl.CostEstimate(**cost) if cost else None,
    )(*ins)


def distances(n):
    return [d | 1 for d in (n >> r for r in range(1, n.bit_length()))]


def exchange(x, n, d):
    return lax.ppermute(x, "src", [(i, i ^ d) for i in range(n)])


def shards(
    src_feat, tile_feat, tile_tgt, tile_live, src_lin, tgt_lin, src_mass, tgt_mass, tgt_count
):
    f32 = jnp.float32
    local, slots, block, width = tile_feat.shape
    n = lax.axis_size("src")
    every = local * n
    pairs = local * slots
    lin = src_lin.reshape(local, block)
    amass = src_mass.reshape(local, block)
    def shape(rows, cols=block, dtype=f32):
        return pltpu.VMEM((rows, cols), dtype)

    (part,) = call(
        pack_kernel,
        (tgt_count, tgt_mass.reshape(local, block), tgt_lin.reshape(local, block), amass),
        (shape(3 * local),),
        scratch=[SMEM((local,), jnp.int32), pltpu.SemaphoreType.DMA((4,))],
        hbm=(0, 1, 2, 3),
    )
    def feats(size):
        return pltpu.VMEM((size, slots, block, width), tile_feat.dtype)

    order = distances(n)
    kern, la = [], []
    following = None
    for at, d in enumerate(order):
        got = exchange(part, n, d)
        if at < len(PIECES):
            size = PIECES[at]
            ahead = [feats(PIECES[at + 1])] if at + 1 < len(PIECES) else []
            outs = (shape(size * slots * block), shape(size * block), *ahead)
            cost = dict(
                flops=2 * size * slots * block * block * width,
                bytes_accessed=2 * size * slots * block * width,
                transcendentals=size * slots * block * block,
            )
        if at == 0:
            k0, la0, following, plan, hit, xv, linv, massv = call(
                first_build,
                (tile_live, tile_tgt, src_feat, lin, amass, tile_feat),
                (
                    *outs,
                    SMEM((local + 1, slots), jnp.int32),
                    shape(every, pairs, jnp.bfloat16),
                    shape(local * block, width, src_feat.dtype),
                    shape(local),
                    shape(local),
                ),
                scratch=[
                    SMEM((local,), jnp.int32),
                    SMEM((local, slots), jnp.int32),
                    VMEM((pairs, every), f32),
                    feats(size),
                    pltpu.SemaphoreType.DMA((6 + size,)),
                ],
                hbm=(0, 1, 2, 3, 4, 5),
                **cost,
            )
        elif at < len(PIECES):
            k0, la0, *following = call(
                functools.partial(later_build, sum(PIECES[:at])),
                (plan, xv, linv, massv, following, tile_feat),
                outs,
                scratch=[pltpu.SemaphoreType.DMA] if ahead else [],
                smem=1,
                hbm=(5,),
                **cost,
            )
            following = following[0] if following else None
        if at < len(PIECES):
            kern.append(k0)
            la.append(la0)
        if at < len(order) - 1:
            part = jnp.stack([part, got], axis=0).reshape(-1, block)
            if at < len(PIECES) - 1:
                part, following, kern[-1] = lax.optimization_barrier((part, following, kern[-1]))
    acc = VMEM((local * block, block), f32)
    col = VMEM((pairs, block), f32)
    w = VMEM((every + 8, block), f32)
    half = every // 2
    keep, send, fb, et, tot = call(
        functools.partial(first_sweep, len(PIECES)),
        (plan, hit, *kern, *la, part, got),
        (shape(half), shape(half), shape(every), shape(every), shape(8)),
        scratch=[w, acc, acc, col],
        smem=1,
    )
    u = None
    for iteration in range(ITERS):
        keep = keep + exchange(send, n, order[-1])
        for d in order[-2:1:-1]:
            keep = keep + exchange(keep, n, d)
        near = n // FAR
        groups = [[i + near * z for z in range(FAR)] for i in range(near)]
        sums = lax.all_gather(keep, "src", axis_index_groups=groups, axis=0)
        keep = functools.reduce(lambda p, q: p + q, [sums[z] for z in range(FAR)])
        other = exchange(keep, n, order[-1])
        if iteration < ITERS - 1:
            last = iteration == ITERS - 2
            outs = (shape(half), shape(half)) + ((shape(local * block),) if last else ())
            keep, send, *u = call(
                functools.partial(next_sweep, len(PIECES)),
                (plan, hit, keep, other, fb, et, tot, *kern, *la),
                outs,
                scratch=[w, acc, col] if last else [acc, w, acc, col],
                smem=1,
            )
    src, tgt = call(
        last_kernel,
        (keep, other, fb, et, tot, *u),
        [jax.ShapeDtypeStruct((local, block), f32)] * 2,
        scratch=[VMEM((every, block), f32)],
    )
    return (src.reshape(-1), tgt.reshape(-1))


def solution(mesh):
    split = P(("pairs", "src"))
    rows = P(("pairs", "src"), None)
    in_specs = (rows, P(("pairs", "src"), None, None, None), rows) + (split,) * 6
    return jax.shard_map(
        shards, mesh=mesh, in_specs=in_specs, out_specs=(split, split), check_vma=False
    )
```

```python
import functools

import jax
import jax.numpy as jnp
from jax import lax
from jax.experimental import pallas as pl
from jax.experimental.pallas import tpu as pltpu
from jax.sharding import PartitionSpec as P

ITERS = 3
EPS = 0.1
RHO = 1.0
ALPHA = 0.5
F = RHO / (RHO + EPS)
LOG2E = 1.4426950408889634
STEP = 4
ABSENT = -1e30
PIECES = (2, 3, 3)

VMEM = pltpu.VMEM
SMEM = pltpu.SMEM
NT = (((1,), (1,)), ((), ()))


def diag_mask(block):
    return lax.broadcasted_iota(jnp.int32, (block, block), 0) == lax.broadcasted_iota(
        jnp.int32, (block, block), 1
    )


def to_column(row, mask):
    return jnp.sum(jnp.where(mask, row, 0.0), axis=1, keepdims=True)


def to_row(column, mask):
    return jnp.sum(jnp.where(mask, column, 0.0), axis=0, keepdims=True)


def position():
    return lax.axis_index("src").astype(jnp.int32)


def parity(x):
    for r in (4, 2, 1):
        x = x ^ (x >> r)
    return x & 1


def place_of(block, local, half, me):
    owner = block >> (local.bit_length() - 1)
    return parity(owner ^ me) * half + (owner >> 1) * local + (block & (local - 1))


def total_of(x):
    return jnp.sum(jnp.sum(x, axis=0, keepdims=True), axis=1, keepdims=True)


def pack_kernel(count_hbm, mass_hbm, lin_hbm, amass_hbm, out_ref, count, sems):
    local, block = mass_hbm.shape
    copies = [(count_hbm, count)]
    for i, x in enumerate((mass_hbm, lin_hbm, amass_hbm)):
        copies.append((x, out_ref.at[pl.ds(i * local, local)]))
    copies = [pltpu.make_async_copy(f, t, sems.at[i]) for i, (f, t) in enumerate(copies)]
    for c in copies:
        c.start()
    for c in copies:
        c.wait()
    lane = lax.broadcasted_iota(jnp.int32, (1, block), 1)
    for i in range(local):
        row = slice(i, i + 1)
        out_ref[row, :] = jnp.where(lane < count[i], out_ref[row, :], 0.0)


def build_tiles(plan, first, x_ref, lin_ref, mass_ref, feat, waits, k_ref, la_ref):
    blocks, slots, block, width = feat.shape
    scale = LOG2E / (width * EPS)
    mask = diag_mask(block)
    for s in range(blocks):
        at = first + s
        x = x_ref[at * block : (at + 1) * block, :]
        x32 = x.astype(jnp.float32)
        sq = jnp.sum(x32 * x32, axis=1, keepdims=True)
        lin = to_column(lin_ref[at : at + 1, :], mask)
        base = (2.0 - sq / width - ALPHA * lin) * (LOG2E / EPS)
        base = jnp.broadcast_to(base, (block, block))
        la = F * jnp.log(to_column(mass_ref[at : at + 1, :], mask))
        la_ref[s * block : (s + 1) * block, :] = jnp.broadcast_to(la, (block, block))
        if waits:
            waits[s].wait()

        def tiles(p, _):
            y = [feat[s, plan[at, p * STEP + q]] for q in range(STEP)]
            y = jnp.concatenate(y, axis=0)
            y32 = y.astype(jnp.float32)
            y2 = y32 * y32
            ysq = jnp.sum(y2[:, : width // 2] + y2[:, width // 2 :], axis=1, keepdims=True)
            cross = lax.dot_general(x, y, NT, preferred_element_type=jnp.float32)
            for q in range(STEP):
                cols = slice(q * block, (q + 1) * block)
                row = to_row(ysq[cols, :], mask)
                e = (2.0 * scale) * cross[:, cols] + (base - row * scale)
                start = pl.multiple_of((s * slots + p * STEP + q) * block, block)
                k_ref[pl.ds(start, block), :] = jnp.exp2(e)
            return 0

        lax.fori_loop(0, plan[2 * lin_ref.shape[0], at], tiles, 0)


def first_build(live_hbm, tgt_hbm, x_hbm, lin_hbm, mass_hbm, feat, *refs):
    k_ref, la_ref, next_ref, plan_ref, hit_ref, x_ref, lin_ref, mass_ref = refs[:8]
    live, tgt, flags, own, sems = refs[8:]
    size, slots = own.shape[:2]
    copies = [(live_hbm, live), (tgt_hbm, tgt), (x_hbm, x_ref), (lin_hbm, lin_ref), (mass_hbm, mass_ref)]
    copies += [(feat.at[s], own.at[s]) for s in range(size)]
    copies += [(feat.at[pl.ds(size, next_ref.shape[0])], next_ref)]
    copies = [pltpu.make_async_copy(f, t, sems.at[i]) for i, (f, t) in enumerate(copies)]
    for c in copies:
        c.start()
    for c in copies[:5]:
        c.wait()
    every = flags.shape[1]
    local = tgt.shape[0]
    me = position()
    lane = lax.broadcasted_iota(jnp.int32, (1, every), 1)
    for s in range(local):
        rows = [place_of(tgt[s, k], local, every // 2, me) for k in range(slots)]
        mine = [jnp.where(r < every // 2, 1, 0) for r in rows]
        used = [jnp.where(k < live[s], 1, 0) for k in range(slots)]
        own_count = functools.reduce(lambda p, q: p + q, [m * v for m, v in zip(mine, used)])
        at_own, at_other = jnp.int32(0), own_count
        for q in range(STEP):
            plan_ref[s, live[s] + q] = 0
            plan_ref[local + s, live[s] + q] = every
        for k in range(slots):
            at = jnp.where(mine[k] == 1, at_own, at_other)
            at = jnp.where(used[k] == 1, at, slots + STEP)
            plan_ref[s, at] = k
            plan_ref[local + s, at] = rows[k]
            at_own += mine[k] * used[k]
            at_other += (1 - mine[k]) * used[k]
        plan_ref[2 * local, s] = (live[s] + (STEP - 1)) // STEP
        plan_ref[2 * local + 1, s] = (own_count + (STEP - 1)) // STEP
        plan_ref[2 * local + 2, s] = own_count // STEP
    for at in range(flags.shape[0]):
        s, k = divmod(at, slots)
        row = jnp.where(k < live[s], plan_ref[local + s, k], every)
        flags[at : at + 1, :] = jnp.where(lane == row, 1.0, 0.0)
    hit_ref[...] = jnp.transpose(flags[...]).astype(jnp.bfloat16)
    build_tiles(plan_ref, 0, x_ref, lin_ref, mass_ref, own, copies[5:-1], k_ref, la_ref)
    copies[-1].wait()


def later_build(first, plan, x_ref, lin_ref, mass_ref, own, feat, k_ref, la_ref, *rest):
    copy = None
    if rest:
        next_ref, sem = rest
        copy = pltpu.make_async_copy(
            feat.at[pl.ds(first + own.shape[0], next_ref.shape[0])], next_ref, sem
        )
        copy.start()
    build_tiles(plan, first, x_ref, lin_ref, mass_ref, own, (), k_ref, la_ref)
    if copy:
        copy.wait()


def place(s):
    piece = 0
    while s >= PIECES[piece]:
        s -= PIECES[piece]
        piece += 1
    return piece, s


def add_rows(plan, span, w_ref, k_refs, done):
    blocks, block = (plan.shape[0] - 3) // 2, w_ref.shape[1]
    slots = plan.shape[1] - 2 * STEP
    for s in range(blocks):
        piece, at = place(s)
        k_ref, base = k_refs[piece], at * slots

        def add_row(p, acc):
            for q in range(STEP):
                k = p * STEP + q
                start = pl.multiple_of((base + k) * block, block)
                w = w_ref[pl.ds(plan[blocks + s, k], 1), :]
                acc = acc + k_ref[pl.ds(start, block), :] * w
            return acc

        first, last = span(s)
        done(s, lax.fori_loop(first, last, add_row, jnp.zeros((block, block), jnp.float32)))


def add_columns(plan, span, u_ref, k_refs, hit, col_ref):
    blocks, block = (plan.shape[0] - 3) // 2, col_ref.shape[1]
    slots = plan.shape[1] - 2 * STEP
    col_ref[...] = jnp.zeros_like(col_ref)
    for s in range(blocks):
        piece, at = place(s)
        k_ref, base = k_refs[piece], at * slots
        u = u_ref[s * block : (s + 1) * block, :]

        def add_col(p, _):
            for q in range(STEP):
                k = p * STEP + q
                start = pl.multiple_of((base + k) * block, block)
                col_ref[pl.ds(s * slots + k, 1), :] = jnp.sum(
                    k_ref[pl.ds(start, block), :] * u, axis=0, keepdims=True
                )
            return 0

        first, last = span(s)
        lax.fori_loop(first, last, add_col, 0)
    col = col_ref[...]
    dense = jnp.zeros((hit.shape[0], block), jnp.float32)
    for _ in range(2):
        term = col.astype(jnp.bfloat16)
        dense += jnp.dot(hit, term, preferred_element_type=jnp.float32)
        col = col - term.astype(jnp.float32)
    return dense


def own_span(plan):
    local = (plan.shape[0] - 3) // 2
    return lambda s: (0, plan[2 * local + 1, s])


def other_span(plan):
    local = (plan.shape[0] - 3) // 2
    return lambda s: (plan[2 * local + 2, s], plan[2 * local, s])


def spread(w_ref, w, other):
    half = w.shape[0]
    zeros = jnp.zeros((half, w.shape[1]), jnp.float32)
    w_ref[:half, :] = zeros if other else w
    w_ref[half : 2 * half, :] = w if other else zeros
    w_ref[2 * half :, :] = zeros[:8, :]


def unpack(part, fb_ref, et_ref):
    half, block = fb_ref.shape
    n = lax.axis_size("src")
    local = 2 * half // n
    order = distances(n)
    am = jnp.zeros((local, block), jnp.float32)
    bm = am
    for at in range(n // 2):
        m = functools.reduce(lambda p, q: p ^ q, [d for r, d in enumerate(order) if at >> r & 1], 0)
        rows = pl.ds(pl.multiple_of(((position() ^ m) >> 1) * local, local), local)
        at = at * 3 * local
        b = part[at : at + local, :]
        fb_ref[rows, :] = jnp.where(b > 0.0, F * jnp.log(b), ABSENT)
        et_ref[rows, :] = jnp.exp((-ALPHA / EPS) * part[at + local : at + 2 * local, :])
        bm += b
        am += part[at + 2 * local : at + 3 * local, :]
    return am, bm


def half_scale(sums, fb_ref, et_ref):
    fb = fb_ref[...]
    col = sums[...] * et_ref[...]
    t = jnp.where(fb > ABSENT, jnp.exp(fb - F * jnp.log(col)), 0.0)
    return t, jnp.sum(t * col, axis=0, keepdims=True)


def finish(plan, hit_ref, factor, acc_ref, w_ref, k_refs, la_refs, send_ref, u_ref, col_ref):
    block = w_ref.shape[1]

    def scale(s, acc):
        rows = pl.ds(s * block, block)
        total = jnp.sum(acc + acc_ref[rows, :], axis=1, keepdims=True)
        if factor is not None:
            total = total * factor
        piece, at = place(s)
        la = la_refs[piece][pl.ds(at * block, block), :]
        u_ref[rows, :] = jnp.exp(la - F * jnp.log(total))

    add_rows(plan, other_span(plan), w_ref, k_refs, scale)
    hit = hit_ref[send_ref.shape[0] :, :]
    send_ref[...] = add_columns(plan, other_span(plan), u_ref, k_refs, hit, col_ref)


def keep_rows(acc_ref):
    block = acc_ref.shape[1]

    def keep(s, acc):
        acc_ref[s * block : (s + 1) * block, :] = acc

    return keep


def first_own(plan, part, *refs):
    k_refs, (acc_ref, fb_ref, et_ref, sums_ref, w_ref) = refs[:-5], refs[-5:]
    am, bm = unpack(part, fb_ref, et_ref)
    sums_ref[:8, :], sums_ref[8:, :] = am, bm
    spread(w_ref, jnp.where(fb_ref[...] > ABSENT, et_ref[...], 0.0), False)
    add_rows(plan, own_span(plan), w_ref, k_refs, keep_rows(acc_ref))


def first_other(plan, hit_ref, part, sums_ref, acc_ref, *refs):
    pieces = len(PIECES)
    k_refs, la_refs = refs[:pieces], refs[pieces : 2 * pieces]
    send_ref, u_ref, fb_ref, et_ref, tot_ref, w_ref, col_ref = refs[2 * pieces :]
    am, bm = unpack(part, fb_ref, et_ref)
    tot = jnp.sqrt(total_of(am + sums_ref[:8, :]) * total_of(bm + sums_ref[8:, :]))
    tot_ref[...] = jnp.broadcast_to(tot, tot_ref.shape)
    spread(w_ref, jnp.where(fb_ref[...] > ABSENT, et_ref[...], 0.0), True)
    finish(plan, hit_ref, None, acc_ref, w_ref, k_refs, la_refs, send_ref, u_ref, col_ref)


def next_own(plan, sums, fb_ref, et_ref, *refs):
    k_refs, (acc_ref, mass_ref, w_ref) = refs[:-3], refs[-3:]
    t, mass = half_scale(sums, fb_ref, et_ref)
    mass_ref[...] = jnp.broadcast_to(mass, mass_ref.shape)
    spread(w_ref, t * et_ref[...], False)
    add_rows(plan, own_span(plan), w_ref, k_refs, keep_rows(acc_ref))


def next_other(plan, hit_ref, sums, fb_ref, et_ref, tot_ref, mass_ref, acc_ref, *refs):
    pieces = len(PIECES)
    k_refs, la_refs = refs[:pieces], refs[pieces : 2 * pieces]
    send_ref, u_ref, w_ref, col_ref = refs[2 * pieces :]
    t, mass = half_scale(sums, fb_ref, et_ref)
    mass = jnp.sum(mass + mass_ref[0:1, :], axis=1, keepdims=True)
    factor = jnp.sqrt(tot_ref[0:1, 0:1] / mass)
    spread(w_ref, t * et_ref[...], True)
    finish(plan, hit_ref, factor, acc_ref, w_ref, k_refs, la_refs, send_ref, u_ref, col_ref)


def own_columns(plan, hit_ref, u_ref, *refs):
    k_refs, (keep_ref, col_ref) = refs[:-2], refs[-2:]
    hit = hit_ref[: keep_ref.shape[0], :]
    keep_ref[...] = add_columns(plan, own_span(plan), u_ref, k_refs, hit, col_ref)


def last_kernel(keep, other, fb0, et0, fb1, et1, tot_ref, u_ref, src_ref, tgt_ref, t_ref):
    local, block = src_ref.shape
    t, mass = half_scale(keep, fb0, et0)
    t_ref[...] = t
    mass += half_scale(other, fb1, et1)[1]
    factor = jnp.sqrt(tot_ref[0:1, 0:1] / jnp.sum(mass, axis=1, keepdims=True))
    own = pl.multiple_of((position() >> 1) * local, local)
    tgt_ref[...] = t_ref[pl.ds(own, local), :] * factor
    mask = diag_mask(block)
    for s in range(local):
        src_ref[s : s + 1, :] = to_row(u_ref[s * block : (s + 1) * block, :] * factor, mask)


def call(kernel, ins, outs, scratch=(), smem=0, hbm=(), vmem_mb=12, **cost):
    specs = [pl.BlockSpec(memory_space=SMEM)] * smem
    for at in range(smem, len(ins)):
        specs.append(pl.BlockSpec(memory_space=pl.ANY if at in hbm else VMEM))
    ins = [
        pltpu.with_memory_space_constraint(x, pltpu.HBM) if at in hbm else x
        for at, x in enumerate(ins)
    ]
    return pl.pallas_call(
        kernel,
        out_shape=outs,
        in_specs=specs,
        out_specs=[
            pl.BlockSpec(memory_space=SMEM if out.dtype == jnp.int32 else VMEM) for out in outs
        ],
        scratch_shapes=scratch,
        compiler_params=pltpu.CompilerParams(vmem_limit_bytes=vmem_mb << 20),
        cost_estimate=pl.CostEstimate(**cost) if cost else None,
    )(*ins)


def distances(n):
    return [d | 1 for d in (n >> r for r in range(1, n.bit_length()))]


def exchange(x, n, d):
    return lax.ppermute(x, "src", [(i, i ^ d) for i in range(n)])


def shards(
    src_feat, tile_feat, tile_tgt, tile_live, src_lin, tgt_lin, src_mass, tgt_mass, tgt_count
):
    f32 = jnp.float32
    local, slots, block, width = tile_feat.shape
    n = lax.axis_size("src")
    every = local * n
    pairs = local * slots
    lin = src_lin.reshape(local, block)
    amass = src_mass.reshape(local, block)
    def shape(rows, cols=block, dtype=f32):
        return pltpu.VMEM((rows, cols), dtype)

    (part,) = call(
        pack_kernel,
        (tgt_count, tgt_mass.reshape(local, block), tgt_lin.reshape(local, block), amass),
        (shape(3 * local),),
        scratch=[SMEM((local,), jnp.int32), pltpu.SemaphoreType.DMA((4,))],
        hbm=(0, 1, 2, 3),
    )
    def feats(size):
        return pltpu.VMEM((size, slots, block, width), tile_feat.dtype)

    order = distances(n)
    kern, la = [], []
    following = None
    for at, d in enumerate(order):
        got = exchange(part, n, d)
        if at < len(PIECES):
            size = PIECES[at]
            ahead = [feats(PIECES[at + 1])] if at + 1 < len(PIECES) else []
            outs = (shape(size * slots * block), shape(size * block), *ahead)
            cost = dict(
                flops=2 * size * slots * block * block * width,
                bytes_accessed=2 * size * slots * block * width,
                transcendentals=size * slots * block * block,
            )
        if at == 0:
            k0, la0, following, plan, hit, xv, linv, massv = call(
                first_build,
                (tile_live, tile_tgt, src_feat, lin, amass, tile_feat),
                (
                    *outs,
                    SMEM((2 * local + 3, slots + 2 * STEP), jnp.int32),
                    shape(every, pairs, jnp.bfloat16),
                    shape(local * block, width, src_feat.dtype),
                    shape(local),
                    shape(local),
                ),
                scratch=[
                    SMEM((local,), jnp.int32),
                    SMEM((local, slots), jnp.int32),
                    VMEM((pairs, every), f32),
                    feats(size),
                    pltpu.SemaphoreType.DMA((6 + size,)),
                ],
                hbm=(0, 1, 2, 3, 4, 5),
                **cost,
            )
        elif at < len(PIECES):
            k0, la0, *following = call(
                functools.partial(later_build, sum(PIECES[:at])),
                (plan, xv, linv, massv, following, tile_feat),
                outs,
                scratch=[pltpu.SemaphoreType.DMA] if ahead else [],
                smem=1,
                hbm=(5,),
                **cost,
            )
            following = following[0] if following else None
        if at < len(PIECES):
            kern.append(k0)
            la.append(la0)
        if at < len(order) - 1:
            part = jnp.stack([part, got], axis=0).reshape(-1, block)
            if at < len(PIECES) - 1:
                part, following, kern[-1] = lax.optimization_barrier((part, following, kern[-1]))
    half = every // 2
    tall = shape(local * block)
    w = VMEM((every + 8, block), f32)
    col = VMEM((pairs, block), f32)
    acc, fb0, et0, sums = call(
        first_own,
        (plan, part, *kern),
        (tall, shape(half), shape(half), shape(16)),
        scratch=[w],
        smem=1,
    )
    send, u, fb1, et1, tot = call(
        first_other,
        (plan, hit, got, sums, acc, *kern, *la),
        (shape(half), tall, shape(half), shape(half), shape(8)),
        scratch=[w, col],
        smem=1,
    )
    for iteration in range(ITERS):
        got = exchange(send, n, order[-1])
        (keep,) = call(
            own_columns, (plan, hit, u, *kern), (shape(half),), scratch=[col], smem=1
        )
        keep = keep + got
        for d in order[-2::-1]:
            keep = keep + exchange(keep, n, d)
        other = exchange(keep, n, order[-1])
        if iteration < ITERS - 1:
            acc, mass = call(
                next_own, (plan, keep, fb0, et0, *kern), (tall, shape(8)), scratch=[w], smem=1
            )
            send, u = call(
                next_other,
                (plan, hit, other, fb1, et1, tot, mass, acc, *kern, *la),
                (shape(half), tall),
                scratch=[w, col],
                smem=1,
            )
    src, tgt = call(
        last_kernel,
        (keep, other, fb0, et0, fb1, et1, tot, u),
        [jax.ShapeDtypeStruct((local, block), f32)] * 2,
        scratch=[VMEM((half, block), f32)],
    )
    return (src.reshape(-1), tgt.reshape(-1))


def solution(mesh):
    split = P(("pairs", "src"))
    rows = P(("pairs", "src"), None)
    in_specs = (rows, P(("pairs", "src"), None, None, None), rows) + (split,) * 6
    return jax.shard_map(
        shards, mesh=mesh, in_specs=in_specs, out_specs=(split, split), check_vma=False
    )
```

```python
import functools

import jax
import jax.numpy as jnp
from jax import lax
from jax.experimental import pallas as pl
from jax.experimental.pallas import tpu as pltpu
from jax.sharding import PartitionSpec as P

ITERS = 3
EPS = 0.1
RHO = 1.0
ALPHA = 0.5
F = RHO / (RHO + EPS)
LOG2E = 1.4426950408889634
STEP = 4
ABSENT = -1e30
PIECES = (2, 3, 3)

VMEM = pltpu.VMEM
SMEM = pltpu.SMEM
NT = (((1,), (1,)), ((), ()))


def diag_mask(block):
    return lax.broadcasted_iota(jnp.int32, (block, block), 0) == lax.broadcasted_iota(
        jnp.int32, (block, block), 1
    )


def to_column(row, mask):
    return jnp.sum(jnp.where(mask, row, 0.0), axis=1, keepdims=True)


def to_row(column, mask):
    return jnp.sum(jnp.where(mask, column, 0.0), axis=0, keepdims=True)


def position():
    return lax.axis_index("src").astype(jnp.int32)


def parity(x):
    for r in (4, 2, 1):
        x = x ^ (x >> r)
    return x & 1


def place_of(block, local, half, me):
    owner = block >> (local.bit_length() - 1)
    return parity(owner ^ me) * half + (owner >> 1) * local + (block & (local - 1))


def total_of(x):
    return jnp.sum(jnp.sum(x, axis=0, keepdims=True), axis=1, keepdims=True)


def pack_kernel(count_hbm, mass_hbm, lin_hbm, amass_hbm, out_ref, count, sems):
    local, block = mass_hbm.shape
    copies = [(count_hbm, count)]
    for i, x in enumerate((mass_hbm, lin_hbm, amass_hbm)):
        copies.append((x, out_ref.at[pl.ds(i * local, local)]))
    copies = [pltpu.make_async_copy(f, t, sems.at[i]) for i, (f, t) in enumerate(copies)]
    for c in copies:
        c.start()
    for c in copies:
        c.wait()
    lane = lax.broadcasted_iota(jnp.int32, (1, block), 1)
    for i in range(local):
        row = slice(i, i + 1)
        out_ref[row, :] = jnp.where(lane < count[i], out_ref[row, :], 0.0)


def build_tiles(plan, first, x_ref, lin_ref, mass_ref, feat, waits, k_ref, la_ref):
    blocks, slots, block, width = feat.shape
    scale = LOG2E / (width * EPS)
    mask = diag_mask(block)
    for s in range(blocks):
        at = first + s
        x = x_ref[at * block : (at + 1) * block, :]
        x32 = x.astype(jnp.float32)
        sq = jnp.sum(x32 * x32, axis=1, keepdims=True)
        lin = to_column(lin_ref[at : at + 1, :], mask)
        base = (2.0 - sq / width - ALPHA * lin) * (LOG2E / EPS)
        base = jnp.broadcast_to(base, (block, block))
        la = F * jnp.log(to_column(mass_ref[at : at + 1, :], mask))
        la_ref[s * block : (s + 1) * block, :] = jnp.broadcast_to(la, (block, block))
        if waits:
            waits[s].wait()

        def tiles(p, _):
            y = [feat[s, plan[at, p * STEP + q]] for q in range(STEP)]
            y = jnp.concatenate(y, axis=0)
            y32 = y.astype(jnp.float32)
            y2 = y32 * y32
            ysq = jnp.sum(y2[:, : width // 2] + y2[:, width // 2 :], axis=1, keepdims=True)
            cross = lax.dot_general(x, y, NT, preferred_element_type=jnp.float32)
            for q in range(STEP):
                cols = slice(q * block, (q + 1) * block)
                row = to_row(ysq[cols, :], mask)
                e = (2.0 * scale) * cross[:, cols] + (base - row * scale)
                start = pl.multiple_of((s * slots + p * STEP + q) * block, block)
                k_ref[pl.ds(start, block), :] = jnp.exp2(e)
            return 0

        lax.fori_loop(0, plan[at, slots + STEP], tiles, 0)


def first_build(live_hbm, tgt_hbm, x_hbm, lin_hbm, mass_hbm, feat, *refs):
    k_ref, la_ref, next_ref, plan_ref, hit_ref, x_ref, lin_ref, mass_ref = refs[:8]
    live, tgt, order_ref, own, sems = refs[8:]
    size = own.shape[0]
    copies = [(live_hbm, live), (tgt_hbm, tgt), (x_hbm, x_ref), (lin_hbm, lin_ref), (mass_hbm, mass_ref)]
    copies += [(feat.at[s], own.at[s]) for s in range(size)]
    copies += [(feat.at[pl.ds(size, next_ref.shape[0])], next_ref)]
    copies = [pltpu.make_async_copy(f, t, sems.at[i]) for i, (f, t) in enumerate(copies)]
    for c in copies:
        c.start()
    for c in copies[:5]:
        c.wait()
    every = hit_ref.shape[0]
    local, slots = tgt.shape
    rows = place_of(tgt[...], local, every // 2, position())
    sub = lax.broadcasted_iota(jnp.int32, (local, slots), 0)
    lives = jnp.zeros((local, slots), jnp.int32)
    for s in range(local):
        lives = jnp.where(sub == s, live[s], lives)
    slot = lax.broadcasted_iota(jnp.int32, (local, slots), 1)
    key = jnp.where(slot < lives, jnp.where(rows < every // 2, 0, slots), 2 * slots) + slot
    rank = jnp.zeros((local, slots), jnp.int32)
    for k in range(slots):
        rank += jnp.where(key[:, k : k + 1] < key, 1, 0)
    lanes = plan_ref.shape[1]
    at = lax.broadcasted_iota(jnp.int32, (local, lanes), 1)
    wide_sub = lax.broadcasted_iota(jnp.int32, (local, lanes), 0)
    lives = jnp.zeros((local, lanes), jnp.int32)
    for s in range(local):
        lives = jnp.where(wide_sub == s, live[s], lives)
    slot_at = jnp.zeros((local, lanes), jnp.int32)
    row_at = jnp.zeros((local, lanes), jnp.int32)
    own_count = jnp.zeros((local, lanes), jnp.int32)
    for k in range(slots):
        here = rank[:, k : k + 1] == at
        slot_at = jnp.where(here, k, slot_at)
        row_at = jnp.where(here, rows[:, k : k + 1], row_at)
        own_count += jnp.where(key[:, k : k + 1] < slots, 1, 0)
    slot_at = jnp.where(at < lives, slot_at, 0)
    row_at = jnp.where(at < lives, row_at, every)
    shift = STEP.bit_length() - 1
    counts = ((lives + (STEP - 1)) >> shift, (own_count + (STEP - 1)) >> shift, own_count >> shift)
    for i, c in enumerate(counts):
        slot_at = jnp.where(at == slots + STEP + i, c, slot_at)
    order_ref[:local, :] = slot_at
    order_ref[local:, :] = row_at
    to_smem = pltpu.make_async_copy(order_ref, plan_ref, sems.at[len(copies)])
    to_smem.start()
    index = jnp.concatenate([row_at[s : s + 1, :slots] for s in range(local)], axis=1)
    rows = lax.broadcasted_iota(jnp.int32, hit_ref.shape, 0)
    hit_ref[...] = jnp.where(rows == index, 1.0, 0.0).astype(jnp.bfloat16)
    to_smem.wait()
    build_tiles(plan_ref, 0, x_ref, lin_ref, mass_ref, own, copies[5:-1], k_ref, la_ref)
    copies[-1].wait()


def later_build(first, plan, x_ref, lin_ref, mass_ref, own, feat, k_ref, la_ref, *rest):
    copy = None
    if rest:
        next_ref, sem = rest
        copy = pltpu.make_async_copy(
            feat.at[pl.ds(first + own.shape[0], next_ref.shape[0])], next_ref, sem
        )
        copy.start()
    build_tiles(plan, first, x_ref, lin_ref, mass_ref, own, (), k_ref, la_ref)
    if copy:
        copy.wait()


def place(s):
    piece = 0
    while s >= PIECES[piece]:
        s -= PIECES[piece]
        piece += 1
    return piece, s


def add_rows(plan, span, w_ref, k_refs, done):
    blocks, block = plan.shape[0] // 2, w_ref.shape[1]
    slots = plan.shape[1] - 2 * STEP
    for s in range(blocks):
        piece, at = place(s)
        k_ref, base = k_refs[piece], at * slots

        def add_row(p, acc):
            for q in range(STEP):
                k = p * STEP + q
                start = pl.multiple_of((base + k) * block, block)
                w = w_ref[pl.ds(plan[blocks + s, k], 1), :]
                acc = acc + k_ref[pl.ds(start, block), :] * w
            return acc

        first, last = span(s)
        done(s, lax.fori_loop(first, last, add_row, jnp.zeros((block, block), jnp.float32)))


def add_columns(plan, span, u_ref, k_refs, hit, col_ref):
    blocks, block = plan.shape[0] // 2, col_ref.shape[1]
    slots = plan.shape[1] - 2 * STEP
    col_ref[...] = jnp.zeros_like(col_ref)
    for s in range(blocks):
        piece, at = place(s)
        k_ref, base = k_refs[piece], at * slots
        u = u_ref[s * block : (s + 1) * block, :]

        def add_col(p, _):
            for q in range(STEP):
                k = p * STEP + q
                start = pl.multiple_of((base + k) * block, block)
                col_ref[pl.ds(s * slots + k, 1), :] = jnp.sum(
                    k_ref[pl.ds(start, block), :] * u, axis=0, keepdims=True
                )
            return 0

        first, last = span(s)
        lax.fori_loop(first, last, add_col, 0)
    col = col_ref[...]
    dense = jnp.zeros((hit.shape[0], block), jnp.float32)
    for _ in range(2):
        term = col.astype(jnp.bfloat16)
        dense += jnp.dot(hit, term, preferred_element_type=jnp.float32)
        col = col - term.astype(jnp.float32)
    return dense


def own_span(plan):
    at = plan.shape[1] - STEP
    return lambda s: (0, plan[s, at + 1])


def other_span(plan):
    at = plan.shape[1] - STEP
    return lambda s: (plan[s, at + 2], plan[s, at])


def spread(w_ref, w, other):
    half = w.shape[0]
    zeros = jnp.zeros((half, w.shape[1]), jnp.float32)
    w_ref[:half, :] = zeros if other else w
    w_ref[half : 2 * half, :] = w if other else zeros
    w_ref[2 * half :, :] = zeros[:8, :]


def unpack(part, fb_ref, et_ref):
    half, block = fb_ref.shape
    n = lax.axis_size("src")
    local = 2 * half // n
    order = distances(n)
    am = jnp.zeros((local, block), jnp.float32)
    bm = am
    for at in range(n // 2):
        m = functools.reduce(lambda p, q: p ^ q, [d for r, d in enumerate(order) if at >> r & 1], 0)
        rows = pl.ds(pl.multiple_of(((position() ^ m) >> 1) * local, local), local)
        at = at * 3 * local
        b = part[at : at + local, :]
        fb_ref[rows, :] = jnp.where(b > 0.0, F * jnp.log(b), ABSENT)
        et_ref[rows, :] = jnp.exp((-ALPHA / EPS) * part[at + local : at + 2 * local, :])
        bm += b
        am += part[at + 2 * local : at + 3 * local, :]
    return am, bm


def half_scale(sums, fb_ref, et_ref):
    fb = fb_ref[...]
    col = sums[...] * et_ref[...]
    t = jnp.where(fb > ABSENT, jnp.exp(fb - F * jnp.log(col)), 0.0)
    return t, jnp.sum(t * col, axis=0, keepdims=True)


def finish(plan, hit_ref, shift, acc_ref, w_ref, k_refs, la_refs, send_ref, u_ref, col_ref, sum_ref):
    block = w_ref.shape[1]
    add_rows(plan, other_span(plan), w_ref, k_refs, keep_rows(sum_ref))
    for s in range(plan.shape[0] // 2):
        rows = pl.ds(s * block, block)
        total = jnp.sum(sum_ref[rows, :] + acc_ref[rows, :], axis=1, keepdims=True)
        piece, at = place(s)
        la = la_refs[piece][pl.ds(at * block, block), :]
        u_ref[rows, :] = jnp.exp((la - shift) - F * jnp.log(total))
    hit = hit_ref[send_ref.shape[0] :, :]
    send_ref[...] = add_columns(plan, other_span(plan), u_ref, k_refs, hit, col_ref)


def keep_rows(acc_ref):
    block = acc_ref.shape[1]

    def keep(s, acc):
        acc_ref[s * block : (s + 1) * block, :] = acc

    return keep


def first_own(plan, part, *refs):
    k_refs, (acc_ref, fb_ref, et_ref, sums_ref, w_ref) = refs[:-5], refs[-5:]
    am, bm = unpack(part, fb_ref, et_ref)
    sums_ref[:8, :], sums_ref[8:, :] = am, bm
    spread(w_ref, jnp.where(fb_ref[...] > ABSENT, et_ref[...], 0.0), False)
    add_rows(plan, own_span(plan), w_ref, k_refs, keep_rows(acc_ref))


def first_other(plan, hit_ref, part, sums_ref, acc_ref, *refs):
    pieces = len(PIECES)
    k_refs, la_refs = refs[:pieces], refs[pieces : 2 * pieces]
    send_ref, u_ref, fb_ref, et_ref, tot_ref, w_ref, col_ref, sum_ref = refs[2 * pieces :]
    am, bm = unpack(part, fb_ref, et_ref)
    tot = jnp.sqrt(total_of(am + sums_ref[:8, :]) * total_of(bm + sums_ref[8:, :]))
    tot_ref[...] = jnp.broadcast_to(tot, tot_ref.shape)
    spread(w_ref, jnp.where(fb_ref[...] > ABSENT, et_ref[...], 0.0), True)
    finish(
        plan, hit_ref, 0.0, acc_ref, w_ref, k_refs, la_refs, send_ref, u_ref, col_ref, sum_ref
    )


def next_own(plan, sums, fb_ref, et_ref, *refs):
    k_refs, (acc_ref, mass_ref, w_ref) = refs[:-3], refs[-3:]
    t, mass = half_scale(sums, fb_ref, et_ref)
    mass_ref[...] = jnp.broadcast_to(mass, mass_ref.shape)
    spread(w_ref, t * et_ref[...], False)
    add_rows(plan, own_span(plan), w_ref, k_refs, keep_rows(acc_ref))


def next_other(plan, hit_ref, sums, fb_ref, et_ref, tot_ref, mass_ref, acc_ref, *refs):
    pieces = len(PIECES)
    k_refs, la_refs = refs[:pieces], refs[pieces : 2 * pieces]
    send_ref, u_ref, w_ref, col_ref, sum_ref = refs[2 * pieces :]
    t, mass = half_scale(sums, fb_ref, et_ref)
    spread(w_ref, t * et_ref[...], True)
    mass = jnp.sum(mass + mass_ref[0:1, :], axis=1, keepdims=True)
    mass = jnp.broadcast_to(mass, (1, w_ref.shape[1]))
    shift = (F / 2) * (jnp.log(tot_ref[0:1, :]) - jnp.log(mass))
    finish(
        plan, hit_ref, shift, acc_ref, w_ref, k_refs, la_refs, send_ref, u_ref, col_ref, sum_ref
    )


def own_columns(plan, hit_ref, u_ref, *refs):
    k_refs, (keep_ref, col_ref) = refs[:-2], refs[-2:]
    hit = hit_ref[: keep_ref.shape[0], :]
    keep_ref[...] = add_columns(plan, own_span(plan), u_ref, k_refs, hit, col_ref)


def last_kernel(keep, other, fb0, et0, fb1, et1, tot_ref, u_ref, src_ref, tgt_ref, t_ref):
    local, block = src_ref.shape
    t, mass = half_scale(keep, fb0, et0)
    t_ref[...] = t
    mass += half_scale(other, fb1, et1)[1]
    factor = jnp.sqrt(tot_ref[0:1, 0:1] / jnp.sum(mass, axis=1, keepdims=True))
    own = pl.multiple_of((position() >> 1) * local, local)
    tgt_ref[...] = t_ref[pl.ds(own, local), :] * factor
    mask = diag_mask(block)
    for s in range(local):
        src_ref[s : s + 1, :] = to_row(u_ref[s * block : (s + 1) * block, :] * factor, mask)


def call(kernel, ins, outs, scratch=(), smem=0, hbm=(), vmem_mb=12, **cost):
    specs = [pl.BlockSpec(memory_space=SMEM)] * smem
    for at in range(smem, len(ins)):
        specs.append(pl.BlockSpec(memory_space=pl.ANY if at in hbm else VMEM))
    ins = [
        pltpu.with_memory_space_constraint(x, pltpu.HBM) if at in hbm else x
        for at, x in enumerate(ins)
    ]
    return pl.pallas_call(
        kernel,
        out_shape=outs,
        in_specs=specs,
        out_specs=[
            pl.BlockSpec(memory_space=SMEM if out.dtype == jnp.int32 else VMEM) for out in outs
        ],
        scratch_shapes=scratch,
        compiler_params=pltpu.CompilerParams(vmem_limit_bytes=vmem_mb << 20),
        cost_estimate=pl.CostEstimate(**cost) if cost else None,
    )(*ins)


def distances(n):
    return [d | 1 for d in (n >> r for r in range(1, n.bit_length()))]


def exchange(x, n, d):
    return lax.ppermute(x, "src", [(i, i ^ d) for i in range(n)])


def shards(
    src_feat, tile_feat, tile_tgt, tile_live, src_lin, tgt_lin, src_mass, tgt_mass, tgt_count
):
    f32 = jnp.float32
    local, slots, block, width = tile_feat.shape
    n = lax.axis_size("src")
    every = local * n
    pairs = local * slots
    lin = src_lin.reshape(local, block)
    amass = src_mass.reshape(local, block)
    def shape(rows, cols=block, dtype=f32):
        return pltpu.VMEM((rows, cols), dtype)

    (part,) = call(
        pack_kernel,
        (tgt_count, tgt_mass.reshape(local, block), tgt_lin.reshape(local, block), amass),
        (shape(3 * local),),
        scratch=[SMEM((local,), jnp.int32), pltpu.SemaphoreType.DMA((4,))],
        hbm=(0, 1, 2, 3),
    )
    def feats(size):
        return pltpu.VMEM((size, slots, block, width), tile_feat.dtype)

    order = distances(n)
    kern, la = [], []
    following = None
    for at, d in enumerate(order):
        got = exchange(part, n, d)
        if at < len(PIECES):
            size = PIECES[at]
            ahead = [feats(PIECES[at + 1])] if at + 1 < len(PIECES) else []
            outs = (shape(size * slots * block), shape(size * block), *ahead)
            cost = dict(
                flops=2 * size * slots * block * block * width,
                bytes_accessed=2 * size * slots * block * width,
                transcendentals=size * slots * block * block,
            )
        if at == 0:
            k0, la0, following, plan, hit, xv, linv, massv = call(
                first_build,
                (tile_live, tile_tgt, src_feat, lin, amass, tile_feat),
                (
                    *outs,
                    SMEM((2 * local, slots + 2 * STEP), jnp.int32),
                    shape(every, pairs, jnp.bfloat16),
                    shape(local * block, width, src_feat.dtype),
                    shape(local),
                    shape(local),
                ),
                scratch=[
                    SMEM((local,), jnp.int32),
                    VMEM((local, slots), jnp.int32),
                    VMEM((2 * local, slots + 2 * STEP), jnp.int32),
                    feats(size),
                    pltpu.SemaphoreType.DMA((7 + size,)),
                ],
                hbm=(0, 1, 2, 3, 4, 5),
                **cost,
            )
        elif at < len(PIECES):
            k0, la0, *following = call(
                functools.partial(later_build, sum(PIECES[:at])),
                (plan, xv, linv, massv, following, tile_feat),
                outs,
                scratch=[pltpu.SemaphoreType.DMA] if ahead else [],
                smem=1,
                hbm=(5,),
                **cost,
            )
            following = following[0] if following else None
        if at < len(PIECES):
            kern.append(k0)
            la.append(la0)
        if at < len(order) - 1:
            part = jnp.stack([part, got], axis=0).reshape(-1, block)
            if at < len(PIECES) - 1:
                part, following, kern[-1] = lax.optimization_barrier((part, following, kern[-1]))
            elif at < len(PIECES):
                part, kern[-1] = lax.optimization_barrier((part, kern[-1]))
    half = every // 2
    tall = shape(local * block)
    w = VMEM((every + 8, block), f32)
    col = VMEM((pairs, block), f32)
    acc, fb0, et0, sums = call(
        first_own,
        (plan, part, *kern),
        (tall, shape(half), shape(half), shape(16)),
        scratch=[w],
        smem=1,
    )
    send, u, fb1, et1, tot = call(
        first_other,
        (plan, hit, got, sums, acc, *kern, *la),
        (shape(half), tall, shape(half), shape(half), shape(8)),
        scratch=[w, col, VMEM((local * block, block), f32)],
        smem=1,
    )
    for iteration in range(ITERS):
        got = exchange(send, n, order[-1])
        (keep,) = call(
            own_columns, (plan, hit, u, *kern), (shape(half),), scratch=[col], smem=1
        )
        keep = keep + got
        for d in order[-2::-1]:
            keep = keep + exchange(keep, n, d)
        other = exchange(keep, n, order[-1])
        if iteration < ITERS - 1:
            acc, mass = call(
                next_own, (plan, keep, fb0, et0, *kern), (tall, shape(8)), scratch=[w], smem=1
            )
            send, u = call(
                next_other,
                (plan, hit, other, fb1, et1, tot, mass, acc, *kern, *la),
                (shape(half), tall),
                scratch=[w, col, VMEM((local * block, block), f32)],
                smem=1,
            )
    src, tgt = call(
        last_kernel,
        (keep, other, fb0, et0, fb1, et1, tot, u),
        [jax.ShapeDtypeStruct((local, block), f32)] * 2,
        scratch=[VMEM((half, block), f32)],
    )
    return (src.reshape(-1), tgt.reshape(-1))


def solution(mesh):
    split = P(("pairs", "src"))
    rows = P(("pairs", "src"), None)
    in_specs = (rows, P(("pairs", "src"), None, None, None), rows) + (split,) * 6
    return jax.shard_map(
        shards, mesh=mesh, in_specs=in_specs, out_specs=(split, split), check_vma=False
    )
```

```python
import functools

import jax
import jax.numpy as jnp
from jax import lax
from jax.experimental import pallas as pl
from jax.experimental.pallas import tpu as pltpu
from jax.sharding import PartitionSpec as P

ITERS = 3
EPS = 0.1
RHO = 1.0
ALPHA = 0.5
F = RHO / (RHO + EPS)
LOG2E = 1.4426950408889634
STEP = 4
ABSENT = -1e30
PIECES = (2, 3, 3)

VMEM = pltpu.VMEM
SMEM = pltpu.SMEM
NT = (((1,), (1,)), ((), ()))


def diag_mask(block):
    return lax.broadcasted_iota(jnp.int32, (block, block), 0) == lax.broadcasted_iota(
        jnp.int32, (block, block), 1
    )


def to_column(row, mask):
    return jnp.sum(jnp.where(mask, row, 0.0), axis=1, keepdims=True)


def to_row(column, mask):
    return jnp.sum(jnp.where(mask, column, 0.0), axis=0, keepdims=True)


def position():
    return lax.axis_index("src").astype(jnp.int32)


def parity(x):
    for r in (4, 2, 1):
        x = x ^ (x >> r)
    return x & 1


def place_of(block, local, half, me):
    owner = block >> (local.bit_length() - 1)
    return parity(owner ^ me) * half + (owner >> 1) * local + (block & (local - 1))


def total_of(x):
    return jnp.sum(jnp.sum(x, axis=0, keepdims=True), axis=1, keepdims=True)


def pack_kernel(count_hbm, mass_hbm, lin_hbm, amass_hbm, out_ref, count, sems):
    local, block = mass_hbm.shape
    copies = [(count_hbm, count)]
    for i, x in enumerate((mass_hbm, lin_hbm, amass_hbm)):
        copies.append((x, out_ref.at[pl.ds(i * local, local)]))
    copies = [pltpu.make_async_copy(f, t, sems.at[i]) for i, (f, t) in enumerate(copies)]
    for c in copies:
        c.start()
    for c in copies:
        c.wait()
    lane = lax.broadcasted_iota(jnp.int32, (1, block), 1)
    for i in range(local):
        row = slice(i, i + 1)
        out_ref[row, :] = jnp.where(lane < count[i], out_ref[row, :], 0.0)


def build_tiles(plan, first, x_ref, lin_ref, mass_ref, feat, waits, k_ref, la_ref):
    blocks, slots, block, width = feat.shape
    scale = LOG2E / (width * EPS)
    mask = diag_mask(block)
    for s in range(blocks):
        at = first + s
        x = x_ref[at * block : (at + 1) * block, :]
        x32 = x.astype(jnp.float32)
        sq = jnp.sum(x32 * x32, axis=1, keepdims=True)
        lin = to_column(lin_ref[at : at + 1, :], mask)
        base = (2.0 - sq / width - ALPHA * lin) * (LOG2E / EPS)
        base = jnp.broadcast_to(base, (block, block))
        la = F * jnp.log(to_column(mass_ref[at : at + 1, :], mask))
        la_ref[s * block : (s + 1) * block, :] = jnp.broadcast_to(la, (block, block))
        if waits:
            waits[s].wait()

        def tiles(p, _):
            y = [feat[s, plan[at, p * STEP + q]] for q in range(STEP)]
            y = jnp.concatenate(y, axis=0)
            y32 = y.astype(jnp.float32)
            y2 = y32 * y32
            ysq = jnp.sum(y2[:, : width // 2] + y2[:, width // 2 :], axis=1, keepdims=True)
            cross = lax.dot_general(x, y, NT, preferred_element_type=jnp.float32)
            for q in range(STEP):
                cols = slice(q * block, (q + 1) * block)
                row = to_row(ysq[cols, :], mask)
                e = (2.0 * scale) * cross[:, cols] + (base - row * scale)
                start = pl.multiple_of((s * slots + p * STEP + q) * block, block)
                k_ref[pl.ds(start, block), :] = jnp.exp2(e)
            return 0

        lax.fori_loop(0, plan[at, slots + STEP], tiles, 0)


def first_build(live_hbm, tgt_hbm, x_hbm, lin_hbm, mass_hbm, feat, *refs):
    k_ref, la_ref, next_ref, plan_ref, hit_ref, x_ref, lin_ref, mass_ref = refs[:8]
    live, tgt, order_ref, own, sems = refs[8:]
    size = own.shape[0]
    copies = [(live_hbm, live), (tgt_hbm, tgt), (x_hbm, x_ref), (lin_hbm, lin_ref), (mass_hbm, mass_ref)]
    copies += [(feat.at[s], own.at[s]) for s in range(size)]
    copies += [(feat.at[pl.ds(size, next_ref.shape[0])], next_ref)]
    copies = [pltpu.make_async_copy(f, t, sems.at[i]) for i, (f, t) in enumerate(copies)]
    for c in copies:
        c.start()
    for c in copies[:5]:
        c.wait()
    every = hit_ref.shape[0]
    local, slots = tgt.shape
    rows = place_of(tgt[...], local, every // 2, position())
    sub = lax.broadcasted_iota(jnp.int32, (local, slots), 0)
    lives = jnp.zeros((local, slots), jnp.int32)
    for s in range(local):
        lives = jnp.where(sub == s, live[s], lives)
    slot = lax.broadcasted_iota(jnp.int32, (local, slots), 1)
    key = jnp.where(slot < lives, jnp.where(rows < every // 2, 0, slots), 2 * slots) + slot
    rank = jnp.zeros((local, slots), jnp.int32)
    for k in range(slots):
        rank += jnp.where(key[:, k : k + 1] < key, 1, 0)
    lanes = plan_ref.shape[1]
    at = lax.broadcasted_iota(jnp.int32, (local, lanes), 1)
    wide_sub = lax.broadcasted_iota(jnp.int32, (local, lanes), 0)
    lives = jnp.zeros((local, lanes), jnp.int32)
    for s in range(local):
        lives = jnp.where(wide_sub == s, live[s], lives)
    slot_at = jnp.zeros((local, lanes), jnp.int32)
    row_at = jnp.zeros((local, lanes), jnp.int32)
    own_count = jnp.zeros((local, lanes), jnp.int32)
    for k in range(slots):
        here = rank[:, k : k + 1] == at
        slot_at = jnp.where(here, k, slot_at)
        row_at = jnp.where(here, rows[:, k : k + 1], row_at)
        own_count += jnp.where(key[:, k : k + 1] < slots, 1, 0)
    slot_at = jnp.where(at < lives, slot_at, 0)
    row_at = jnp.where(at < lives, row_at, every)
    shift = STEP.bit_length() - 1
    counts = ((lives + (STEP - 1)) >> shift, (own_count + (STEP - 1)) >> shift, own_count >> shift)
    for i, c in enumerate(counts):
        slot_at = jnp.where(at == slots + STEP + i, c, slot_at)
    order_ref[:local, :] = slot_at
    order_ref[local:, :] = row_at
    to_smem = pltpu.make_async_copy(order_ref, plan_ref, sems.at[len(copies)])
    to_smem.start()
    index = jnp.concatenate([row_at[s : s + 1, :slots] for s in range(local)], axis=1)
    rows = lax.broadcasted_iota(jnp.int32, hit_ref.shape, 0)
    hit_ref[...] = jnp.where(rows == index, 1.0, 0.0).astype(jnp.bfloat16)
    to_smem.wait()
    build_tiles(plan_ref, 0, x_ref, lin_ref, mass_ref, own, copies[5:-1], k_ref, la_ref)
    copies[-1].wait()


def later_build(first, plan, x_ref, lin_ref, mass_ref, own, feat, k_ref, la_ref, *rest):
    copy = None
    if rest:
        next_ref, sem = rest
        copy = pltpu.make_async_copy(
            feat.at[pl.ds(first + own.shape[0], next_ref.shape[0])], next_ref, sem
        )
        copy.start()
    build_tiles(plan, first, x_ref, lin_ref, mass_ref, own, (), k_ref, la_ref)
    if copy:
        copy.wait()


def place(s):
    piece = 0
    while s >= PIECES[piece]:
        s -= PIECES[piece]
        piece += 1
    return piece, s


def add_rows(plan, span, w_ref, k_refs, out_ref, from_ref=None):
    blocks, block = plan.shape[0] // 2, w_ref.shape[1]
    slots = plan.shape[1] - 2 * STEP
    for s in range(blocks):
        piece, at = place(s)
        k_ref, base = k_refs[piece], at * slots

        def add_row(p, acc):
            for q in range(STEP):
                k = p * STEP + q
                start = pl.multiple_of((base + k) * block, block)
                w = w_ref[pl.ds(plan[blocks + s, k], 1), :]
                acc = acc + k_ref[pl.ds(start, block), :] * w
            return acc

        first, last = span(s)
        rows = slice(s * block, (s + 1) * block)
        acc = jnp.zeros((block, block), jnp.float32) if from_ref is None else from_ref[rows, :]
        out_ref[rows, :] = lax.fori_loop(first, last, add_row, acc)


def add_columns(plan, span, u_ref, k_refs, hit, col_ref):
    blocks, block = plan.shape[0] // 2, col_ref.shape[1]
    slots = plan.shape[1] - 2 * STEP
    col_ref[...] = jnp.zeros_like(col_ref)
    for s in range(blocks):
        piece, at = place(s)
        k_ref, base = k_refs[piece], at * slots
        u = u_ref[s * block : (s + 1) * block, :]

        def add_col(p, _):
            for q in range(STEP):
                k = p * STEP + q
                start = pl.multiple_of((base + k) * block, block)
                col_ref[pl.ds(s * slots + k, 1), :] = jnp.sum(
                    k_ref[pl.ds(start, block), :] * u, axis=0, keepdims=True
                )
            return 0

        first, last = span(s)
        lax.fori_loop(first, last, add_col, 0)
    col = col_ref[...]
    dense = jnp.zeros((hit.shape[0], block), jnp.float32)
    for _ in range(2):
        term = col.astype(jnp.bfloat16)
        dense += jnp.dot(hit, term, preferred_element_type=jnp.float32)
        col = col - term.astype(jnp.float32)
    return dense


def own_span(plan):
    at = plan.shape[1] - STEP
    return lambda s: (0, plan[s, at + 1])


def other_span(plan):
    at = plan.shape[1] - STEP
    return lambda s: (plan[s, at + 2], plan[s, at])


def spread(w_ref, w, other):
    half = w.shape[0]
    zeros = jnp.zeros((half, w.shape[1]), jnp.float32)
    w_ref[:half, :] = zeros if other else w
    w_ref[half : 2 * half, :] = w if other else zeros
    w_ref[2 * half :, :] = zeros[:8, :]


def unpack(part, fb_ref, et_ref):
    half, block = fb_ref.shape
    n = lax.axis_size("src")
    local = 2 * half // n
    order = distances(n)
    am = jnp.zeros((local, block), jnp.float32)
    bm = am
    for at in range(n // 2):
        m = functools.reduce(lambda p, q: p ^ q, [d for r, d in enumerate(order) if at >> r & 1], 0)
        rows = pl.ds(pl.multiple_of(((position() ^ m) >> 1) * local, local), local)
        at = at * 3 * local
        b = part[at : at + local, :]
        fb_ref[rows, :] = jnp.where(b > 0.0, F * jnp.log(b), ABSENT)
        et_ref[rows, :] = jnp.exp((-ALPHA / EPS) * part[at + local : at + 2 * local, :])
        bm += b
        am += part[at + 2 * local : at + 3 * local, :]
    return am, bm


def half_scale(sums, fb_ref, et_ref):
    fb = fb_ref[...]
    col = sums[...] * et_ref[...]
    t = jnp.where(fb > ABSENT, jnp.exp(fb - F * jnp.log(col)), 0.0)
    return t, jnp.sum(t * col, axis=0, keepdims=True)


def finish(plan, hit_ref, shift, acc_ref, w_ref, k_refs, la_refs, send_ref, u_ref, col_ref, sum_ref):
    block = w_ref.shape[1]
    add_rows(plan, other_span(plan), w_ref, k_refs, sum_ref, acc_ref)
    for s in range(plan.shape[0] // 2):
        rows = pl.ds(s * block, block)
        total = jnp.sum(sum_ref[rows, :], axis=1, keepdims=True)
        piece, at = place(s)
        la = la_refs[piece][pl.ds(at * block, block), :]
        u_ref[rows, :] = jnp.exp((la - shift) - F * jnp.log(total))
    hit = hit_ref[send_ref.shape[0] :, :]
    send_ref[...] = add_columns(plan, other_span(plan), u_ref, k_refs, hit, col_ref)


def first_own(plan, part, *refs):
    k_refs, (acc_ref, fb_ref, et_ref, sums_ref, w_ref) = refs[:-5], refs[-5:]
    am, bm = unpack(part, fb_ref, et_ref)
    sums_ref[:8, :], sums_ref[8:, :] = am, bm
    spread(w_ref, jnp.where(fb_ref[...] > ABSENT, et_ref[...], 0.0), False)
    add_rows(plan, own_span(plan), w_ref, k_refs, acc_ref)


def first_other(plan, hit_ref, part, sums_ref, acc_ref, *refs):
    pieces = len(PIECES)
    k_refs, la_refs = refs[:pieces], refs[pieces : 2 * pieces]
    send_ref, u_ref, fb_ref, et_ref, tot_ref, w_ref, col_ref, sum_ref = refs[2 * pieces :]
    am, bm = unpack(part, fb_ref, et_ref)
    tot = jnp.sqrt(total_of(am + sums_ref[:8, :]) * total_of(bm + sums_ref[8:, :]))
    tot_ref[...] = jnp.broadcast_to(tot, tot_ref.shape)
    spread(w_ref, jnp.where(fb_ref[...] > ABSENT, et_ref[...], 0.0), True)
    finish(
        plan, hit_ref, 0.0, acc_ref, w_ref, k_refs, la_refs, send_ref, u_ref, col_ref, sum_ref
    )


def next_own(plan, sums, fb_ref, et_ref, *refs):
    k_refs, (acc_ref, mass_ref, w_ref) = refs[:-3], refs[-3:]
    t, mass = half_scale(sums, fb_ref, et_ref)
    mass_ref[...] = jnp.broadcast_to(mass, mass_ref.shape)
    spread(w_ref, t * et_ref[...], False)
    add_rows(plan, own_span(plan), w_ref, k_refs, acc_ref)


def next_other(plan, hit_ref, sums, fb_ref, et_ref, tot_ref, mass_ref, acc_ref, *refs):
    pieces = len(PIECES)
    k_refs, la_refs = refs[:pieces], refs[pieces : 2 * pieces]
    send_ref, u_ref, w_ref, col_ref, sum_ref = refs[2 * pieces :]
    t, mass = half_scale(sums, fb_ref, et_ref)
    spread(w_ref, t * et_ref[...], True)
    mass = jnp.sum(mass + mass_ref[0:1, :], axis=1, keepdims=True)
    mass = jnp.broadcast_to(mass, (1, w_ref.shape[1]))
    shift = (F / 2) * (jnp.log(tot_ref[0:1, :]) - jnp.log(mass))
    finish(
        plan, hit_ref, shift, acc_ref, w_ref, k_refs, la_refs, send_ref, u_ref, col_ref, sum_ref
    )


def own_columns(plan, hit_ref, u_ref, *refs):
    k_refs, (keep_ref, col_ref) = refs[:-2], refs[-2:]
    hit = hit_ref[: keep_ref.shape[0], :]
    keep_ref[...] = add_columns(plan, own_span(plan), u_ref, k_refs, hit, col_ref)


def last_own(keep, fb_ref, et_ref, u_ref, src_ref, tgt_ref, mass_ref, t_ref):
    local, block = src_ref.shape
    t, mass = half_scale(keep, fb_ref, et_ref)
    mass_ref[...] = jnp.broadcast_to(mass, mass_ref.shape)
    t_ref[...] = t
    tgt_ref[...] = t_ref[pl.ds(pl.multiple_of((position() >> 1) * local, local), local), :]
    mask = diag_mask(block)
    for s in range(local):
        src_ref[s : s + 1, :] = to_row(u_ref[s * block : (s + 1) * block, :], mask)


def last_other(other, fb_ref, et_ref, tot_ref, mass_ref, src, tgt, src_ref, tgt_ref):
    mass = half_scale(other, fb_ref, et_ref)[1] + mass_ref[0:1, :]
    factor = jnp.sqrt(tot_ref[0:1, 0:1] / jnp.sum(mass, axis=1, keepdims=True))
    src_ref[...] = src[...] * factor
    tgt_ref[...] = tgt[...] * factor


def call(kernel, ins, outs, scratch=(), smem=0, hbm=(), vmem_mb=12, **cost):
    specs = [pl.BlockSpec(memory_space=SMEM)] * smem
    for at in range(smem, len(ins)):
        specs.append(pl.BlockSpec(memory_space=pl.ANY if at in hbm else VMEM))
    ins = [
        pltpu.with_memory_space_constraint(x, pltpu.HBM) if at in hbm else x
        for at, x in enumerate(ins)
    ]
    return pl.pallas_call(
        kernel,
        out_shape=outs,
        in_specs=specs,
        out_specs=[
            pl.BlockSpec(memory_space=SMEM if out.dtype == jnp.int32 else VMEM) for out in outs
        ],
        scratch_shapes=scratch,
        compiler_params=pltpu.CompilerParams(vmem_limit_bytes=vmem_mb << 20),
        cost_estimate=pl.CostEstimate(**cost) if cost else None,
    )(*ins)


def distances(n):
    return [d | 1 for d in (n >> r for r in range(1, n.bit_length()))]


def exchange(x, n, d):
    return lax.ppermute(x, "src", [(i, i ^ d) for i in range(n)])


def shards(
    src_feat, tile_feat, tile_tgt, tile_live, src_lin, tgt_lin, src_mass, tgt_mass, tgt_count
):
    f32 = jnp.float32
    local, slots, block, width = tile_feat.shape
    n = lax.axis_size("src")
    every = local * n
    pairs = local * slots
    lin = src_lin.reshape(local, block)
    amass = src_mass.reshape(local, block)
    def shape(rows, cols=block, dtype=f32):
        return pltpu.VMEM((rows, cols), dtype)

    (part,) = call(
        pack_kernel,
        (tgt_count, tgt_mass.reshape(local, block), tgt_lin.reshape(local, block), amass),
        (shape(3 * local),),
        scratch=[SMEM((local,), jnp.int32), pltpu.SemaphoreType.DMA((4,))],
        hbm=(0, 1, 2, 3),
    )
    def feats(size):
        return pltpu.VMEM((size, slots, block, width), tile_feat.dtype)

    order = distances(n)
    kern, la = [], []
    following = None
    for at, d in enumerate(order):
        got = exchange(part, n, d)
        if at < len(PIECES):
            size = PIECES[at]
            ahead = [feats(PIECES[at + 1])] if at + 1 < len(PIECES) else []
            outs = (shape(size * slots * block), shape(size * block), *ahead)
            cost = dict(
                flops=2 * size * slots * block * block * width,
                bytes_accessed=2 * size * slots * block * width,
                transcendentals=size * slots * block * block,
            )
        if at == 0:
            k0, la0, following, plan, hit, xv, linv, massv = call(
                first_build,
                (tile_live, tile_tgt, src_feat, lin, amass, tile_feat),
                (
                    *outs,
                    SMEM((2 * local, slots + 2 * STEP), jnp.int32),
                    shape(every, pairs, jnp.bfloat16),
                    shape(local * block, width, src_feat.dtype),
                    shape(local),
                    shape(local),
                ),
                scratch=[
                    SMEM((local,), jnp.int32),
                    VMEM((local, slots), jnp.int32),
                    VMEM((2 * local, slots + 2 * STEP), jnp.int32),
                    feats(size),
                    pltpu.SemaphoreType.DMA((7 + size,)),
                ],
                hbm=(0, 1, 2, 3, 4, 5),
                **cost,
            )
        elif at < len(PIECES):
            k0, la0, *following = call(
                functools.partial(later_build, sum(PIECES[:at])),
                (plan, xv, linv, massv, following, tile_feat),
                outs,
                scratch=[pltpu.SemaphoreType.DMA] if ahead else [],
                smem=1,
                hbm=(5,),
                **cost,
            )
            following = following[0] if following else None
        if at < len(PIECES):
            kern.append(k0)
            la.append(la0)
        if at < len(order) - 1:
            part = jnp.stack([part, got], axis=0).reshape(-1, block)
            if at < len(PIECES) - 1:
                part, following, kern[-1] = lax.optimization_barrier((part, following, kern[-1]))
            elif at < len(PIECES):
                part, kern[-1] = lax.optimization_barrier((part, kern[-1]))
    half = every // 2
    tall = shape(local * block)
    w = VMEM((every + 8, block), f32)
    col = VMEM((pairs, block), f32)
    acc, fb0, et0, sums = call(
        first_own,
        (plan, part, *kern),
        (tall, shape(half), shape(half), shape(16)),
        scratch=[w],
        smem=1,
    )
    send, u, fb1, et1, tot = call(
        first_other,
        (plan, hit, got, sums, acc, *kern, *la),
        (shape(half), tall, shape(half), shape(half), shape(8)),
        scratch=[w, col, VMEM((local * block, block), f32)],
        smem=1,
    )
    for iteration in range(ITERS):
        got = exchange(send, n, order[-1])
        (keep,) = call(
            own_columns, (plan, hit, u, *kern), (shape(half),), scratch=[col], smem=1
        )
        keep = keep + got
        for d in order[-2::-1]:
            keep = keep + exchange(keep, n, d)
        other = exchange(keep, n, order[-1])
        if iteration < ITERS - 1:
            acc, mass = call(
                next_own, (plan, keep, fb0, et0, *kern), (tall, shape(8)), scratch=[w], smem=1
            )
            send, u = call(
                next_other,
                (plan, hit, other, fb1, et1, tot, mass, acc, *kern, *la),
                (shape(half), tall),
                scratch=[w, col, VMEM((local * block, block), f32)],
                smem=1,
            )
    src, tgt, mass = call(
        last_own,
        (keep, fb0, et0, u),
        (shape(local), shape(local), shape(8)),
        scratch=[VMEM((half, block), f32)],
    )
    src, tgt = call(
        last_other,
        (other, fb1, et1, tot, mass, src, tgt),
        [jax.ShapeDtypeStruct((local, block), f32)] * 2,
    )
    return (src.reshape(-1), tgt.reshape(-1))


def solution(mesh):
    split = P(("pairs", "src"))
    rows = P(("pairs", "src"), None)
    in_specs = (rows, P(("pairs", "src"), None, None, None), rows) + (split,) * 6
    return jax.shard_map(
        shards, mesh=mesh, in_specs=in_specs, out_specs=(split, split), check_vma=False
    )
```

```python
import functools

import jax
import jax.numpy as jnp
from jax import lax
from jax.experimental import pallas as pl
from jax.experimental.pallas import tpu as pltpu
from jax.sharding import PartitionSpec as P

ITERS = 3
EPS = 0.1
RHO = 1.0
ALPHA = 0.5
F = RHO / (RHO + EPS)
LOG2E = 1.4426950408889634
STEP = 4
ABSENT = -1e30
PIECES = (2, 3, 3)

VMEM = pltpu.VMEM
SMEM = pltpu.SMEM
NT = (((1,), (1,)), ((), ()))


def diag_mask(block):
    return lax.broadcasted_iota(jnp.int32, (block, block), 0) == lax.broadcasted_iota(
        jnp.int32, (block, block), 1
    )


def to_column(row, mask):
    return jnp.sum(jnp.where(mask, row, 0.0), axis=1, keepdims=True)


def to_row(column, mask):
    return jnp.sum(jnp.where(mask, column, 0.0), axis=0, keepdims=True)


def position():
    return lax.axis_index("src").astype(jnp.int32)


def parity(x):
    for r in (4, 2, 1):
        x = x ^ (x >> r)
    return x & 1


def place_of(block, local, half, me):
    owner = block >> (local.bit_length() - 1)
    return parity(owner ^ me) * half + (owner >> 1) * local + (block & (local - 1))


def total_of(x):
    return jnp.sum(jnp.sum(x, axis=0, keepdims=True), axis=1, keepdims=True)


def pack_kernel(count_hbm, mass_hbm, lin_hbm, amass_hbm, out_ref, count, sems):
    local, block = mass_hbm.shape
    copies = [(count_hbm, count)]
    for i, x in enumerate((mass_hbm, lin_hbm, amass_hbm)):
        copies.append((x, out_ref.at[pl.ds(i * local, local)]))
    copies = [pltpu.make_async_copy(f, t, sems.at[i]) for i, (f, t) in enumerate(copies)]
    for c in copies:
        c.start()
    for c in copies:
        c.wait()
    lane = lax.broadcasted_iota(jnp.int32, (1, block), 1)
    for i in range(local):
        row = slice(i, i + 1)
        out_ref[row, :] = jnp.where(lane < count[i], out_ref[row, :], 0.0)


def build_tiles(plan, first, x_ref, lin_ref, mass_ref, feat, waits, k_ref, la_ref):
    blocks, slots, block, width = feat.shape
    scale = LOG2E / (width * EPS)
    mask = diag_mask(block)
    for s in range(blocks):
        at = first + s
        x = x_ref[at * block : (at + 1) * block, :]
        x32 = x.astype(jnp.float32)
        sq = jnp.sum(x32 * x32, axis=1, keepdims=True)
        lin = to_column(lin_ref[at : at + 1, :], mask)
        base = (2.0 - sq / width - ALPHA * lin) * (LOG2E / EPS)
        base = jnp.broadcast_to(base, (block, block))
        la = F * jnp.log(to_column(mass_ref[at : at + 1, :], mask))
        la_ref[s * block : (s + 1) * block, :] = jnp.broadcast_to(la, (block, block))
        if waits:
            waits[s].wait()

        def tiles(p, _):
            y = [feat[s, plan[at, p * STEP + q]] for q in range(STEP)]
            y = jnp.concatenate(y, axis=0)
            y32 = y.astype(jnp.float32)
            y2 = y32 * y32
            ysq = jnp.sum(y2[:, : width // 2] + y2[:, width // 2 :], axis=1, keepdims=True)
            cross = lax.dot_general(x, y, NT, preferred_element_type=jnp.float32)
            for q in range(STEP):
                cols = slice(q * block, (q + 1) * block)
                row = to_row(ysq[cols, :], mask)
                e = (2.0 * scale) * cross[:, cols] + (base - row * scale)
                start = pl.multiple_of((s * (slots + STEP) + p * STEP + q) * block, block)
                k_ref[pl.ds(start, block), :] = jnp.exp2(e)
            return 0

        lax.fori_loop(0, plan[at, slots + STEP], tiles, 0)


def first_build(live_hbm, tgt_hbm, x_hbm, lin_hbm, mass_hbm, feat, *refs):
    k_ref, la_ref, next_ref, plan_ref, hit_ref, x_ref, lin_ref, mass_ref = refs[:8]
    live, tgt, order_ref, own, sems = refs[8:]
    size = own.shape[0]
    copies = [(live_hbm, live), (tgt_hbm, tgt), (x_hbm, x_ref), (lin_hbm, lin_ref), (mass_hbm, mass_ref)]
    copies += [(feat.at[s], own.at[s]) for s in range(size)]
    copies += [(feat.at[pl.ds(size, next_ref.shape[0])], next_ref)]
    copies = [pltpu.make_async_copy(f, t, sems.at[i]) for i, (f, t) in enumerate(copies)]
    for c in copies:
        c.start()
    for c in copies[:5]:
        c.wait()
    every = hit_ref.shape[0]
    local, slots = tgt.shape
    rows = place_of(tgt[...], local, every // 2, position())
    sub = lax.broadcasted_iota(jnp.int32, (local, slots), 0)
    lives = jnp.zeros((local, slots), jnp.int32)
    for s in range(local):
        lives = jnp.where(sub == s, live[s], lives)
    slot = lax.broadcasted_iota(jnp.int32, (local, slots), 1)
    key = jnp.where(slot < lives, jnp.where(rows < every // 2, 0, slots), 2 * slots) + slot
    rank = jnp.zeros((local, slots), jnp.int32)
    own_count = jnp.zeros((local, slots), jnp.int32)
    for k in range(slots):
        rank += jnp.where(key[:, k : k + 1] < key, 1, 0)
        own_count += jnp.where(key[:, k : k + 1] < slots, 1, 0)
    rank += (-own_count) & (STEP - 1)
    lanes = plan_ref.shape[1]
    at = lax.broadcasted_iota(jnp.int32, (local, lanes), 1)
    wide_sub = lax.broadcasted_iota(jnp.int32, (local, lanes), 0)
    lives = jnp.zeros((local, lanes), jnp.int32)
    for s in range(local):
        lives = jnp.where(wide_sub == s, live[s], lives)
    slot_at = jnp.zeros((local, lanes), jnp.int32)
    row_at = jnp.zeros((local, lanes), jnp.int32)
    own_count = jnp.zeros((local, lanes), jnp.int32)
    for k in range(slots):
        here = rank[:, k : k + 1] == at
        slot_at = jnp.where(here, k, slot_at)
        row_at = jnp.where(here, rows[:, k : k + 1], row_at)
        own_count += jnp.where(key[:, k : k + 1] < slots, 1, 0)
    empty = (-own_count) & (STEP - 1)
    used = jnp.logical_and(at >= empty, at < empty + lives)
    slot_at = jnp.where(used, slot_at, 0)
    row_at = jnp.where(used, row_at, every)
    shift = STEP.bit_length() - 1
    counts = ((empty + lives + (STEP - 1)) >> shift, (empty + own_count) >> shift)
    for i, c in enumerate(counts):
        slot_at = jnp.where(at == slots + STEP + i, c, slot_at)
    order_ref[:local, :] = slot_at
    order_ref[local:, :] = row_at
    to_smem = pltpu.make_async_copy(order_ref, plan_ref, sems.at[len(copies)])
    to_smem.start()
    index = jnp.concatenate([row_at[s : s + 1, : slots + STEP] for s in range(local)], axis=1)
    rows = lax.broadcasted_iota(jnp.int32, hit_ref.shape, 0)
    hit_ref[...] = jnp.where(rows == index, 1.0, 0.0).astype(jnp.bfloat16)
    to_smem.wait()
    build_tiles(plan_ref, 0, x_ref, lin_ref, mass_ref, own, copies[5:-1], k_ref, la_ref)
    copies[-1].wait()


def later_build(first, plan, x_ref, lin_ref, mass_ref, own, feat, k_ref, la_ref, *rest):
    copy = None
    if rest:
        next_ref, sem = rest
        copy = pltpu.make_async_copy(
            feat.at[pl.ds(first + own.shape[0], next_ref.shape[0])], next_ref, sem
        )
        copy.start()
    build_tiles(plan, first, x_ref, lin_ref, mass_ref, own, (), k_ref, la_ref)
    if copy:
        copy.wait()


def place(s):
    piece = 0
    while s >= PIECES[piece]:
        s -= PIECES[piece]
        piece += 1
    return piece, s


def add_rows(plan, span, w_ref, k_refs, out_ref, from_ref=None):
    blocks, block = plan.shape[0] // 2, w_ref.shape[1]
    slots = plan.shape[1] - STEP
    for s in range(blocks):
        piece, at = place(s)
        k_ref, base = k_refs[piece], at * slots

        def add_row(p, acc):
            for q in range(STEP):
                k = p * STEP + q
                start = pl.multiple_of((base + k) * block, block)
                w = w_ref[pl.ds(plan[blocks + s, k], 1), :]
                acc = acc + k_ref[pl.ds(start, block), :] * w
            return acc

        first, last = span(s)
        rows = slice(s * block, (s + 1) * block)
        acc = jnp.zeros((block, block), jnp.float32) if from_ref is None else from_ref[rows, :]
        out_ref[rows, :] = lax.fori_loop(first, last, add_row, acc)


def add_columns(plan, span, u_ref, k_refs, hit, col_ref):
    blocks, block = plan.shape[0] // 2, col_ref.shape[1]
    slots = plan.shape[1] - STEP
    col_ref[...] = jnp.zeros_like(col_ref)
    for s in range(blocks):
        piece, at = place(s)
        k_ref, base = k_refs[piece], at * slots
        u = u_ref[s * block : (s + 1) * block, :]

        def add_col(p, _):
            for q in range(STEP):
                k = p * STEP + q
                start = pl.multiple_of((base + k) * block, block)
                col_ref[pl.ds(s * slots + k, 1), :] = jnp.sum(
                    k_ref[pl.ds(start, block), :] * u, axis=0, keepdims=True
                )
            return 0

        first, last = span(s)
        lax.fori_loop(first, last, add_col, 0)
    col = col_ref[...]
    dense = jnp.zeros((hit.shape[0], block), jnp.float32)
    for _ in range(2):
        term = col.astype(jnp.bfloat16)
        dense += jnp.dot(hit, term, preferred_element_type=jnp.float32)
        col = col - term.astype(jnp.float32)
    return dense


def own_span(plan):
    at = plan.shape[1] - STEP
    return lambda s: (0, plan[s, at + 1])


def other_span(plan):
    at = plan.shape[1] - STEP
    return lambda s: (plan[s, at + 1], plan[s, at])


def spread(w_ref, w, other):
    half = w.shape[0]
    zeros = jnp.zeros((half, w.shape[1]), jnp.float32)
    w_ref[:half, :] = zeros if other else w
    w_ref[half : 2 * half, :] = w if other else zeros
    w_ref[2 * half :, :] = zeros[:8, :]


def unpack(part, fb_ref, et_ref):
    half, block = fb_ref.shape
    n = lax.axis_size("src")
    local = 2 * half // n
    order = distances(n)
    am = jnp.zeros((local, block), jnp.float32)
    bm = am
    for at in range(n // 2):
        m = functools.reduce(lambda p, q: p ^ q, [d for r, d in enumerate(order) if at >> r & 1], 0)
        rows = pl.ds(pl.multiple_of(((position() ^ m) >> 1) * local, local), local)
        at = at * 3 * local
        b = part[at : at + local, :]
        fb_ref[rows, :] = jnp.where(b > 0.0, F * jnp.log(b), ABSENT)
        et_ref[rows, :] = jnp.exp((-ALPHA / EPS) * part[at + local : at + 2 * local, :])
        bm += b
        am += part[at + 2 * local : at + 3 * local, :]
    return am, bm


def half_scale(sums, fb_ref, et_ref):
    fb = fb_ref[...]
    col = sums[...] * et_ref[...]
    t = jnp.where(fb > ABSENT, jnp.exp(fb - F * jnp.log(col)), 0.0)
    return t, jnp.sum(t * col, axis=0, keepdims=True)


def finish(plan, hit_ref, shift, acc_ref, w_ref, k_refs, la_refs, send_ref, u_ref, col_ref, sum_ref):
    block = w_ref.shape[1]
    add_rows(plan, other_span(plan), w_ref, k_refs, sum_ref, acc_ref)
    for s in range(plan.shape[0] // 2):
        rows = pl.ds(s * block, block)
        total = jnp.sum(sum_ref[rows, :], axis=1, keepdims=True)
        piece, at = place(s)
        la = la_refs[piece][pl.ds(at * block, block), :]
        u_ref[rows, :] = jnp.exp((la - shift) - F * jnp.log(total))
    hit = hit_ref[send_ref.shape[0] :, :]
    send_ref[...] = add_columns(plan, other_span(plan), u_ref, k_refs, hit, col_ref)


def first_own(plan, part, *refs):
    k_refs, (acc_ref, fb_ref, et_ref, sums_ref, w_ref) = refs[:-5], refs[-5:]
    am, bm = unpack(part, fb_ref, et_ref)
    sums_ref[:8, :], sums_ref[8:, :] = am, bm
    spread(w_ref, jnp.where(fb_ref[...] > ABSENT, et_ref[...], 0.0), False)
    add_rows(plan, own_span(plan), w_ref, k_refs, acc_ref)


def first_other(plan, hit_ref, part, sums_ref, acc_ref, *refs):
    pieces = len(PIECES)
    k_refs, la_refs = refs[:pieces], refs[pieces : 2 * pieces]
    send_ref, u_ref, fb_ref, et_ref, tot_ref, w_ref, col_ref, sum_ref = refs[2 * pieces :]
    am, bm = unpack(part, fb_ref, et_ref)
    tot = jnp.sqrt(total_of(am + sums_ref[:8, :]) * total_of(bm + sums_ref[8:, :]))
    tot_ref[...] = jnp.broadcast_to(tot, tot_ref.shape)
    spread(w_ref, jnp.where(fb_ref[...] > ABSENT, et_ref[...], 0.0), True)
    finish(
        plan, hit_ref, 0.0, acc_ref, w_ref, k_refs, la_refs, send_ref, u_ref, col_ref, sum_ref
    )


def next_own(plan, sums, fb_ref, et_ref, *refs):
    k_refs, (acc_ref, mass_ref, w_ref) = refs[:-3], refs[-3:]
    t, mass = half_scale(sums, fb_ref, et_ref)
    mass_ref[...] = jnp.broadcast_to(mass, mass_ref.shape)
    spread(w_ref, t * et_ref[...], False)
    add_rows(plan, own_span(plan), w_ref, k_refs, acc_ref)


def next_other(plan, hit_ref, sums, fb_ref, et_ref, tot_ref, mass_ref, acc_ref, *refs):
    pieces = len(PIECES)
    k_refs, la_refs = refs[:pieces], refs[pieces : 2 * pieces]
    send_ref, u_ref, w_ref, col_ref, sum_ref = refs[2 * pieces :]
    t, mass = half_scale(sums, fb_ref, et_ref)
    spread(w_ref, t * et_ref[...], True)
    mass = jnp.sum(mass + mass_ref[0:1, :], axis=1, keepdims=True)
    mass = jnp.broadcast_to(mass, (1, w_ref.shape[1]))
    shift = (F / 2) * (jnp.log(tot_ref[0:1, :]) - jnp.log(mass))
    finish(
        plan, hit_ref, shift, acc_ref, w_ref, k_refs, la_refs, send_ref, u_ref, col_ref, sum_ref
    )


def own_columns(plan, hit_ref, u_ref, *refs):
    k_refs, (keep_ref, col_ref) = refs[:-2], refs[-2:]
    hit = hit_ref[: keep_ref.shape[0], :]
    keep_ref[...] = add_columns(plan, own_span(plan), u_ref, k_refs, hit, col_ref)


def last_own(keep, fb_ref, et_ref, u_ref, src_ref, tgt_ref, mass_ref, t_ref):
    local, block = src_ref.shape
    t, mass = half_scale(keep, fb_ref, et_ref)
    mass_ref[...] = jnp.broadcast_to(mass, mass_ref.shape)
    t_ref[...] = t
    tgt_ref[...] = t_ref[pl.ds(pl.multiple_of((position() >> 1) * local, local), local), :]
    mask = diag_mask(block)
    for s in range(local):
        src_ref[s : s + 1, :] = to_row(u_ref[s * block : (s + 1) * block, :], mask)


def last_other(other, fb_ref, et_ref, tot_ref, mass_ref, src, tgt, src_ref, tgt_ref):
    mass = half_scale(other, fb_ref, et_ref)[1] + mass_ref[0:1, :]
    factor = jnp.sqrt(tot_ref[0:1, 0:1] / jnp.sum(mass, axis=1, keepdims=True))
    src_ref[...] = src[...] * factor
    tgt_ref[...] = tgt[...] * factor


def call(kernel, ins, outs, scratch=(), smem=0, hbm=(), vmem_mb=12, **cost):
    specs = [pl.BlockSpec(memory_space=SMEM)] * smem
    for at in range(smem, len(ins)):
        specs.append(pl.BlockSpec(memory_space=pl.ANY if at in hbm else VMEM))
    ins = [
        pltpu.with_memory_space_constraint(x, pltpu.HBM) if at in hbm else x
        for at, x in enumerate(ins)
    ]
    return pl.pallas_call(
        kernel,
        out_shape=outs,
        in_specs=specs,
        out_specs=[
            pl.BlockSpec(memory_space=SMEM if out.dtype == jnp.int32 else VMEM) for out in outs
        ],
        scratch_shapes=scratch,
        compiler_params=pltpu.CompilerParams(vmem_limit_bytes=vmem_mb << 20),
        cost_estimate=pl.CostEstimate(**cost) if cost else None,
    )(*ins)


def distances(n):
    return [d | 1 for d in (n >> r for r in range(1, n.bit_length()))]


def exchange(x, n, d):
    return lax.ppermute(x, "src", [(i, i ^ d) for i in range(n)])


def shards(
    src_feat, tile_feat, tile_tgt, tile_live, src_lin, tgt_lin, src_mass, tgt_mass, tgt_count
):
    f32 = jnp.float32
    local, slots, block, width = tile_feat.shape
    n = lax.axis_size("src")
    every = local * n
    places = slots + STEP
    pairs = local * places
    lin = src_lin.reshape(local, block)
    amass = src_mass.reshape(local, block)
    def shape(rows, cols=block, dtype=f32):
        return pltpu.VMEM((rows, cols), dtype)

    (part,) = call(
        pack_kernel,
        (tgt_count, tgt_mass.reshape(local, block), tgt_lin.reshape(local, block), amass),
        (shape(3 * local),),
        scratch=[SMEM((local,), jnp.int32), pltpu.SemaphoreType.DMA((4,))],
        hbm=(0, 1, 2, 3),
    )
    def feats(size):
        return pltpu.VMEM((size, slots, block, width), tile_feat.dtype)

    order = distances(n)
    kern, la = [], []
    following = None
    for at, d in enumerate(order):
        got = exchange(part, n, d)
        if at < len(PIECES):
            size = PIECES[at]
            ahead = [feats(PIECES[at + 1])] if at + 1 < len(PIECES) else []
            outs = (shape(size * places * block), shape(size * block), *ahead)
            cost = dict(
                flops=2 * size * slots * block * block * width,
                bytes_accessed=2 * size * slots * block * width,
                transcendentals=size * slots * block * block,
            )
        if at == 0:
            k0, la0, following, plan, hit, xv, linv, massv = call(
                first_build,
                (tile_live, tile_tgt, src_feat, lin, amass, tile_feat),
                (
                    *outs,
                    SMEM((2 * local, places + STEP), jnp.int32),
                    shape(every, pairs, jnp.bfloat16),
                    shape(local * block, width, src_feat.dtype),
                    shape(local),
                    shape(local),
                ),
                scratch=[
                    SMEM((local,), jnp.int32),
                    VMEM((local, slots), jnp.int32),
                    VMEM((2 * local, places + STEP), jnp.int32),
                    feats(size),
                    pltpu.SemaphoreType.DMA((7 + size,)),
                ],
                hbm=(0, 1, 2, 3, 4, 5),
                **cost,
            )
        elif at < len(PIECES):
            k0, la0, *following = call(
                functools.partial(later_build, sum(PIECES[:at])),
                (plan, xv, linv, massv, following, tile_feat),
                outs,
                scratch=[pltpu.SemaphoreType.DMA] if ahead else [],
                smem=1,
                hbm=(5,),
                **cost,
            )
            following = following[0] if following else None
        if at < len(PIECES):
            kern.append(k0)
            la.append(la0)
        if at < len(order) - 1:
            part = jnp.stack([part, got], axis=0).reshape(-1, block)
            if at < len(PIECES) - 1:
                part, following, kern[-1] = lax.optimization_barrier((part, following, kern[-1]))
            elif at < len(PIECES):
                part, kern[-1] = lax.optimization_barrier((part, kern[-1]))
    half = every // 2
    tall = shape(local * block)
    w = VMEM((every + 8, block), f32)
    col = VMEM((pairs, block), f32)
    acc, fb0, et0, sums = call(
        first_own,
        (plan, part, *kern),
        (tall, shape(half), shape(half), shape(16)),
        scratch=[w],
        smem=1,
    )
    send, u, fb1, et1, tot = call(
        first_other,
        (plan, hit, got, sums, acc, *kern, *la),
        (shape(half), tall, shape(half), shape(half), shape(8)),
        scratch=[w, col, VMEM((local * block, block), f32)],
        smem=1,
    )
    for iteration in range(ITERS):
        got = exchange(send, n, order[-1])
        (keep,) = call(
            own_columns, (plan, hit, u, *kern), (shape(half),), scratch=[col], smem=1
        )
        keep = keep + got
        for d in order[-2::-1]:
            keep = keep + exchange(keep, n, d)
        other = exchange(keep, n, order[-1])
        if iteration < ITERS - 1:
            acc, mass = call(
                next_own, (plan, keep, fb0, et0, *kern), (tall, shape(8)), scratch=[w], smem=1
            )
            send, u = call(
                next_other,
                (plan, hit, other, fb1, et1, tot, mass, acc, *kern, *la),
                (shape(half), tall),
                scratch=[w, col, VMEM((local * block, block), f32)],
                smem=1,
            )
    src, tgt, mass = call(
        last_own,
        (keep, fb0, et0, u),
        (shape(local), shape(local), shape(8)),
        scratch=[VMEM((half, block), f32)],
    )
    src, tgt = call(
        last_other,
        (other, fb1, et1, tot, mass, src, tgt),
        [jax.ShapeDtypeStruct((local, block), f32)] * 2,
    )
    return (src.reshape(-1), tgt.reshape(-1))


def solution(mesh):
    split = P(("pairs", "src"))
    rows = P(("pairs", "src"), None)
    in_specs = (rows, P(("pairs", "src"), None, None, None), rows) + (split,) * 6
    return jax.shard_map(
        shards, mesh=mesh, in_specs=in_specs, out_specs=(split, split), check_vma=False
    )
```

```python
import functools

import jax
import jax.numpy as jnp
from jax import lax
from jax.experimental import pallas as pl
from jax.experimental.pallas import tpu as pltpu
from jax.sharding import PartitionSpec as P

ITERS = 3
EPS = 0.1
RHO = 1.0
ALPHA = 0.5
F = RHO / (RHO + EPS)
LOG2E = 1.4426950408889634
STEP = 4
ABSENT = -1e30
PIECES = (2, 3, 3)

VMEM = pltpu.VMEM
SMEM = pltpu.SMEM
NT = (((1,), (1,)), ((), ()))


def diag_mask(block):
    return lax.broadcasted_iota(jnp.int32, (block, block), 0) == lax.broadcasted_iota(
        jnp.int32, (block, block), 1
    )


def to_column(row, mask):
    return jnp.sum(jnp.where(mask, row, 0.0), axis=1, keepdims=True)


def to_row(column, mask):
    return jnp.sum(jnp.where(mask, column, 0.0), axis=0, keepdims=True)


def position():
    return lax.axis_index("src").astype(jnp.int32)


def parity(x):
    for r in (4, 2, 1):
        x = x ^ (x >> r)
    return x & 1


def place_of(block, local, half, me):
    owner = block >> (local.bit_length() - 1)
    return parity(owner ^ me) * half + (owner >> 1) * local + (block & (local - 1))


def total_of(x):
    return jnp.sum(jnp.sum(x, axis=0, keepdims=True), axis=1, keepdims=True)


def pack_kernel(count_hbm, mass_hbm, lin_hbm, amass_hbm, out_ref, count, sems):
    local, block = mass_hbm.shape
    copies = [(count_hbm, count)]
    for i, x in enumerate((mass_hbm, lin_hbm, amass_hbm)):
        copies.append((x, out_ref.at[pl.ds(i * local, local)]))
    copies = [pltpu.make_async_copy(f, t, sems.at[i]) for i, (f, t) in enumerate(copies)]
    for c in copies:
        c.start()
    for c in copies:
        c.wait()
    lane = lax.broadcasted_iota(jnp.int32, (1, block), 1)
    for i in range(local):
        row = slice(i, i + 1)
        out_ref[row, :] = jnp.where(lane < count[i], out_ref[row, :], 0.0)


def build_tiles(plan, first, x_ref, lin_ref, mass_ref, feat, waits, k_ref, la_ref):
    blocks, slots, block, width = feat.shape
    scale = LOG2E / (width * EPS)
    mask = diag_mask(block)
    for s in range(blocks):
        at = first + s
        x = x_ref[at * block : (at + 1) * block, :]
        x32 = x.astype(jnp.float32)
        sq = jnp.sum(x32 * x32, axis=1, keepdims=True)
        lin = to_column(lin_ref[at : at + 1, :], mask)
        base = (2.0 - sq / width - ALPHA * lin) * (LOG2E / EPS)
        base = jnp.broadcast_to(base, (block, block))
        la = F * jnp.log(to_column(mass_ref[at : at + 1, :], mask))
        la_ref[s * block : (s + 1) * block, :] = jnp.broadcast_to(la, (block, block))
        if waits:
            waits[s].wait()

        def tiles(p, _):
            y = [feat[s, plan[at, p * STEP + q]] for q in range(STEP)]
            y = jnp.concatenate(y, axis=0)
            y32 = y.astype(jnp.float32)
            y2 = y32 * y32
            ysq = jnp.sum(y2[:, : width // 2] + y2[:, width // 2 :], axis=1, keepdims=True)
            cross = lax.dot_general(x, y, NT, preferred_element_type=jnp.float32)
            for q in range(STEP):
                cols = slice(q * block, (q + 1) * block)
                row = to_row(ysq[cols, :], mask)
                e = (2.0 * scale) * cross[:, cols] + (base - row * scale)
                start = pl.multiple_of((s * slots + p * STEP + q) * block, block)
                k_ref[pl.ds(start, block), :] = jnp.exp2(e)
            return 0

        lax.fori_loop(0, plan[at, slots + STEP], tiles, 0)


def first_build(live_hbm, tgt_hbm, x_hbm, lin_hbm, mass_hbm, feat, *refs):
    k_ref, la_ref, next_ref, plan_ref, hit_ref, x_ref, lin_ref, mass_ref = refs[:8]
    live, tgt, order_ref, own, sems = refs[8:]
    size = own.shape[0]
    copies = [(live_hbm, live), (tgt_hbm, tgt), (x_hbm, x_ref), (lin_hbm, lin_ref), (mass_hbm, mass_ref)]
    copies += [(feat.at[s], own.at[s]) for s in range(size)]
    copies += [(feat.at[pl.ds(size, next_ref.shape[0])], next_ref)]
    copies = [pltpu.make_async_copy(f, t, sems.at[i]) for i, (f, t) in enumerate(copies)]
    for c in copies:
        c.start()
    for c in copies[:5]:
        c.wait()
    every = hit_ref.shape[0]
    local, slots = tgt.shape
    rows = place_of(tgt[...], local, every // 2, position())
    sub = lax.broadcasted_iota(jnp.int32, (local, slots), 0)
    lives = jnp.zeros((local, slots), jnp.int32)
    for s in range(local):
        lives = jnp.where(sub == s, live[s], lives)
    slot = lax.broadcasted_iota(jnp.int32, (local, slots), 1)
    key = jnp.where(slot < lives, jnp.where(rows < every // 2, 0, slots), 2 * slots) + slot
    rank = jnp.zeros((local, slots), jnp.int32)
    for k in range(slots):
        rank += jnp.where(key[:, k : k + 1] < key, 1, 0)
    lanes = plan_ref.shape[1]
    at = lax.broadcasted_iota(jnp.int32, (local, lanes), 1)
    wide_sub = lax.broadcasted_iota(jnp.int32, (local, lanes), 0)
    lives = jnp.zeros((local, lanes), jnp.int32)
    for s in range(local):
        lives = jnp.where(wide_sub == s, live[s], lives)
    slot_at = jnp.zeros((local, lanes), jnp.int32)
    row_at = jnp.zeros((local, lanes), jnp.int32)
    own_count = jnp.zeros((local, lanes), jnp.int32)
    for k in range(slots):
        here = rank[:, k : k + 1] == at
        slot_at = jnp.where(here, k, slot_at)
        row_at = jnp.where(here, rows[:, k : k + 1], row_at)
        own_count += jnp.where(key[:, k : k + 1] < slots, 1, 0)
    slot_at = jnp.where(at < lives, slot_at, 0)
    row_at = jnp.where(at < lives, row_at, every)
    shift = STEP.bit_length() - 1
    counts = ((lives + (STEP - 1)) >> shift, (own_count + (STEP - 1)) >> shift, own_count >> shift)
    for i, c in enumerate(counts):
        slot_at = jnp.where(at == slots + STEP + i, c, slot_at)
    order_ref[:local, :] = slot_at
    order_ref[local:, :] = row_at
    to_smem = pltpu.make_async_copy(order_ref, plan_ref, sems.at[len(copies)])
    to_smem.start()
    index = jnp.concatenate([row_at[s : s + 1, :slots] for s in range(local)], axis=1)
    rows = lax.broadcasted_iota(jnp.int32, hit_ref.shape, 0)
    hit_ref[...] = jnp.where(rows == index, 1.0, 0.0).astype(jnp.bfloat16)
    to_smem.wait()
    build_tiles(plan_ref, 0, x_ref, lin_ref, mass_ref, own, copies[5:-1], k_ref, la_ref)
    copies[-1].wait()


def later_build(first, plan, x_ref, lin_ref, mass_ref, own, feat, k_ref, la_ref, *rest):
    copy = None
    if rest:
        next_ref, sem = rest
        copy = pltpu.make_async_copy(
            feat.at[pl.ds(first + own.shape[0], next_ref.shape[0])], next_ref, sem
        )
        copy.start()
    build_tiles(plan, first, x_ref, lin_ref, mass_ref, own, (), k_ref, la_ref)
    if copy:
        copy.wait()


def place(s):
    piece = 0
    while s >= PIECES[piece]:
        s -= PIECES[piece]
        piece += 1
    return piece, s


def add_rows(plan, span, w_ref, k_refs, out_ref, from_ref=None):
    blocks, block = plan.shape[0] // 2, w_ref.shape[1]
    slots = plan.shape[1] - 2 * STEP
    for s in range(blocks):
        piece, at = place(s)
        k_ref, base = k_refs[piece], at * slots

        def add_row(p, acc):
            for q in range(STEP):
                k = p * STEP + q
                start = pl.multiple_of((base + k) * block, block)
                w = w_ref[pl.ds(plan[blocks + s, k], 1), :]
                acc = acc + k_ref[pl.ds(start, block), :] * w
            return acc

        first, last = span(s)
        rows = slice(s * block, (s + 1) * block)
        acc = jnp.zeros((block, block), jnp.float32) if from_ref is None else from_ref[rows, :]
        out_ref[rows, :] = lax.fori_loop(first, last, add_row, acc)


def add_columns(plan, span, u_ref, k_refs, hit, col_ref):
    blocks, block = plan.shape[0] // 2, col_ref.shape[1]
    slots = plan.shape[1] - 2 * STEP
    col_ref[...] = jnp.zeros_like(col_ref)
    for s in range(blocks):
        piece, at = place(s)
        k_ref, base = k_refs[piece], at * slots
        u = u_ref[s * block : (s + 1) * block, :]

        def add_col(p, _):
            for q in range(STEP):
                k = p * STEP + q
                start = pl.multiple_of((base + k) * block, block)
                col_ref[pl.ds(s * slots + k, 1), :] = jnp.sum(
                    k_ref[pl.ds(start, block), :] * u, axis=0, keepdims=True
                )
            return 0

        first, last = span(s)
        lax.fori_loop(first, last, add_col, 0)
    col = col_ref[...]
    dense = jnp.zeros((hit.shape[0], block), jnp.float32)
    for _ in range(2):
        term = col.astype(jnp.bfloat16)
        dense += jnp.dot(hit, term, preferred_element_type=jnp.float32)
        col = col - term.astype(jnp.float32)
    return dense


def own_span(plan):
    at = plan.shape[1] - STEP
    return lambda s: (0, plan[s, at + 1])


def other_span(plan):
    at = plan.shape[1] - STEP
    return lambda s: (plan[s, at + 2], plan[s, at])


def spread(w_ref, w, other):
    half = w.shape[0]
    zeros = jnp.zeros((half, w.shape[1]), jnp.float32)
    w_ref[:half, :] = zeros if other else w
    w_ref[half : 2 * half, :] = w if other else zeros
    w_ref[2 * half :, :] = zeros[:8, :]


def unpack(part, fb_ref, et_ref):
    half, block = fb_ref.shape
    n = lax.axis_size("src")
    local = 2 * half // n
    order = distances(n)
    am = jnp.zeros((local, block), jnp.float32)
    bm = am
    for at in range(n // 2):
        m = functools.reduce(lambda p, q: p ^ q, [d for r, d in enumerate(order) if at >> r & 1], 0)
        rows = pl.ds(pl.multiple_of(((position() ^ m) >> 1) * local, local), local)
        at = at * 3 * local
        b = part[at : at + local, :]
        fb_ref[rows, :] = jnp.where(b > 0.0, F * jnp.log(b), ABSENT)
        et_ref[rows, :] = jnp.exp((-ALPHA / EPS) * part[at + local : at + 2 * local, :])
        bm += b
        am += part[at + 2 * local : at + 3 * local, :]
    return am, bm


def half_scale(sums, fb_ref, et_ref):
    fb = fb_ref[...]
    col = sums[...] * et_ref[...]
    t = jnp.where(fb > ABSENT, jnp.exp(fb - F * jnp.log(col)), 0.0)
    return t, jnp.sum(t * col, axis=0, keepdims=True)


def finish(plan, hit_ref, shift, acc_ref, w_ref, k_refs, la_refs, send_ref, u_ref, col_ref, sum_ref):
    block = w_ref.shape[1]
    add_rows(plan, other_span(plan), w_ref, k_refs, sum_ref, acc_ref)
    for s in range(plan.shape[0] // 2):
        rows = pl.ds(s * block, block)
        total = jnp.sum(sum_ref[rows, :], axis=1, keepdims=True)
        piece, at = place(s)
        la = la_refs[piece][pl.ds(at * block, block), :]
        u_ref[rows, :] = jnp.exp((la - shift) - F * jnp.log(total))
    hit = hit_ref[send_ref.shape[0] :, :]
    send_ref[...] = add_columns(plan, other_span(plan), u_ref, k_refs, hit, col_ref)


def first_own(plan, part, *refs):
    k_refs, (acc_ref, fb_ref, et_ref, sums_ref, w_ref) = refs[:-5], refs[-5:]
    am, bm = unpack(part, fb_ref, et_ref)
    sums_ref[:8, :], sums_ref[8:, :] = am, bm
    spread(w_ref, jnp.where(fb_ref[...] > ABSENT, et_ref[...], 0.0), False)
    add_rows(plan, own_span(plan), w_ref, k_refs, acc_ref)


def first_other(plan, hit_ref, part, sums_ref, acc_ref, *refs):
    pieces = len(PIECES)
    k_refs, la_refs = refs[:pieces], refs[pieces : 2 * pieces]
    send_ref, u_ref, fb_ref, et_ref, tot_ref, w_ref, col_ref, sum_ref = refs[2 * pieces :]
    am, bm = unpack(part, fb_ref, et_ref)
    tot = jnp.sqrt(total_of(am + sums_ref[:8, :]) * total_of(bm + sums_ref[8:, :]))
    tot_ref[...] = jnp.broadcast_to(tot, tot_ref.shape)
    spread(w_ref, jnp.where(fb_ref[...] > ABSENT, et_ref[...], 0.0), True)
    finish(
        plan, hit_ref, 0.0, acc_ref, w_ref, k_refs, la_refs, send_ref, u_ref, col_ref, sum_ref
    )


def next_own(plan, sums, fb_ref, et_ref, *refs):
    k_refs, (acc_ref, mass_ref, w_ref) = refs[:-3], refs[-3:]
    t, mass = half_scale(sums, fb_ref, et_ref)
    mass_ref[...] = jnp.broadcast_to(mass, mass_ref.shape)
    spread(w_ref, t * et_ref[...], False)
    add_rows(plan, own_span(plan), w_ref, k_refs, acc_ref)


def next_other(plan, hit_ref, sums, fb_ref, et_ref, tot_ref, mass_ref, acc_ref, *refs):
    pieces = len(PIECES)
    k_refs, la_refs = refs[:pieces], refs[pieces : 2 * pieces]
    send_ref, u_ref, w_ref, col_ref, sum_ref = refs[2 * pieces :]
    t, mass = half_scale(sums, fb_ref, et_ref)
    spread(w_ref, t * et_ref[...], True)
    mass = jnp.sum(mass + mass_ref[0:1, :], axis=1, keepdims=True)
    mass = jnp.broadcast_to(mass, (1, w_ref.shape[1]))
    shift = (F / 2) * (jnp.log(tot_ref[0:1, :]) - jnp.log(mass))
    finish(
        plan, hit_ref, shift, acc_ref, w_ref, k_refs, la_refs, send_ref, u_ref, col_ref, sum_ref
    )


def own_columns(plan, hit_ref, u_ref, *refs):
    k_refs, (keep_ref, col_ref) = refs[:-2], refs[-2:]
    hit = hit_ref[: keep_ref.shape[0], :]
    keep_ref[...] = add_columns(plan, own_span(plan), u_ref, k_refs, hit, col_ref)


def last_own(keep, fb_ref, et_ref, u_ref, src_ref, tgt_ref, mass_ref, t_ref):
    local, block = src_ref.shape
    t, mass = half_scale(keep, fb_ref, et_ref)
    mass_ref[...] = jnp.broadcast_to(mass, mass_ref.shape)
    t_ref[...] = t
    tgt_ref[...] = t_ref[pl.ds(pl.multiple_of((position() >> 1) * local, local), local), :]
    mask = diag_mask(block)
    for s in range(local):
        src_ref[s : s + 1, :] = to_row(u_ref[s * block : (s + 1) * block, :], mask)


def last_other(other, fb_ref, et_ref, tot_ref, mass_ref, src, tgt, src_ref, tgt_ref):
    mass = half_scale(other, fb_ref, et_ref)[1] + mass_ref[0:1, :]
    factor = jnp.sqrt(tot_ref[0:1, 0:1] / jnp.sum(mass, axis=1, keepdims=True))
    src_ref[...] = src[...] * factor
    tgt_ref[...] = tgt[...] * factor


def call(kernel, ins, outs, scratch=(), smem=0, hbm=(), vmem_mb=12, **cost):
    specs = [pl.BlockSpec(memory_space=SMEM)] * smem
    for at in range(smem, len(ins)):
        specs.append(pl.BlockSpec(memory_space=pl.ANY if at in hbm else VMEM))
    ins = [
        pltpu.with_memory_space_constraint(x, pltpu.HBM) if at in hbm else x
        for at, x in enumerate(ins)
    ]
    return pl.pallas_call(
        kernel,
        out_shape=outs,
        in_specs=specs,
        out_specs=[
            pl.BlockSpec(memory_space=SMEM if out.dtype == jnp.int32 else VMEM) for out in outs
        ],
        scratch_shapes=scratch,
        compiler_params=pltpu.CompilerParams(vmem_limit_bytes=vmem_mb << 20),
        cost_estimate=pl.CostEstimate(**cost) if cost else None,
    )(*ins)


def distances(n):
    return [d | 1 for d in (n >> r for r in range(1, n.bit_length()))]


def exchange(x, n, d):
    return lax.ppermute(x, "src", [(i, i ^ d) for i in range(n)])


def shards(
    src_feat, tile_feat, tile_tgt, tile_live, src_lin, tgt_lin, src_mass, tgt_mass, tgt_count
):
    f32 = jnp.float32
    local, slots, block, width = tile_feat.shape
    n = lax.axis_size("src")
    every = local * n
    pairs = local * slots
    lin = src_lin.reshape(local, block)
    amass = src_mass.reshape(local, block)
    def shape(rows, cols=block, dtype=f32):
        return pltpu.VMEM((rows, cols), dtype)

    (part,) = call(
        pack_kernel,
        (tgt_count, tgt_mass.reshape(local, block), tgt_lin.reshape(local, block), amass),
        (shape(3 * local),),
        scratch=[SMEM((local,), jnp.int32), pltpu.SemaphoreType.DMA((4,))],
        hbm=(0, 1, 2, 3),
    )
    def feats(size):
        return pltpu.VMEM((size, slots, block, width), tile_feat.dtype)

    order = distances(n)
    kern, la = [], []
    following = None
    for at, d in enumerate(order):
        got = exchange(part, n, d)
        if at < len(PIECES):
            size = PIECES[at]
            ahead = [feats(PIECES[at + 1])] if at + 1 < len(PIECES) else []
            outs = (shape(size * slots * block), shape(size * block), *ahead)
            cost = dict(
                flops=2 * size * slots * block * block * width,
                bytes_accessed=2 * size * slots * block * width,
                transcendentals=size * slots * block * block,
            )
        if at == 0:
            k0, la0, following, plan, hit, xv, linv, massv = call(
                first_build,
                (tile_live, tile_tgt, src_feat, lin, amass, tile_feat),
                (
                    *outs,
                    SMEM((2 * local, slots + 2 * STEP), jnp.int32),
                    shape(every, pairs, jnp.bfloat16),
                    shape(local * block, width, src_feat.dtype),
                    shape(local),
                    shape(local),
                ),
                scratch=[
                    SMEM((local,), jnp.int32),
                    VMEM((local, slots), jnp.int32),
                    VMEM((2 * local, slots + 2 * STEP), jnp.int32),
                    feats(size),
                    pltpu.SemaphoreType.DMA((7 + size,)),
                ],
                hbm=(0, 1, 2, 3, 4, 5),
                **cost,
            )
        elif at < len(PIECES):
            k0, la0, *following = call(
                functools.partial(later_build, sum(PIECES[:at])),
                (plan, xv, linv, massv, following, tile_feat),
                outs,
                scratch=[pltpu.SemaphoreType.DMA] if ahead else [],
                smem=1,
                hbm=(5,),
                **cost,
            )
            following = following[0] if following else None
        if at < len(PIECES):
            kern.append(k0)
            la.append(la0)
        if at < len(order) - 1:
            part = jnp.stack([part, got], axis=0).reshape(-1, block)
            if at < len(PIECES) - 1:
                part, following, kern[-1] = lax.optimization_barrier((part, following, kern[-1]))
            elif at < len(PIECES):
                part, kern[-1] = lax.optimization_barrier((part, kern[-1]))
    half = every // 2
    tall = shape(local * block)
    w = VMEM((every + 8, block), f32)
    col = VMEM((pairs, block), f32)
    acc, fb0, et0, sums = call(
        first_own,
        (plan, part, *kern),
        (tall, shape(half), shape(half), shape(16)),
        scratch=[w],
        smem=1,
    )
    send, u, fb1, et1, tot = call(
        first_other,
        (plan, hit, got, sums, acc, *kern, *la),
        (shape(half), tall, shape(half), shape(half), shape(8)),
        scratch=[w, col, VMEM((local * block, block), f32)],
        smem=1,
    )
    for iteration in range(ITERS):
        got = exchange(send, n, order[-1])
        (keep,) = call(
            own_columns, (plan, hit, u, *kern), (shape(half),), scratch=[col], smem=1
        )
        keep = keep + got
        for d in order[:-1]:
            keep = keep + exchange(keep, n, d)
        other = exchange(keep, n, order[-1])
        if iteration < ITERS - 1:
            acc, mass = call(
                next_own, (plan, keep, fb0, et0, *kern), (tall, shape(8)), scratch=[w], smem=1
            )
            send, u = call(
                next_other,
                (plan, hit, other, fb1, et1, tot, mass, acc, *kern, *la),
                (shape(half), tall),
                scratch=[w, col, VMEM((local * block, block), f32)],
                smem=1,
            )
    src, tgt, mass = call(
        last_own,
        (keep, fb0, et0, u),
        (shape(local), shape(local), shape(8)),
        scratch=[VMEM((half, block), f32)],
    )
    src, tgt = call(
        last_other,
        (other, fb1, et1, tot, mass, src, tgt),
        [jax.ShapeDtypeStruct((local, block), f32)] * 2,
    )
    return (src.reshape(-1), tgt.reshape(-1))


def solution(mesh):
    split = P(("pairs", "src"))
    rows = P(("pairs", "src"), None)
    in_specs = (rows, P(("pairs", "src"), None, None, None), rows) + (split,) * 6
    return jax.shard_map(
        shards, mesh=mesh, in_specs=in_specs, out_specs=(split, split), check_vma=False
    )
```

```python
import functools

import jax
import jax.numpy as jnp
from jax import lax
from jax.experimental import pallas as pl
from jax.experimental.pallas import tpu as pltpu
from jax.sharding import PartitionSpec as P

ITERS = 3
EPS = 0.1
RHO = 1.0
ALPHA = 0.5
F = RHO / (RHO + EPS)
LOG2E = 1.4426950408889634
STEP = 4
ABSENT = -1e30
PIECES = (2, 3, 2, 1)

VMEM = pltpu.VMEM
SMEM = pltpu.SMEM
NT = (((1,), (1,)), ((), ()))


def diag_mask(block):
    return lax.broadcasted_iota(jnp.int32, (block, block), 0) == lax.broadcasted_iota(
        jnp.int32, (block, block), 1
    )


def to_column(row, mask):
    return jnp.sum(jnp.where(mask, row, 0.0), axis=1, keepdims=True)


def to_row(column, mask):
    return jnp.sum(jnp.where(mask, column, 0.0), axis=0, keepdims=True)


def position():
    return lax.axis_index("src").astype(jnp.int32)


def parity(x):
    for r in (4, 2, 1):
        x = x ^ (x >> r)
    return x & 1


def place_of(block, local, half, me):
    owner = block >> (local.bit_length() - 1)
    return parity(owner ^ me) * half + (owner >> 1) * local + (block & (local - 1))


def total_of(x):
    return jnp.sum(jnp.sum(x, axis=0, keepdims=True), axis=1, keepdims=True)


def pack_kernel(count_hbm, mass_hbm, lin_hbm, amass_hbm, out_ref, count, sems):
    local, block = mass_hbm.shape
    copies = [(count_hbm, count)]
    for i, x in enumerate((mass_hbm, lin_hbm, amass_hbm)):
        copies.append((x, out_ref.at[pl.ds(i * local, local)]))
    copies = [pltpu.make_async_copy(f, t, sems.at[i]) for i, (f, t) in enumerate(copies)]
    for c in copies:
        c.start()
    for c in copies:
        c.wait()
    lane = lax.broadcasted_iota(jnp.int32, (1, block), 1)
    for i in range(local):
        row = slice(i, i + 1)
        out_ref[row, :] = jnp.where(lane < count[i], out_ref[row, :], 0.0)


def build_tiles(plan, first, x_ref, lin_ref, mass_ref, feat, waits, k_ref, la_ref):
    blocks, slots, block, width = feat.shape
    scale = LOG2E / (width * EPS)
    mask = diag_mask(block)
    for s in range(blocks):
        at = first + s
        x = x_ref[at * block : (at + 1) * block, :]
        x32 = x.astype(jnp.float32)
        sq = jnp.sum(x32 * x32, axis=1, keepdims=True)
        lin = to_column(lin_ref[at : at + 1, :], mask)
        base = (2.0 - sq / width - ALPHA * lin) * (LOG2E / EPS)
        base = jnp.broadcast_to(base, (block, block))
        la = F * jnp.log(to_column(mass_ref[at : at + 1, :], mask))
        la_ref[s * block : (s + 1) * block, :] = jnp.broadcast_to(la, (block, block))
        if waits:
            waits[s].wait()

        def tiles(p, _):
            y = [feat[s, plan[at, p * STEP + q]] for q in range(STEP)]
            y = jnp.concatenate(y, axis=0)
            y32 = y.astype(jnp.float32)
            y2 = y32 * y32
            ysq = jnp.sum(y2[:, : width // 2] + y2[:, width // 2 :], axis=1, keepdims=True)
            cross = lax.dot_general(x, y, NT, preferred_element_type=jnp.float32)
            for q in range(STEP):
                cols = slice(q * block, (q + 1) * block)
                row = to_row(ysq[cols, :], mask)
                e = (2.0 * scale) * cross[:, cols] + (base - row * scale)
                start = pl.multiple_of((s * slots + p * STEP + q) * block, block)
                k_ref[pl.ds(start, block), :] = jnp.exp2(e)
            return 0

        lax.fori_loop(0, plan[at, slots + STEP], tiles, 0)


def first_build(live_hbm, tgt_hbm, x_hbm, lin_hbm, mass_hbm, feat, *refs):
    k_ref, la_ref, next_ref, plan_ref, hit_ref, x_ref, lin_ref, mass_ref = refs[:8]
    live, tgt, order_ref, own, sems = refs[8:]
    size = own.shape[0]
    copies = [(live_hbm, live), (tgt_hbm, tgt), (x_hbm, x_ref), (lin_hbm, lin_ref), (mass_hbm, mass_ref)]
    copies += [(feat.at[s], own.at[s]) for s in range(size)]
    copies += [(feat.at[pl.ds(size, next_ref.shape[0])], next_ref)]
    copies = [pltpu.make_async_copy(f, t, sems.at[i]) for i, (f, t) in enumerate(copies)]
    for c in copies:
        c.start()
    for c in copies[:5]:
        c.wait()
    every = hit_ref.shape[0]
    local, slots = tgt.shape
    rows = place_of(tgt[...], local, every // 2, position())
    sub = lax.broadcasted_iota(jnp.int32, (local, slots), 0)
    lives = jnp.zeros((local, slots), jnp.int32)
    for s in range(local):
        lives = jnp.where(sub == s, live[s], lives)
    slot = lax.broadcasted_iota(jnp.int32, (local, slots), 1)
    key = jnp.where(slot < lives, jnp.where(rows < every // 2, 0, slots), 2 * slots) + slot
    rank = jnp.zeros((local, slots), jnp.int32)
    for k in range(slots):
        rank += jnp.where(key[:, k : k + 1] < key, 1, 0)
    lanes = plan_ref.shape[1]
    at = lax.broadcasted_iota(jnp.int32, (local, lanes), 1)
    wide_sub = lax.broadcasted_iota(jnp.int32, (local, lanes), 0)
    lives = jnp.zeros((local, lanes), jnp.int32)
    for s in range(local):
        lives = jnp.where(wide_sub == s, live[s], lives)
    slot_at = jnp.zeros((local, lanes), jnp.int32)
    row_at = jnp.zeros((local, lanes), jnp.int32)
    own_count = jnp.zeros((local, lanes), jnp.int32)
    for k in range(slots):
        here = rank[:, k : k + 1] == at
        slot_at = jnp.where(here, k, slot_at)
        row_at = jnp.where(here, rows[:, k : k + 1], row_at)
        own_count += jnp.where(key[:, k : k + 1] < slots, 1, 0)
    slot_at = jnp.where(at < lives, slot_at, 0)
    row_at = jnp.where(at < lives, row_at, every)
    shift = STEP.bit_length() - 1
    counts = ((lives + (STEP - 1)) >> shift, (own_count + (STEP - 1)) >> shift, own_count >> shift)
    for i, c in enumerate(counts):
        slot_at = jnp.where(at == slots + STEP + i, c, slot_at)
    order_ref[:local, :] = slot_at
    order_ref[local:, :] = row_at
    to_smem = pltpu.make_async_copy(order_ref, plan_ref, sems.at[len(copies)])
    to_smem.start()
    index = jnp.concatenate([row_at[s : s + 1, :slots] for s in range(local)], axis=1)
    rows = lax.broadcasted_iota(jnp.int32, hit_ref.shape, 0)
    hit_ref[...] = jnp.where(rows == index, 1.0, 0.0).astype(jnp.bfloat16)
    to_smem.wait()
    build_tiles(plan_ref, 0, x_ref, lin_ref, mass_ref, own, copies[5:-1], k_ref, la_ref)
    copies[-1].wait()


def later_build(first, plan, x_ref, lin_ref, mass_ref, own, feat, k_ref, la_ref, *rest):
    copy = None
    if rest:
        next_ref, sem = rest
        copy = pltpu.make_async_copy(
            feat.at[pl.ds(first + own.shape[0], next_ref.shape[0])], next_ref, sem
        )
        copy.start()
    build_tiles(plan, first, x_ref, lin_ref, mass_ref, own, (), k_ref, la_ref)
    if copy:
        copy.wait()


def place(s):
    piece = 0
    while s >= PIECES[piece]:
        s -= PIECES[piece]
        piece += 1
    return piece, s


def add_rows(plan, span, w_ref, k_refs, out_ref, from_ref=None):
    blocks, block = plan.shape[0] // 2, w_ref.shape[1]
    slots = plan.shape[1] - 2 * STEP
    for s in range(blocks):
        piece, at = place(s)
        k_ref, base = k_refs[piece], at * slots

        def add_row(p, acc):
            for q in range(STEP):
                k = p * STEP + q
                start = pl.multiple_of((base + k) * block, block)
                w = w_ref[pl.ds(plan[blocks + s, k], 1), :]
                acc = acc + k_ref[pl.ds(start, block), :] * w
            return acc

        first, last = span(s)
        rows = slice(s * block, (s + 1) * block)
        acc = jnp.zeros((block, block), jnp.float32) if from_ref is None else from_ref[rows, :]
        out_ref[rows, :] = lax.fori_loop(first, last, add_row, acc)


def add_columns(plan, span, u_ref, k_refs, hit, col_ref):
    blocks, block = plan.shape[0] // 2, col_ref.shape[1]
    slots = plan.shape[1] - 2 * STEP
    col_ref[...] = jnp.zeros_like(col_ref)
    for s in range(blocks):
        piece, at = place(s)
        k_ref, base = k_refs[piece], at * slots
        u = u_ref[s * block : (s + 1) * block, :]

        def add_col(p, _):
            for q in range(STEP):
                k = p * STEP + q
                start = pl.multiple_of((base + k) * block, block)
                col_ref[pl.ds(s * slots + k, 1), :] = jnp.sum(
                    k_ref[pl.ds(start, block), :] * u, axis=0, keepdims=True
                )
            return 0

        first, last = span(s)
        lax.fori_loop(first, last, add_col, 0)
    col = col_ref[...]
    dense = jnp.zeros((hit.shape[0], block), jnp.float32)
    for _ in range(2):
        term = col.astype(jnp.bfloat16)
        dense += jnp.dot(hit, term, preferred_element_type=jnp.float32)
        col = col - term.astype(jnp.float32)
    return dense


def own_span(plan):
    at = plan.shape[1] - STEP
    return lambda s: (0, plan[s, at + 1])


def other_span(plan):
    at = plan.shape[1] - STEP
    return lambda s: (plan[s, at + 2], plan[s, at])


def spread(w_ref, w, other):
    half = w.shape[0]
    zeros = jnp.zeros((half, w.shape[1]), jnp.float32)
    w_ref[:half, :] = zeros if other else w
    w_ref[half : 2 * half, :] = w if other else zeros
    w_ref[2 * half :, :] = zeros[:8, :]


def unpack(part, fb_ref, et_ref):
    half, block = fb_ref.shape
    n = lax.axis_size("src")
    local = 2 * half // n
    order = distances(n)
    am = jnp.zeros((local, block), jnp.float32)
    bm = am
    for at in range(n // 2):
        m = functools.reduce(lambda p, q: p ^ q, [d for r, d in enumerate(order) if at >> r & 1], 0)
        rows = pl.ds(pl.multiple_of(((position() ^ m) >> 1) * local, local), local)
        at = at * 3 * local
        b = part[at : at + local, :]
        fb_ref[rows, :] = jnp.where(b > 0.0, F * jnp.log(b), ABSENT)
        et_ref[rows, :] = jnp.exp((-ALPHA / EPS) * part[at + local : at + 2 * local, :])
        bm += b
        am += part[at + 2 * local : at + 3 * local, :]
    return am, bm


def half_scale(sums, fb_ref, et_ref):
    fb = fb_ref[...]
    col = sums[...] * et_ref[...]
    t = jnp.where(fb > ABSENT, jnp.exp(fb - F * jnp.log(col)), 0.0)
    return t, jnp.sum(t * col, axis=0, keepdims=True)


def finish(plan, hit_ref, shift, acc_ref, w_ref, k_refs, la_refs, send_ref, u_ref, col_ref, sum_ref):
    block = w_ref.shape[1]
    add_rows(plan, other_span(plan), w_ref, k_refs, sum_ref, acc_ref)
    for s in range(plan.shape[0] // 2):
        rows = pl.ds(s * block, block)
        total = jnp.sum(sum_ref[rows, :], axis=1, keepdims=True)
        piece, at = place(s)
        la = la_refs[piece][pl.ds(at * block, block), :]
        u_ref[rows, :] = jnp.exp((la - shift) - F * jnp.log(total))
    hit = hit_ref[send_ref.shape[0] :, :]
    send_ref[...] = add_columns(plan, other_span(plan), u_ref, k_refs, hit, col_ref)


def first_own(plan, part, *refs):
    k_refs, (acc_ref, fb_ref, et_ref, sums_ref, w_ref) = refs[:-5], refs[-5:]
    am, bm = unpack(part, fb_ref, et_ref)
    sums_ref[:8, :], sums_ref[8:, :] = am, bm
    spread(w_ref, jnp.where(fb_ref[...] > ABSENT, et_ref[...], 0.0), False)
    add_rows(plan, own_span(plan), w_ref, k_refs, acc_ref)


def first_other(plan, hit_ref, part, sums_ref, acc_ref, *refs):
    pieces = len(PIECES)
    k_refs, la_refs = refs[:pieces], refs[pieces : 2 * pieces]
    send_ref, u_ref, fb_ref, et_ref, tot_ref, w_ref, col_ref, sum_ref = refs[2 * pieces :]
    am, bm = unpack(part, fb_ref, et_ref)
    tot = jnp.sqrt(total_of(am + sums_ref[:8, :]) * total_of(bm + sums_ref[8:, :]))
    tot_ref[...] = jnp.broadcast_to(tot, tot_ref.shape)
    spread(w_ref, jnp.where(fb_ref[...] > ABSENT, et_ref[...], 0.0), True)
    finish(
        plan, hit_ref, 0.0, acc_ref, w_ref, k_refs, la_refs, send_ref, u_ref, col_ref, sum_ref
    )


def next_own(plan, sums, fb_ref, et_ref, *refs):
    k_refs, (acc_ref, mass_ref, w_ref) = refs[:-3], refs[-3:]
    t, mass = half_scale(sums, fb_ref, et_ref)
    mass_ref[...] = jnp.broadcast_to(mass, mass_ref.shape)
    spread(w_ref, t * et_ref[...], False)
    add_rows(plan, own_span(plan), w_ref, k_refs, acc_ref)


def next_other(plan, hit_ref, sums, fb_ref, et_ref, tot_ref, mass_ref, acc_ref, *refs):
    pieces = len(PIECES)
    k_refs, la_refs = refs[:pieces], refs[pieces : 2 * pieces]
    send_ref, u_ref, w_ref, col_ref, sum_ref = refs[2 * pieces :]
    t, mass = half_scale(sums, fb_ref, et_ref)
    spread(w_ref, t * et_ref[...], True)
    mass = jnp.sum(mass + mass_ref[0:1, :], axis=1, keepdims=True)
    mass = jnp.broadcast_to(mass, (1, w_ref.shape[1]))
    shift = (F / 2) * (jnp.log(tot_ref[0:1, :]) - jnp.log(mass))
    finish(
        plan, hit_ref, shift, acc_ref, w_ref, k_refs, la_refs, send_ref, u_ref, col_ref, sum_ref
    )


def own_columns(plan, hit_ref, u_ref, *refs):
    k_refs, (keep_ref, col_ref) = refs[:-2], refs[-2:]
    hit = hit_ref[: keep_ref.shape[0], :]
    keep_ref[...] = add_columns(plan, own_span(plan), u_ref, k_refs, hit, col_ref)


def last_own(keep, fb_ref, et_ref, u_ref, src_ref, tgt_ref, mass_ref, t_ref):
    local, block = src_ref.shape
    t, mass = half_scale(keep, fb_ref, et_ref)
    mass_ref[...] = jnp.broadcast_to(mass, mass_ref.shape)
    t_ref[...] = t
    tgt_ref[...] = t_ref[pl.ds(pl.multiple_of((position() >> 1) * local, local), local), :]
    mask = diag_mask(block)
    for s in range(local):
        src_ref[s : s + 1, :] = to_row(u_ref[s * block : (s + 1) * block, :], mask)


def last_other(other, fb_ref, et_ref, tot_ref, mass_ref, src, tgt, src_ref, tgt_ref):
    mass = half_scale(other, fb_ref, et_ref)[1] + mass_ref[0:1, :]
    factor = jnp.sqrt(tot_ref[0:1, 0:1] / jnp.sum(mass, axis=1, keepdims=True))
    src_ref[...] = src[...] * factor
    tgt_ref[...] = tgt[...] * factor


def call(kernel, ins, outs, scratch=(), smem=0, hbm=(), vmem_mb=12, **cost):
    specs = [pl.BlockSpec(memory_space=SMEM)] * smem
    for at in range(smem, len(ins)):
        specs.append(pl.BlockSpec(memory_space=pl.ANY if at in hbm else VMEM))
    ins = [
        pltpu.with_memory_space_constraint(x, pltpu.HBM) if at in hbm else x
        for at, x in enumerate(ins)
    ]
    return pl.pallas_call(
        kernel,
        out_shape=outs,
        in_specs=specs,
        out_specs=[
            pl.BlockSpec(memory_space=SMEM if out.dtype == jnp.int32 else VMEM) for out in outs
        ],
        scratch_shapes=scratch,
        compiler_params=pltpu.CompilerParams(vmem_limit_bytes=vmem_mb << 20),
        cost_estimate=pl.CostEstimate(**cost) if cost else None,
    )(*ins)


def distances(n):
    return [d | 1 for d in (n >> r for r in range(1, n.bit_length()))]


def exchange(x, n, d):
    return lax.ppermute(x, "src", [(i, i ^ d) for i in range(n)])


def shards(
    src_feat, tile_feat, tile_tgt, tile_live, src_lin, tgt_lin, src_mass, tgt_mass, tgt_count
):
    f32 = jnp.float32
    local, slots, block, width = tile_feat.shape
    n = lax.axis_size("src")
    every = local * n
    pairs = local * slots
    lin = src_lin.reshape(local, block)
    amass = src_mass.reshape(local, block)
    def shape(rows, cols=block, dtype=f32):
        return pltpu.VMEM((rows, cols), dtype)

    (part,) = call(
        pack_kernel,
        (tgt_count, tgt_mass.reshape(local, block), tgt_lin.reshape(local, block), amass),
        (shape(3 * local),),
        scratch=[SMEM((local,), jnp.int32), pltpu.SemaphoreType.DMA((4,))],
        hbm=(0, 1, 2, 3),
    )
    def feats(size):
        return pltpu.VMEM((size, slots, block, width), tile_feat.dtype)

    order = distances(n)
    kern, la = [], []
    following = None
    for at, d in enumerate(order):
        got = exchange(part, n, d)
        if at < len(PIECES):
            size = PIECES[at]
            ahead = [feats(PIECES[at + 1])] if at + 1 < len(PIECES) else []
            outs = (shape(size * slots * block), shape(size * block), *ahead)
            cost = dict(
                flops=2 * size * slots * block * block * width,
                bytes_accessed=2 * size * slots * block * width,
                transcendentals=size * slots * block * block,
            )
        if at == 0:
            k0, la0, following, plan, hit, xv, linv, massv = call(
                first_build,
                (tile_live, tile_tgt, src_feat, lin, amass, tile_feat),
                (
                    *outs,
                    SMEM((2 * local, slots + 2 * STEP), jnp.int32),
                    shape(every, pairs, jnp.bfloat16),
                    shape(local * block, width, src_feat.dtype),
                    shape(local),
                    shape(local),
                ),
                scratch=[
                    SMEM((local,), jnp.int32),
                    VMEM((local, slots), jnp.int32),
                    VMEM((2 * local, slots + 2 * STEP), jnp.int32),
                    feats(size),
                    pltpu.SemaphoreType.DMA((7 + size,)),
                ],
                hbm=(0, 1, 2, 3, 4, 5),
                **cost,
            )
        elif at < len(PIECES):
            k0, la0, *following = call(
                functools.partial(later_build, sum(PIECES[:at])),
                (plan, xv, linv, massv, following, tile_feat),
                outs,
                scratch=[pltpu.SemaphoreType.DMA] if ahead else [],
                smem=1,
                hbm=(5,),
                **cost,
            )
            following = following[0] if following else None
        if at < len(PIECES):
            kern.append(k0)
            la.append(la0)
        if at < len(order) - 1:
            part = jnp.stack([part, got], axis=0).reshape(-1, block)
            if at < len(PIECES) - 1:
                part, following, kern[-1] = lax.optimization_barrier((part, following, kern[-1]))
            elif at < len(PIECES):
                part, kern[-1] = lax.optimization_barrier((part, kern[-1]))
    half = every // 2
    tall = shape(local * block)
    w = VMEM((every + 8, block), f32)
    col = VMEM((pairs, block), f32)
    acc, fb0, et0, sums = call(
        first_own,
        (plan, part, *kern),
        (tall, shape(half), shape(half), shape(16)),
        scratch=[w],
        smem=1,
    )
    send, u, fb1, et1, tot = call(
        first_other,
        (plan, hit, got, sums, acc, *kern, *la),
        (shape(half), tall, shape(half), shape(half), shape(8)),
        scratch=[w, col, VMEM((local * block, block), f32)],
        smem=1,
    )
    for iteration in range(ITERS):
        got = exchange(send, n, order[-1])
        (keep,) = call(
            own_columns, (plan, hit, u, *kern), (shape(half),), scratch=[col], smem=1
        )
        keep = keep + got
        for d in order[:-1]:
            keep = keep + exchange(keep, n, d)
        other = exchange(keep, n, order[-1])
        if iteration < ITERS - 1:
            acc, mass = call(
                next_own, (plan, keep, fb0, et0, *kern), (tall, shape(8)), scratch=[w], smem=1
            )
            send, u = call(
                next_other,
                (plan, hit, other, fb1, et1, tot, mass, acc, *kern, *la),
                (shape(half), tall),
                scratch=[w, col, VMEM((local * block, block), f32)],
                smem=1,
            )
    src, tgt, mass = call(
        last_own,
        (keep, fb0, et0, u),
        (shape(local), shape(local), shape(8)),
        scratch=[VMEM((half, block), f32)],
    )
    src, tgt = call(
        last_other,
        (other, fb1, et1, tot, mass, src, tgt),
        [jax.ShapeDtypeStruct((local, block), f32)] * 2,
    )
    return (src.reshape(-1), tgt.reshape(-1))


def solution(mesh):
    split = P(("pairs", "src"))
    rows = P(("pairs", "src"), None)
    in_specs = (rows, P(("pairs", "src"), None, None, None), rows) + (split,) * 6
    return jax.shard_map(
        shards, mesh=mesh, in_specs=in_specs, out_specs=(split, split), check_vma=False
    )
```
